32 devices in a mesh: gx: 8 (over z, y), gy: 4 (over x, core).
Axes of the slice: x: 2, y: 2, z: 4, core: 2. Of those that a mesh axis runs over, the one named last changes fastest.
Arguments:
- amplitudes: bfloat16 [64, 1048576], P(None, ('gy', 'gx')), may hold values from -6 to 6
- virt_irreps: int32 [8], replicated, may hold values from 0 to 7, as said below
- w_tiles: bfloat16 [8192, 128, 128], P(('gx', 'gy')), may hold values from -0.1875 to 0.1875
- tile_rows: int32 [8192], P(('gx', 'gy')), may hold values from 0 to 2047, as said below
- tile_cols: int32 [8192], P(('gx', 'gy')), may hold values from 0 to 31
Outputs:
- ladder: float32 [64, 32768], P(None, ('gx', 'gy'))
The draws below stay inside these ranges and needn't reach their ends.
Inputs may be any that keep to these rules, and one draw needn't show every extreme that they name: virt_irreps names each of the 8 irreps once. `tile_rows`: slot s of a device (s = t % 256) names a row tile in [q * 2048 // 8, (q + 1) * 2048 // 8) with q = s // (256 // 8); every stored tile has irrep(row(t)) == irrep(col(t)) for the drawn virt_irreps.
All inputs are finite; a program needn't handle non-finite values.
Results may differ from the reference program's by a relative error of at most 0.0003.
Values may be sent and summed in bfloat16 or wider, within the bound.
No kernel may reach another device: no remote copies, remote signals or barrier semaphores. Data moves between devices by JAX's collectives and lax.ppermute only.
A program may use at most 128 MiB of HBM per device.

```python
import jax
import jax.numpy as jnp
from jax import lax

V = 1024
BLK = 128
OCC = 64
ABT_X = 32
SLOTS = 256
NB = 8
CD = 1048576
CDT = 2048
AB = 32768
TILES = 8192
N_GX = 8
N_GY = 4


def shared_pattern(key):
    irreps = jax.random.permutation(jax.random.fold_in(key, 11), NB).astype(jnp.int32)
    cols = jax.random.randint(jax.random.fold_in(key, 12), (TILES,), 0, ABT_X, dtype=jnp.int32)
    local_count = CDT // N_GX
    per_peer = SLOTS // N_GX
    groups = jax.random.randint(jax.random.fold_in(key, 13), (TILES,), 0, local_count // NB, dtype=jnp.int32)
    index = jnp.arange(TILES, dtype=jnp.int32)
    owner = index // SLOTS
    slot = index % SLOTS
    peer = slot // per_peer
    base = peer * local_count + groups * NB
    col_global = owner // N_GY * ABT_X + cols
    col_first = irreps[col_global * BLK // V // BLK]
    col_second = irreps[col_global * BLK % V // BLK]
    wanted = jnp.bitwise_xor(col_first, col_second)
    row_base = owner % N_GY * CDT + base
    row_first = irreps[row_base * BLK // V // BLK]
    needed = jnp.bitwise_xor(wanted, row_first)
    labels = jnp.arange(NB, dtype=jnp.int32)
    match = (irreps[None, :] == needed[:, None]).astype(jnp.int32)
    second_block = jnp.sum(match * labels[None, :], axis=1).astype(jnp.int32)
    rows = base + second_block
    return (irreps, rows, cols)


def draw_virt_irreps(key, part):
    return shared_pattern(key)[0]


def draw_tile_rows(key, part):
    return shared_pattern(key)[1]


def draw_tile_cols(key, part):
    return shared_pattern(key)[2]


def steps_of(own_key, dims, cuts, low, top_value):
    factor_of = 1.0
    for dim, blocks in cuts:
        draws = jax.random.uniform(jax.random.fold_in(jax.random.fold_in(own_key, 6), dim), (blocks,), jnp.float32, low / len(cuts), top_value / len(cuts))
        factor_of = factor_of * jnp.repeat(jnp.exp(draws), dims[dim] // blocks).reshape((-1,) + (1,) * (len(dims) - 1 - dim))
    return factor_of


def centred(rng, dims, deviation, bound, cuts=(), held_as=jnp.bfloat16):
    values = jax.random.normal(rng, dims, jnp.float32) * deviation
    if len(cuts) > 0:
        values = steps_of(rng, dims, cuts, -0.22, 0.18) * values
    return jnp.clip(values, min=-bound, max=bound).astype(held_as)


def setup_inputs(seed: int = 0) -> dict:
    splits = jax.random.split(jax.random.key(seed), 6)
    amplitudes = centred(splits[0], (OCC, CD), 1.0, 6.0, ((1, 32),))
    virt_irreps = draw_virt_irreps(jax.random.fold_in(splits[5], 71), 0)
    w_tiles = centred(splits[2], (TILES, BLK, BLK), (BLK * 8) ** -0.5, 0.1875, ((0, 32),))
    tile_rows = draw_tile_rows(jax.random.fold_in(splits[5], 71), 0)
    tile_cols = draw_tile_cols(jax.random.fold_in(splits[5], 71), 0)
    return {"amplitudes": amplitudes, "virt_irreps": virt_irreps, "w_tiles": w_tiles, "tile_rows": tile_rows, "tile_cols": tile_cols}


def pair_irrep(tile, virt_irreps):
    first = ((tile * BLK) // V) // BLK
    second = ((tile * BLK) % V) // BLK
    return jnp.bitwise_xor(virt_irreps[first], virt_irreps[second])


def reference(amplitudes, virt_irreps, w_tiles, tile_rows, tile_cols):
    owner = jnp.arange(TILES, dtype=jnp.int32) // SLOTS
    row_tile = (owner % N_GY) * CDT + tile_rows
    col_tile = (owner // N_GY) * ABT_X + tile_cols
    live = (pair_irrep(row_tile, virt_irreps) == pair_irrep(col_tile, virt_irreps)).astype(jnp.float32)
    amp_tiles = amplitudes.reshape(OCC, CD // BLK, BLK)
    count = TILES // SLOTS
    xs = (row_tile.reshape(count, SLOTS), col_tile.reshape(count, SLOTS),
          live.reshape(count, SLOTS), w_tiles.reshape(count, SLOTS, BLK, BLK))

    def step(total, item):
        rows, cols, alive, weights = item
        pieces = jnp.take(amp_tiles, rows, axis=1).astype(jnp.float32)
        product = jnp.einsum("psk,skn->spn", pieces, weights.astype(jnp.float32))
        product = product * alive[:, None, None]
        return total.at[cols].add(product), None

    total = jnp.zeros((AB // BLK, OCC, BLK), jnp.float32)
    total, _ = lax.scan(step, total, xs)
    return jnp.transpose(total, (1, 0, 2)).reshape(OCC, AB)
```

```python
import functools

import jax
import jax.numpy as jnp
from jax import lax
from jax.experimental import pallas as pl
from jax.experimental.pallas import tpu as pltpu
from jax.sharding import PartitionSpec as P

V = 1024
BLK = 128
ABT_X = 32
CORES = 2
UNROLL = 4


def pair_irrep(tile, virt_irreps):
    first = tile * BLK // V // BLK
    second = tile * BLK % V // BLK
    return jnp.bitwise_xor(virt_irreps[first], virt_irreps[second])


def pick_kernel(peers, per, wanted, amp, *outs):
    for peer in range(peers):
        out = outs[peer]

        def step(i, carry):
            lane = pl.multiple_of(wanted[peer * per + i] * BLK, BLK)
            out[i] = amp[:, pl.ds(lane, BLK)]
            return carry

        lax.fori_loop(0, per, step, 0, unroll=8)


def pick(amplitudes, wanted, peers, per):
    occupied = amplitudes.shape[0]
    shape = jax.ShapeDtypeStruct((per, occupied, BLK), amplitudes.dtype)
    size = amplitudes.size * 2
    return pl.pallas_call(
        functools.partial(pick_kernel, peers, per),
        out_shape=[shape] * peers,
        in_specs=[
            pl.BlockSpec(memory_space=pltpu.SMEM),
            pl.BlockSpec(memory_space=pltpu.VMEM),
        ],
        out_specs=[pl.BlockSpec(memory_space=pltpu.VMEM)] * peers,
        compiler_params=pltpu.CompilerParams(vmem_limit_bytes=40 * 1024 * 1024),
        cost_estimate=pl.CostEstimate(flops=0, bytes_accessed=2 * size, transcendentals=0),
        name="pick_tiles",
    )(wanted, amplitudes)


def ladder_kernel(count, per, first, last, blocks, cols, live, w, *refs):
    pieces = refs[:count]
    refs = refs[count:]
    if not first:
        start, refs = refs[0], refs[1:]
    if last:
        keep, give, total, wbuf, pbuf, sems = refs
    else:
        total, wbuf, pbuf, sems = refs
    copies = []
    for j in range(count):
        a = pltpu.make_async_copy(w.at[blocks[j]], wbuf.at[j], sems.at[0, j])
        b = pltpu.make_async_copy(pieces[j], pbuf.at[j], sems.at[1, j])
        a.start()
        b.start()
        copies.append((a, b))
    total[...] = jnp.zeros_like(total) if first else start[...]
    for j in range(count):
        for copy in copies[j]:
            copy.wait()
        base = blocks[j] * per

        def step(i, carry):
            slots = [i * UNROLL + u for u in range(UNROLL)]
            products = [
                jnp.dot(pbuf[j, s], wbuf[j, s], preferred_element_type=jnp.float32)
                for s in slots
            ]
            for s, product in zip(slots, products):
                col = cols[base + s]
                total[col] += product * live[base + s]
            return carry

        lax.fori_loop(0, per // UNROLL, step, 0)
    if last:
        half = total.shape[0] // 2
        keep[...] = total[:half]
        give[...] = total[half:]


def ladder(blocks, cols, live, w, pieces, start, last):
    count = len(pieces)
    per, occupied, _ = pieces[0].shape
    first = start is None
    vmem = pl.BlockSpec(memory_space=pltpu.VMEM)
    smem = pl.BlockSpec(memory_space=pltpu.SMEM)
    anyspace = pl.BlockSpec(memory_space=pl.ANY)
    whole = (ABT_X, occupied, BLK)
    half = jax.ShapeDtypeStruct((ABT_X // 2, occupied, BLK), jnp.float32)
    scratch = [
        pltpu.VMEM((count, per, BLK, BLK), w.dtype),
        pltpu.VMEM((count, per, occupied, BLK), w.dtype),
        pltpu.SemaphoreType.DMA((2, count)),
    ]
    if last:
        out_shape = [half, half]
        scratch = [pltpu.VMEM(whole, jnp.float32)] + scratch
    else:
        out_shape = [jax.ShapeDtypeStruct(whole, jnp.float32)]
    args = [blocks, cols, live, w, *pieces] + ([] if first else [start])
    out = pl.pallas_call(
        functools.partial(ladder_kernel, count, per, first, last),
        out_shape=out_shape,
        in_specs=[smem] * 3 + [anyspace] * (1 + count) + [vmem] * (not first),
        out_specs=[vmem] * len(out_shape),
        scratch_shapes=scratch,
        compiler_params=pltpu.CompilerParams(vmem_limit_bytes=40 * 1024 * 1024),
        cost_estimate=pl.CostEstimate(
            flops=2 * count * per * occupied * BLK * BLK,
            bytes_accessed=count * per * 2 * BLK * (BLK + occupied),
            transcendentals=0,
        ),
        name="ladder_tiles",
    )(*args)
    return out if last else out[0]


def per_device(amplitudes, virt_irreps, w_tiles, tile_rows, tile_cols):
    occupied = amplitudes.shape[0]
    peers = lax.axis_size("gx")
    groups = lax.axis_size("gy")
    me = lax.axis_index("gx")
    mine = lax.axis_index("gy")
    local_tiles = amplitudes.shape[1] // BLK
    row_count = local_tiles * peers
    slots = tile_rows.shape[0]
    per = slots // peers

    by_peer = tile_rows.reshape(peers, per) - jnp.arange(peers, dtype=jnp.int32)[:, None] * local_tiles
    wanted = lax.all_to_all(by_peer, "gx", 0, 0)
    order = jnp.arange(peers, dtype=jnp.int32) ^ me
    wanted = jnp.take(wanted, order, axis=0).reshape(slots)

    row_tile = mine * row_count + tile_rows
    col_tile = me * ABT_X + tile_cols
    live = (pair_irrep(row_tile, virt_irreps) == pair_irrep(col_tile, virt_irreps)).astype(
        jnp.float32
    )
    share = ABT_X // groups
    xs = groups // CORES
    owner = tile_cols // share
    other_core = (owner % CORES) ^ (mine % CORES)
    other_x = (owner // CORES) ^ (mine // CORES)
    cols = other_core * (ABT_X // CORES) + other_x * share + tile_cols % share

    outgoing = pick(amplitudes, wanted, peers, per)
    w = w_tiles.reshape(peers, per, BLK, BLK)
    arrived = [outgoing[0]]
    for k in range(1, peers):
        arrived.append(lax.ppermute(outgoing[k], "gx", [(i, i ^ k) for i in range(peers)]))
    near = peers // 2
    total = ladder(order[:near], cols, live, w, arrived[:near], None, False)
    keep, give = ladder(order[near:], cols, live, w, arrived[near:], total, True)

    got = lax.ppermute(give, "gy", [(i, i ^ 1) for i in range(groups)])
    keep = keep.reshape(xs, share, occupied, BLK)
    got = got.reshape(xs, share, occupied, BLK)
    result = keep[0] + got[0]
    for k in range(1, xs):
        result = result + lax.ppermute(
            keep[k] + got[k], "gy", [(i, i ^ (k * CORES)) for i in range(groups)]
        )
    return jnp.transpose(result, (1, 0, 2)).reshape(occupied, share * BLK)


def solution(mesh):
    in_specs = (
        P(None, ("gy", "gx")),
        P(),
        P(("gx", "gy"), None, None),
        P(("gx", "gy")),
        P(("gx", "gy")),
    )
    out_specs = P(None, ("gx", "gy"))
    return jax.shard_map(
        per_device, mesh=mesh, in_specs=in_specs, out_specs=out_specs, check_vma=False
    )
```

```python
import functools

import jax
import jax.numpy as jnp
from jax import lax
from jax.experimental import pallas as pl
from jax.experimental.pallas import tpu as pltpu
from jax.sharding import PartitionSpec as P

V = 1024
BLK = 128
ABT_X = 32
CORES = 2
UNROLL = 16
MIB = 1024 * 1024

VMEM_SPEC = pl.BlockSpec(memory_space=pltpu.VMEM)
SMEM_SPEC = pl.BlockSpec(memory_space=pltpu.SMEM)
ANY_SPEC = pl.BlockSpec(memory_space=pl.ANY)


def pair_irrep(tile, virt_irreps):
    first = tile * BLK // V // BLK
    second = tile * BLK % V // BLK
    return jnp.bitwise_xor(virt_irreps[first], virt_irreps[second])


def stage_kernel(source, held, sem):
    copy = pltpu.make_async_copy(source, held, sem)
    copy.start()
    copy.wait()


def stage(x):
    return pl.pallas_call(
        stage_kernel,
        out_shape=pltpu.VMEM(x.shape, x.dtype),
        in_specs=[ANY_SPEC],
        out_specs=VMEM_SPEC,
        scratch_shapes=[pltpu.SemaphoreType.DMA],
        compiler_params=pltpu.CompilerParams(vmem_limit_bytes=8 * MIB),
        cost_estimate=pl.CostEstimate(flops=0, bytes_accessed=2 * x.size, transcendentals=0),
        name="stage_amplitudes",
    )(pltpu.with_memory_space_constraint(x, pltpu.HBM))


def pick_kernel(per, local_tiles, me, before, rows, amp, out, after):
    base = me[0] * per
    origin = me[0] * local_tiles
    after[0] = before[0]

    def step(i, carry):
        lane = pl.multiple_of((rows[base + i] - origin) * BLK, BLK)
        out[i] = amp[:, pl.ds(lane, BLK)]
        return carry

    lax.fori_loop(0, per, step, 0, unroll=8)


def pick(me, before, rows, amp, per):
    occupied, width = amp.shape
    return pl.pallas_call(
        functools.partial(pick_kernel, per, width // BLK),
        out_shape=[
            jax.ShapeDtypeStruct((per, occupied, BLK), amp.dtype),
            jax.ShapeDtypeStruct((1,), jnp.int32),
        ],
        in_specs=[SMEM_SPEC] * 3 + [VMEM_SPEC],
        out_specs=[VMEM_SPEC, SMEM_SPEC],
        compiler_params=pltpu.CompilerParams(vmem_limit_bytes=8 * MIB),
        cost_estimate=pl.CostEstimate(
            flops=0, bytes_accessed=4 * per * occupied * BLK, transcendentals=0
        ),
        name="pick_tiles",
    )(me, before, rows, amp)


def add_products(per, base, cols, live, piece, weights, total):
    unroll = min(UNROLL, per)

    def step(i, carry):
        slots = [i * unroll + u for u in range(unroll)]
        products = [
            jnp.dot(piece[s], weights[s], preferred_element_type=jnp.float32) for s in slots
        ]
        for s, product in zip(slots, products):
            total[cols[base + s]] += product * live[base + s]
        return carry

    lax.fori_loop(0, per // unroll, step, 0)


def near_kernel(near, per, order, cols, live, w, *refs):
    pieces = refs[:near]
    total, far_w, near_w, sems = refs[near:]
    count = far_w.shape[0]
    copies = []
    for j in range(near + count):
        target = near_w.at[j] if j < near else far_w.at[j - near]
        copies.append(pltpu.make_async_copy(w.at[order[j]], target, sems.at[j]))
        copies[-1].start()
    total[...] = jnp.zeros_like(total)
    for j in range(near):
        copies[j].wait()
        add_products(per, order[j] * per, cols, live, pieces[j], near_w.at[j], total)
    for copy in copies[near:]:
        copy.wait()


def near_part(order, cols, live, w, pieces):
    near = len(pieces)
    peers = w.shape[0]
    per, occupied, _ = pieces[0].shape
    return pl.pallas_call(
        functools.partial(near_kernel, near, per),
        out_shape=[
            pltpu.VMEM((ABT_X, occupied, BLK), jnp.float32),
            pltpu.VMEM((peers - near, per, BLK, BLK), w.dtype),
        ],
        in_specs=[SMEM_SPEC] * 3 + [ANY_SPEC] + [VMEM_SPEC] * near,
        out_specs=[VMEM_SPEC, VMEM_SPEC],
        scratch_shapes=[
            pltpu.VMEM((near, per, BLK, BLK), w.dtype),
            pltpu.SemaphoreType.DMA((peers,)),
        ],
        compiler_params=pltpu.CompilerParams(vmem_limit_bytes=12 * MIB),
        cost_estimate=pl.CostEstimate(
            flops=2 * near * per * occupied * BLK * BLK,
            bytes_accessed=2 * w.size,
            transcendentals=0,
        ),
        name="near_products",
    )(order, cols, live, pltpu.with_memory_space_constraint(w, pltpu.HBM), *pieces)


def far_kernel(count, skip, per, last, order, cols, live, w, start, *refs):
    pieces = refs[:count]
    outs = refs[count:]
    total = start if last else outs[0]
    for j in range(count):
        base = order[order.shape[0] - w.shape[0] + skip + j] * per
        add_products(per, base, cols, live, pieces[j], w.at[skip + j], total)
    if last:
        at = 0
        for out in outs:
            out[...] = total[at : at + out.shape[0]]
            at += out.shape[0]


def far_part(order, cols, live, w, skip, start, pieces, last):
    count = len(pieces)
    per, occupied, _ = pieces[0].shape
    if last:
        out_shape = [jax.ShapeDtypeStruct((n, occupied, BLK), jnp.float32) for n in last]
        aliases = {}
    else:
        out_shape = [pltpu.VMEM(start.shape, start.dtype)]
        aliases = {4: 0}
    return pl.pallas_call(
        functools.partial(far_kernel, count, skip, per, last),
        out_shape=out_shape,
        in_specs=[SMEM_SPEC] * 3 + [VMEM_SPEC] * (2 + count),
        out_specs=[VMEM_SPEC] * len(out_shape),
        input_output_aliases=aliases,
        compiler_params=pltpu.CompilerParams(vmem_limit_bytes=8 * MIB),
        cost_estimate=pl.CostEstimate(
            flops=2 * count * per * occupied * BLK * BLK,
            bytes_accessed=4 * start.size,
            transcendentals=0,
        ),
        name="far_products",
    )(order, cols, live, w, start, *pieces)


def per_device(amplitudes, virt_irreps, w_tiles, tile_rows, tile_cols):
    occupied = amplitudes.shape[0]
    peers = lax.axis_size("gx")
    groups = lax.axis_size("gy")
    me = lax.axis_index("gx")
    mine = lax.axis_index("gy")
    row_count = amplitudes.shape[1] // BLK * peers
    per = tile_rows.shape[0] // peers
    near = peers // 2

    def swap(x, k):
        return lax.ppermute(x, "gx", [(i, i ^ k) for i in range(peers)])

    amp = stage(amplitudes)
    here = me.reshape(1)
    zero = jnp.zeros((1,), jnp.int32)
    arrived = {}
    for group in (range(near, peers), range(1, near)):
        rows = tile_rows + zero
        rows_of = [swap(rows, k) for k in group]
        for k, wanted in zip(group, rows_of):
            picked, zero = pick(here, zero, wanted, amp, per)
            arrived[k] = swap(picked, k)
    arrived[0], _ = pick(here, zero, tile_rows, amp, per)

    row_tile = mine * row_count + tile_rows
    col_tile = me * ABT_X + tile_cols
    live = (pair_irrep(row_tile, virt_irreps) == pair_irrep(col_tile, virt_irreps)).astype(
        jnp.float32
    )
    share = ABT_X // groups
    xs = groups // CORES
    owner = tile_cols // share
    other_core = (owner % CORES) ^ (mine % CORES)
    other_x = (owner // CORES) ^ (mine // CORES)
    cols = other_core * (ABT_X // CORES) + other_x * share + tile_cols % share
    order = jnp.arange(peers, dtype=jnp.int32) ^ me

    w = w_tiles.reshape(peers, per, BLK, BLK)
    total, far_w = near_part(order, cols, live, w, [arrived[k] for k in range(near)])
    half = near // 2
    (total,) = far_part(
        order, cols, live, far_w, 0, total, [arrived[near + k] for k in range(half)], None
    )
    sizes = (share, (xs - 1) * share) * CORES
    keep, keep_rest, give, give_rest = far_part(
        order, cols, live, far_w, half, total, [arrived[near + k] for k in range(half, near)], sizes
    )

    def swap_gy(x, k):
        return lax.ppermute(x, "gy", [(i, i ^ k) for i in range(groups)])

    rest = (keep_rest + swap_gy(give_rest, 1)).reshape(xs - 1, share, occupied, BLK)
    result = keep + swap_gy(give, 1)
    for k in range(1, xs):
        result = result + swap_gy(rest[k - 1], k * CORES)
    return jnp.transpose(result, (1, 0, 2)).reshape(occupied, share * BLK)


def solution(mesh):
    in_specs = (
        P(None, ("gy", "gx")),
        P(),
        P(("gx", "gy"), None, None),
        P(("gx", "gy")),
        P(("gx", "gy")),
    )
    out_specs = P(None, ("gx", "gy"))
    return jax.shard_map(
        per_device, mesh=mesh, in_specs=in_specs, out_specs=out_specs, check_vma=False
    )
```

```python
import functools

import jax
import jax.numpy as jnp
from jax import lax
from jax.experimental import pallas as pl
from jax.experimental.pallas import tpu as pltpu
from jax.sharding import PartitionSpec as P

V = 1024
BLK = 128
ABT_X = 32
CORES = 2
UNROLL = 16
MIB = 1024 * 1024

VMEM_SPEC = pl.BlockSpec(memory_space=pltpu.VMEM)
SMEM_SPEC = pl.BlockSpec(memory_space=pltpu.SMEM)
ANY_SPEC = pl.BlockSpec(memory_space=pl.ANY)


def pair_irrep(tile, virt_irreps):
    first = tile * BLK // V // BLK
    second = tile * BLK % V // BLK
    return jnp.bitwise_xor(virt_irreps[first], virt_irreps[second])


def stage_kernel(source, held, sem):
    copy = pltpu.make_async_copy(source, held, sem)
    copy.start()
    copy.wait()


def stage(x):
    return pl.pallas_call(
        stage_kernel,
        out_shape=pltpu.VMEM(x.shape, x.dtype),
        in_specs=[ANY_SPEC],
        out_specs=VMEM_SPEC,
        scratch_shapes=[pltpu.SemaphoreType.DMA],
        compiler_params=pltpu.CompilerParams(vmem_limit_bytes=8 * MIB),
        cost_estimate=pl.CostEstimate(flops=0, bytes_accessed=2 * x.size, transcendentals=0),
        name="stage_amplitudes",
    )(pltpu.with_memory_space_constraint(x, pltpu.HBM))


def pick_kernel(per, local_tiles, peers_of, me, before, wanted, amp, *refs):
    outs, after = refs[:-1], refs[-1]
    origin = me[0] * local_tiles
    after[0] = before[0]
    for peer, out in zip(peers_of(me[0]), outs):

        def step(i, carry):
            lane = pl.multiple_of((wanted[peer, i] - origin) * BLK, BLK)
            out[i] = amp[:, pl.ds(lane, BLK)]
            return carry

        lax.fori_loop(0, per, step, 0, unroll=8)


def near_pick_kernel(per, local_tiles, me, before, wanted, amp, out, after):
    near = out.shape[0]
    first = me[0] // near * near
    pick_kernel(
        per,
        local_tiles,
        lambda _: [first + j for j in range(near)],
        me,
        before,
        wanted,
        amp,
        *[out.at[j] for j in range(near)],
        after,
    )


def pick(kernel, shapes, me, before, wanted, amp):
    shapes = [jax.ShapeDtypeStruct(s, amp.dtype) for s in shapes]
    return pl.pallas_call(
        kernel,
        out_shape=shapes + [jax.ShapeDtypeStruct((1,), jnp.int32)],
        in_specs=[SMEM_SPEC] * 3 + [VMEM_SPEC],
        out_specs=[VMEM_SPEC] * len(shapes) + [SMEM_SPEC],
        compiler_params=pltpu.CompilerParams(vmem_limit_bytes=8 * MIB),
        cost_estimate=pl.CostEstimate(
            flops=0, bytes_accessed=4 * sum(s.size for s in shapes), transcendentals=0
        ),
        name="pick_tiles",
    )(me, before, wanted, amp)


def add_products(per, base, cols, live, piece, weights, total):
    unroll = min(UNROLL, per)

    def step(i, carry):
        slots = [i * unroll + u for u in range(unroll)]
        products = [
            jnp.dot(piece[s], weights[s], preferred_element_type=jnp.float32) for s in slots
        ]
        for s, product in zip(slots, products):
            total[cols[base + s]] += product * live[base + s]
        return carry

    lax.fori_loop(0, per // unroll, step, 0)


def near_kernel(per, order, cols, live, w, pieces, total, far_w, near_w, sems):
    near = pieces.shape[0]
    first = order[0] // near * near
    copies = []
    for j in range(near):
        copies.append(pltpu.make_async_copy(w.at[first + j], near_w.at[j], sems.at[j]))
    for j in range(far_w.shape[0]):
        copies.append(pltpu.make_async_copy(w.at[order[near + j]], far_w.at[j], sems.at[near + j]))
    for copy in copies:
        copy.start()
    total[...] = jnp.zeros_like(total)
    for j in range(near):
        copies[j].wait()
        add_products(per, (first + j) * per, cols, live, pieces.at[j], near_w.at[j], total)
    for copy in copies[near:]:
        copy.wait()


def near_part(order, cols, live, w, pieces):
    near, per, occupied, _ = pieces.shape
    peers = w.shape[0]
    return pl.pallas_call(
        functools.partial(near_kernel, per),
        out_shape=[
            pltpu.VMEM((ABT_X, occupied, BLK), jnp.float32),
            pltpu.VMEM((peers - near, per, BLK, BLK), w.dtype),
        ],
        in_specs=[SMEM_SPEC] * 3 + [ANY_SPEC, VMEM_SPEC],
        out_specs=[VMEM_SPEC, VMEM_SPEC],
        scratch_shapes=[
            pltpu.VMEM((near, per, BLK, BLK), w.dtype),
            pltpu.SemaphoreType.DMA((peers,)),
        ],
        compiler_params=pltpu.CompilerParams(vmem_limit_bytes=12 * MIB),
        cost_estimate=pl.CostEstimate(
            flops=2 * near * per * occupied * BLK * BLK,
            bytes_accessed=2 * w.size,
            transcendentals=0,
        ),
        name="near_products",
    )(order, cols, live, pltpu.with_memory_space_constraint(w, pltpu.HBM), pieces)


def far_kernel(count, skip, per, last, order, cols, live, w, start, *refs):
    pieces = refs[:count]
    outs = refs[count:]
    total = start if last else outs[0]
    for j in range(count):
        base = order[order.shape[0] - w.shape[0] + skip + j] * per
        add_products(per, base, cols, live, pieces[j], w.at[skip + j], total)
    if last:
        at = 0
        for out in outs:
            out[...] = total[at : at + out.shape[0]]
            at += out.shape[0]


def far_part(order, cols, live, w, skip, start, pieces, last):
    count = len(pieces)
    per, occupied, _ = pieces[0].shape
    if last:
        out_shape = [jax.ShapeDtypeStruct((n, occupied, BLK), jnp.float32) for n in last]
        aliases = {}
    else:
        out_shape = [pltpu.VMEM(start.shape, start.dtype)]
        aliases = {4: 0}
    return pl.pallas_call(
        functools.partial(far_kernel, count, skip, per, last),
        out_shape=out_shape,
        in_specs=[SMEM_SPEC] * 3 + [VMEM_SPEC] * (2 + count),
        out_specs=[VMEM_SPEC] * len(out_shape),
        input_output_aliases=aliases,
        compiler_params=pltpu.CompilerParams(vmem_limit_bytes=8 * MIB),
        cost_estimate=pl.CostEstimate(
            flops=2 * count * per * occupied * BLK * BLK,
            bytes_accessed=4 * start.size,
            transcendentals=0,
        ),
        name="far_products",
    )(order, cols, live, w, start, *pieces)


def per_device(amplitudes, virt_irreps, w_tiles, tile_rows, tile_cols):
    occupied = amplitudes.shape[0]
    peers = lax.axis_size("gx")
    groups = lax.axis_size("gy")
    me = lax.axis_index("gx")
    mine = lax.axis_index("gy")
    local_tiles = amplitudes.shape[1] // BLK
    row_count = local_tiles * peers
    per = tile_rows.shape[0] // peers
    near = peers // 2

    wanted = lax.all_to_all(tile_rows.reshape(peers, per), "gx", 0, 0)
    amp = stage(amplitudes)
    here = me.reshape(1)
    zero = jnp.zeros((1,), jnp.int32)
    shape = (per, occupied, BLK)
    far_kernel_of = functools.partial(
        pick_kernel, per, local_tiles, lambda i: [i ^ k for k in range(near, peers)]
    )
    *picked, zero = pick(far_kernel_of, [shape] * near, here, zero, wanted, amp)
    arrived = [
        lax.ppermute(x, "gx", [(i, i ^ k) for i in range(peers)])
        for k, x in zip(range(near, peers), picked)
    ]
    near_kernel_of = functools.partial(near_pick_kernel, per, local_tiles)
    picked, _ = pick(near_kernel_of, [(near, *shape)], here, zero, wanted, amp)
    halves = [list(range(near)), list(range(near, peers))]
    near_pieces = lax.all_to_all(picked, "gx", 0, 0, axis_index_groups=halves)

    row_tile = mine * row_count + tile_rows
    col_tile = me * ABT_X + tile_cols
    live = (pair_irrep(row_tile, virt_irreps) == pair_irrep(col_tile, virt_irreps)).astype(
        jnp.float32
    )
    share = ABT_X // groups
    xs = groups // CORES
    owner = tile_cols // share
    other_core = (owner % CORES) ^ (mine % CORES)
    other_x = (owner // CORES) ^ (mine // CORES)
    cols = other_core * (ABT_X // CORES) + other_x * share + tile_cols % share
    order = jnp.arange(peers, dtype=jnp.int32) ^ me

    w = w_tiles.reshape(peers, per, BLK, BLK)
    total, far_w = near_part(order, cols, live, w, near_pieces)
    half = near // 2
    (total,) = far_part(
        order, cols, live, far_w, 0, total, arrived[:half], None
    )
    sizes = (share, (xs - 1) * share) * CORES
    keep, keep_rest, give, give_rest = far_part(
        order, cols, live, far_w, half, total, arrived[half:], sizes
    )

    def swap_gy(x, k):
        return lax.ppermute(x, "gy", [(i, i ^ k) for i in range(groups)])

    rest = (keep_rest + swap_gy(give_rest, 1)).reshape(xs - 1, share, occupied, BLK)
    result = keep + swap_gy(give, 1)
    for k in range(1, xs):
        result = result + swap_gy(rest[k - 1], k * CORES)
    return jnp.transpose(result, (1, 0, 2)).reshape(occupied, share * BLK)


def solution(mesh):
    in_specs = (
        P(None, ("gy", "gx")),
        P(),
        P(("gx", "gy"), None, None),
        P(("gx", "gy")),
        P(("gx", "gy")),
    )
    out_specs = P(None, ("gx", "gy"))
    return jax.shard_map(
        per_device, mesh=mesh, in_specs=in_specs, out_specs=out_specs, check_vma=False
    )
```

```python
import functools

import jax
import jax.numpy as jnp
from jax import lax
from jax.experimental import pallas as pl
from jax.experimental.pallas import tpu as pltpu
from jax.sharding import PartitionSpec as P

V = 1024
BLK = 128
ABT_X = 32
CORES = 2
UNROLL = 16
MIB = 1024 * 1024

VMEM_SPEC = pl.BlockSpec(memory_space=pltpu.VMEM)
SMEM_SPEC = pl.BlockSpec(memory_space=pltpu.SMEM)
ANY_SPEC = pl.BlockSpec(memory_space=pl.ANY)


def pair_irrep(tile, virt_irreps):
    first = tile * BLK // V // BLK
    second = tile * BLK % V // BLK
    return jnp.bitwise_xor(virt_irreps[first], virt_irreps[second])


def stage_kernel(source, held, sem):
    copy = pltpu.make_async_copy(source, held, sem)
    copy.start()
    copy.wait()


def stage(x):
    return pl.pallas_call(
        stage_kernel,
        out_shape=pltpu.VMEM(x.shape, x.dtype),
        in_specs=[ANY_SPEC],
        out_specs=VMEM_SPEC,
        scratch_shapes=[pltpu.SemaphoreType.DMA],
        compiler_params=pltpu.CompilerParams(vmem_limit_bytes=8 * MIB),
        cost_estimate=pl.CostEstimate(flops=0, bytes_accessed=2 * x.size, transcendentals=0),
        name="stage_amplitudes",
    )(pltpu.with_memory_space_constraint(x, pltpu.HBM))


def pick_kernel(per, local_tiles, me, rows, amp, out):
    base = me[0] * per
    origin = me[0] * local_tiles

    def step(i, carry):
        lane = pl.multiple_of((rows[base + i] - origin) * BLK, BLK)
        out[i] = amp[:, pl.ds(lane, BLK)]
        return carry

    lax.fori_loop(0, per, step, 0, unroll=8)


def pick(me, rows, amp, per):
    occupied, width = amp.shape
    return pl.pallas_call(
        functools.partial(pick_kernel, per, width // BLK),
        out_shape=jax.ShapeDtypeStruct((per, occupied, BLK), amp.dtype),
        in_specs=[SMEM_SPEC, SMEM_SPEC, VMEM_SPEC],
        out_specs=VMEM_SPEC,
        compiler_params=pltpu.CompilerParams(vmem_limit_bytes=8 * MIB),
        cost_estimate=pl.CostEstimate(
            flops=0, bytes_accessed=4 * per * occupied * BLK, transcendentals=0
        ),
        name="pick_tiles",
    )(me, rows, amp)


def add_products(per, base, cols, live, piece, weights, total):
    unroll = min(UNROLL, per)

    def step(i, carry):
        slots = [i * unroll + u for u in range(unroll)]
        products = [
            jnp.dot(piece[s], weights[s], preferred_element_type=jnp.float32) for s in slots
        ]
        for s, product in zip(slots, products):
            total[cols[base + s]] += product * live[base + s]
        return carry

    lax.fori_loop(0, per // unroll, step, 0)


def ladder_kernel(peers_at, per, first, last, order, cols, live, w, *refs):
    count = len(peers_at)
    pieces, refs = refs[:count], refs[count:]
    if not first:
        start, refs = refs[0], refs[1:]
    *outs, held, sems = refs
    total = start if last else outs[0]
    copies = []
    for j, k in enumerate(peers_at):
        copies.append(pltpu.make_async_copy(w.at[order[k]], held.at[j], sems.at[j]))
        copies[-1].start()
    if first:
        total[...] = jnp.zeros_like(total)
    for j, k in enumerate(peers_at):
        copies[j].wait()
        add_products(per, order[k] * per, cols, live, pieces[j], held.at[j], total)
    if last:
        at = 0
        for out in outs:
            out[...] = total[at : at + out.shape[0]]
            at += out.shape[0]


def ladder(order, cols, live, w, start, arrived, peers_at, last=None):
    pieces = [arrived[k] for k in peers_at]
    count = len(pieces)
    per, occupied, _ = pieces[0].shape
    whole = (ABT_X, occupied, BLK)
    first = start is None
    if last:
        out_shape = [jax.ShapeDtypeStruct((n, occupied, BLK), jnp.float32) for n in last]
    else:
        out_shape = [pltpu.VMEM(whole, jnp.float32)]
    out = pl.pallas_call(
        functools.partial(ladder_kernel, peers_at, per, first, bool(last)),
        out_shape=out_shape,
        in_specs=[SMEM_SPEC] * 3 + [ANY_SPEC] + [VMEM_SPEC] * (count + (not first)),
        out_specs=[VMEM_SPEC] * len(out_shape),
        input_output_aliases={} if first or last else {4 + count: 0},
        scratch_shapes=[
            pltpu.VMEM((count, per, BLK, BLK), w.dtype),
            pltpu.SemaphoreType.DMA((count,)),
        ],
        compiler_params=pltpu.CompilerParams(vmem_limit_bytes=8 * MIB),
        cost_estimate=pl.CostEstimate(
            flops=2 * count * per * occupied * BLK * BLK,
            bytes_accessed=2 * count * per * BLK * BLK,
            transcendentals=0,
        ),
        name="ladder_products",
    )(order, cols, live, pltpu.with_memory_space_constraint(w, pltpu.HBM), *pieces, *([] if first else [start]))
    return out if last else out[0]


def per_device(amplitudes, virt_irreps, w_tiles, tile_rows, tile_cols):
    occupied = amplitudes.shape[0]
    peers = lax.axis_size("gx")
    groups = lax.axis_size("gy")
    me = lax.axis_index("gx")
    mine = lax.axis_index("gy")
    row_count = amplitudes.shape[1] // BLK * peers
    per = tile_rows.shape[0] // peers
    near = peers // 2

    def swap(x, k):
        return lax.ppermute(x, "gx", [(i, i ^ k) for i in range(peers)])

    amp = stage(amplitudes)
    here = me.reshape(1)
    arrived = {0: pick(here, tile_rows, amp, per)}
    for k in range(1, peers):
        arrived[k] = swap(pick(here, swap(tile_rows, k), amp, per), k)

    row_tile = mine * row_count + tile_rows
    col_tile = me * ABT_X + tile_cols
    live = (pair_irrep(row_tile, virt_irreps) == pair_irrep(col_tile, virt_irreps)).astype(
        jnp.float32
    )
    share = ABT_X // groups
    xs = groups // CORES
    owner = tile_cols // share
    other_core = (owner % CORES) ^ (mine % CORES)
    other_x = (owner // CORES) ^ (mine // CORES)
    cols = other_core * (ABT_X // CORES) + other_x * share + tile_cols % share
    order = jnp.arange(peers, dtype=jnp.int32) ^ me

    w = w_tiles.reshape(peers, per, BLK, BLK)
    quarter = near // 4
    far = [list(range(near + j * quarter, near + (j + 1) * quarter)) for j in range(4)]
    total = None
    for peers_at in (far[0], far[1], list(range(near)), far[2]):
        total = ladder(order, cols, live, w, total, arrived, peers_at)
    sizes = (share, (xs - 1) * share) * CORES
    keep, keep_rest, give, give_rest = ladder(order, cols, live, w, total, arrived, far[3], sizes)

    def swap_gy(x, k):
        return lax.ppermute(x, "gy", [(i, i ^ k) for i in range(groups)])

    rest = (keep_rest + swap_gy(give_rest, 1)).reshape(xs - 1, share, occupied, BLK)
    result = keep + swap_gy(give, 1)
    for k in range(1, xs):
        result = result + swap_gy(rest[k - 1], k * CORES)
    return jnp.transpose(result, (1, 0, 2)).reshape(occupied, share * BLK)


def solution(mesh):
    in_specs = (
        P(None, ("gy", "gx")),
        P(),
        P(("gx", "gy"), None, None),
        P(("gx", "gy")),
        P(("gx", "gy")),
    )
    out_specs = P(None, ("gx", "gy"))
    return jax.shard_map(
        per_device, mesh=mesh, in_specs=in_specs, out_specs=out_specs, check_vma=False
    )
```

```python
import functools

import jax
import jax.numpy as jnp
from jax import lax
from jax.experimental import pallas as pl
from jax.experimental.pallas import tpu as pltpu
from jax.sharding import PartitionSpec as P

V = 1024
BLK = 128
ABT_X = 32
CORES = 2
UNROLL = 16
MIB = 1024 * 1024

VMEM_SPEC = pl.BlockSpec(memory_space=pltpu.VMEM)
SMEM_SPEC = pl.BlockSpec(memory_space=pltpu.SMEM)
ANY_SPEC = pl.BlockSpec(memory_space=pl.ANY)


def pair_irrep(tile, virt_irreps):
    first = tile * BLK // V // BLK
    second = tile * BLK % V // BLK
    return jnp.bitwise_xor(virt_irreps[first], virt_irreps[second])


def pick_kernel(step, per, local_tiles, me, wanted, amp, out, sem):
    peer = me[0] ^ step
    origin = me[0] * local_tiles

    def start(i, carry):
        lane = pl.multiple_of((wanted[peer, i] - origin) * BLK, BLK)
        pltpu.make_async_copy(amp.at[:, pl.ds(lane, BLK)], out.at[i], sem).start()
        return carry

    lax.fori_loop(0, per, start, 0, unroll=8)
    pltpu.make_async_copy(out, out, sem).wait()


def pick(step, me, wanted, amp):
    occupied, width = amp.shape
    peers, per = wanted.shape
    return pl.pallas_call(
        functools.partial(pick_kernel, step, per, width // BLK),
        out_shape=pltpu.HBM((per, occupied, BLK), amp.dtype),
        in_specs=[SMEM_SPEC, SMEM_SPEC, ANY_SPEC],
        out_specs=pl.BlockSpec(memory_space=pltpu.HBM),
        scratch_shapes=[pltpu.SemaphoreType.DMA],
        compiler_params=pltpu.CompilerParams(vmem_limit_bytes=MIB),
        cost_estimate=pl.CostEstimate(
            flops=0, bytes_accessed=4 * per * occupied * BLK, transcendentals=0
        ),
        name="pick_tiles",
    )(me, wanted, pltpu.with_memory_space_constraint(amp, pltpu.HBM))


def add_products(per, base, cols, live, piece, weights, total):
    unroll = min(UNROLL, per)

    def step(i, carry):
        slots = [i * unroll + u for u in range(unroll)]
        products = [
            jnp.dot(piece[s], weights[s], preferred_element_type=jnp.float32) for s in slots
        ]
        for s, product in zip(slots, products):
            total[cols[base + s]] += product * live[base + s]
        return carry

    lax.fori_loop(0, per // unroll, step, 0)


def ladder_kernel(peers_at, ahead, per, first, last, order, cols, live, w, *refs):
    count = len(peers_at)
    pieces, refs = refs[:count], refs[count:]
    if not first:
        start, refs = refs[0], refs[1:]
    if last:
        outs, held, total = refs, w, start
    else:
        *outs, held, sems = refs
        total = outs[0]
    copies = []
    for j, k in enumerate([] if last else peers_at + ahead):
        target = held.at[j] if j < count else outs[1].at[j - count]
        copies.append(pltpu.make_async_copy(w.at[order[k]], target, sems.at[j]))
        copies[-1].start()
    if first:
        total[...] = jnp.zeros_like(total)
    for j, k in enumerate(peers_at):
        if not last:
            copies[j].wait()
        add_products(per, order[k] * per, cols, live, pieces[j], held.at[j], total)
    for copy in copies[count:]:
        copy.wait()
    if last:
        at = 0
        for out in outs:
            out[...] = total[at : at + out.shape[0]]
            at += out.shape[0]


def ladder(order, cols, live, w, start, arrived, peers_at, ahead=(), last=None):
    pieces = [arrived[k] for k in peers_at]
    count = len(pieces)
    per, occupied, _ = pieces[0].shape
    first = start is None
    scratch = []
    if last:
        out_shape = [jax.ShapeDtypeStruct((n, occupied, BLK), jnp.float32) for n in last]
    else:
        out_shape = [pltpu.VMEM((ABT_X, occupied, BLK), jnp.float32)]
        if ahead:
            out_shape.append(pltpu.VMEM((len(ahead), per, BLK, BLK), w.dtype))
        scratch = [
            pltpu.VMEM((count, per, BLK, BLK), w.dtype),
            pltpu.SemaphoreType.DMA((count + len(ahead),)),
        ]
        w = pltpu.with_memory_space_constraint(w, pltpu.HBM)
    return pl.pallas_call(
        functools.partial(ladder_kernel, peers_at, list(ahead), per, first, bool(last)),
        out_shape=out_shape,
        in_specs=[SMEM_SPEC] * 3
        + [VMEM_SPEC if last else ANY_SPEC]
        + [VMEM_SPEC] * (count + (not first)),
        out_specs=[VMEM_SPEC] * len(out_shape),
        input_output_aliases={} if first or last else {4 + count: 0},
        scratch_shapes=scratch,
        compiler_params=pltpu.CompilerParams(vmem_limit_bytes=8 * MIB),
        cost_estimate=pl.CostEstimate(
            flops=2 * count * per * occupied * BLK * BLK,
            bytes_accessed=2 * (count + len(ahead)) * per * BLK * BLK,
            transcendentals=0,
        ),
        name="ladder_products",
    )(order, cols, live, w, *pieces, *([] if first else [start]))


def per_device(amplitudes, virt_irreps, w_tiles, tile_rows, tile_cols):
    occupied = amplitudes.shape[0]
    peers = lax.axis_size("gx")
    groups = lax.axis_size("gy")
    me = lax.axis_index("gx")
    mine = lax.axis_index("gy")
    row_count = amplitudes.shape[1] // BLK * peers
    per = tile_rows.shape[0] // peers
    near = peers // 2

    def swap(x, k):
        return lax.ppermute(x, "gx", [(i, i ^ k) for i in range(peers)])

    wanted = lax.all_to_all(tile_rows.reshape(peers, per), "gx", 0, 0)
    here = me.reshape(1)
    arrived = {0: pick(0, here, wanted, amplitudes)}
    for k in range(1, peers):
        arrived[k] = swap(pick(k, here, wanted, amplitudes), k)

    row_tile = mine * row_count + tile_rows
    col_tile = me * ABT_X + tile_cols
    live = (pair_irrep(row_tile, virt_irreps) == pair_irrep(col_tile, virt_irreps)).astype(
        jnp.float32
    )
    share = ABT_X // groups
    xs = groups // CORES
    owner = tile_cols // share
    other_core = (owner % CORES) ^ (mine % CORES)
    other_x = (owner // CORES) ^ (mine // CORES)
    cols = other_core * (ABT_X // CORES) + other_x * share + tile_cols % share
    order = jnp.arange(peers, dtype=jnp.int32) ^ me

    w = w_tiles.reshape(peers, per, BLK, BLK)
    quarter = near // 4
    far = [list(range(near + j * quarter, near + (j + 1) * quarter)) for j in range(4)]
    args = (order, cols, live, w)
    (total,) = ladder(*args, None, arrived, far[0])
    (total,) = ladder(*args, total, arrived, far[1])
    total, held = ladder(*args, total, arrived, list(range(near)), ahead=far[3])
    (total,) = ladder(*args, total, arrived, far[2])
    sizes = (share, (xs - 1) * share) * CORES
    keep, keep_rest, give, give_rest = ladder(
        order, cols, live, held, total, arrived, far[3], last=sizes
    )

    def swap_gy(x, k):
        return lax.ppermute(x, "gy", [(i, i ^ k) for i in range(groups)])

    rest = (keep_rest + swap_gy(give_rest, 1)).reshape(xs - 1, share, occupied, BLK)
    result = keep + swap_gy(give, 1)
    for k in range(1, xs):
        result = result + swap_gy(rest[k - 1], k * CORES)
    return jnp.transpose(result, (1, 0, 2)).reshape(occupied, share * BLK)


def solution(mesh):
    in_specs = (
        P(None, ("gy", "gx")),
        P(),
        P(("gx", "gy"), None, None),
        P(("gx", "gy")),
        P(("gx", "gy")),
    )
    out_specs = P(None, ("gx", "gy"))
    return jax.shard_map(
        per_device, mesh=mesh, in_specs=in_specs, out_specs=out_specs, check_vma=False
    )
```

```python
import functools

import jax
import jax.numpy as jnp
from jax import lax
from jax.experimental import pallas as pl
from jax.experimental.pallas import tpu as pltpu
from jax.sharding import PartitionSpec as P

V = 1024
BLK = 128
ABT_X = 32
CORES = 2
UNROLL = 16
MIB = 1024 * 1024

VMEM_SPEC = pl.BlockSpec(memory_space=pltpu.VMEM)
SMEM_SPEC = pl.BlockSpec(memory_space=pltpu.SMEM)
ANY_SPEC = pl.BlockSpec(memory_space=pl.ANY)


def pair_irrep(tile, virt_irreps):
    first = tile * BLK // V // BLK
    second = tile * BLK % V // BLK
    return jnp.bitwise_xor(virt_irreps[first], virt_irreps[second])


def stage_kernel(source, held, sem):
    copy = pltpu.make_async_copy(source, held, sem)
    copy.start()
    copy.wait()


def stage(x):
    return pl.pallas_call(
        stage_kernel,
        out_shape=pltpu.VMEM(x.shape, x.dtype),
        in_specs=[ANY_SPEC],
        out_specs=VMEM_SPEC,
        scratch_shapes=[pltpu.SemaphoreType.DMA],
        compiler_params=pltpu.CompilerParams(vmem_limit_bytes=8 * MIB),
        cost_estimate=pl.CostEstimate(flops=0, bytes_accessed=2 * x.size, transcendentals=0),
        name="stage_amplitudes",
    )(pltpu.with_memory_space_constraint(x, pltpu.HBM))


def pick_kernel(per, local_tiles, me, rows, amp, *refs):
    out = refs[-1]
    base = me[0] * per
    origin = me[0] * local_tiles

    def step(i, carry):
        lane = pl.multiple_of((rows[base + i] - origin) * BLK, BLK)
        out[i] = amp[:, pl.ds(lane, BLK)]
        return carry

    lax.fori_loop(0, per, step, 0, unroll=8)


def pick(me, rows, amp, per, after=()):
    occupied, width = amp.shape
    return pl.pallas_call(
        functools.partial(pick_kernel, per, width // BLK),
        out_shape=jax.ShapeDtypeStruct((per, occupied, BLK), amp.dtype),
        in_specs=[SMEM_SPEC, SMEM_SPEC, VMEM_SPEC] + [ANY_SPEC] * len(after),
        out_specs=VMEM_SPEC,
        compiler_params=pltpu.CompilerParams(vmem_limit_bytes=8 * MIB),
        cost_estimate=pl.CostEstimate(
            flops=0, bytes_accessed=4 * per * occupied * BLK, transcendentals=0
        ),
        name="pick_tiles",
    )(me, rows, amp, *after)


def add_products(per, base, cols, live, piece, weights, total):
    unroll = min(UNROLL, per)

    def step(i, carry):
        slots = [i * unroll + u for u in range(unroll)]
        products = [
            jnp.dot(piece[s], weights[s], preferred_element_type=jnp.float32) for s in slots
        ]
        for s, product in zip(slots, products):
            total[cols[base + s]] += product * live[base + s]
        return carry

    lax.fori_loop(0, per // unroll, step, 0)


def ladder_kernel(peers_at, ahead, per, first, last, order, cols, live, w, *refs):
    count = len(peers_at)
    pieces, refs = refs[:count], refs[count:]
    if not first:
        start, refs = refs[0], refs[1:]
    if last:
        outs, held, total = refs, w, start
    else:
        *outs, held, sems = refs
        total = outs[0]
    copies = []
    for j, k in enumerate([] if last else peers_at + ahead):
        target = held.at[j] if j < count else outs[1].at[j - count]
        copies.append(pltpu.make_async_copy(w.at[order[k]], target, sems.at[j]))
        copies[-1].start()
    if first:
        total[...] = jnp.zeros_like(total)
    for j, k in enumerate(peers_at):
        if not last:
            copies[j].wait()
        add_products(per, order[k] * per, cols, live, pieces[j], held.at[j], total)
    for copy in copies[count:]:
        copy.wait()
    if last:
        at = 0
        for out in outs:
            out[...] = total[at : at + out.shape[0]]
            at += out.shape[0]


def ladder(order, cols, live, w, start, arrived, peers_at, ahead=(), last=None):
    pieces = [arrived[k] for k in peers_at]
    count = len(pieces)
    per, occupied, _ = pieces[0].shape
    first = start is None
    scratch = []
    if last:
        out_shape = [jax.ShapeDtypeStruct((n, occupied, BLK), jnp.float32) for n in last]
    else:
        out_shape = [pltpu.VMEM((ABT_X, occupied, BLK), jnp.float32)]
        if ahead:
            out_shape.append(pltpu.VMEM((len(ahead), per, BLK, BLK), w.dtype))
        scratch = [
            pltpu.VMEM((count, per, BLK, BLK), w.dtype),
            pltpu.SemaphoreType.DMA((count + len(ahead),)),
        ]
        w = pltpu.with_memory_space_constraint(w, pltpu.HBM)
    return pl.pallas_call(
        functools.partial(ladder_kernel, peers_at, list(ahead), per, first, bool(last)),
        out_shape=out_shape,
        in_specs=[SMEM_SPEC] * 3
        + [VMEM_SPEC if last else ANY_SPEC]
        + [VMEM_SPEC] * (count + (not first)),
        out_specs=[VMEM_SPEC] * len(out_shape),
        input_output_aliases={} if first or last else {4 + count: 0},
        scratch_shapes=scratch,
        compiler_params=pltpu.CompilerParams(vmem_limit_bytes=8 * MIB),
        cost_estimate=pl.CostEstimate(
            flops=2 * count * per * occupied * BLK * BLK,
            bytes_accessed=2 * (count + len(ahead)) * per * BLK * BLK,
            transcendentals=0,
        ),
        name="ladder_products",
    )(order, cols, live, w, *pieces, *([] if first else [start]))


def per_device(amplitudes, virt_irreps, w_tiles, tile_rows, tile_cols):
    occupied = amplitudes.shape[0]
    peers = lax.axis_size("gx")
    groups = lax.axis_size("gy")
    me = lax.axis_index("gx")
    mine = lax.axis_index("gy")
    row_count = amplitudes.shape[1] // BLK * peers
    per = tile_rows.shape[0] // peers
    near = peers // 2

    def swap(x, k):
        return lax.ppermute(x, "gx", [(i, i ^ k) for i in range(peers)])

    rows = [tile_rows] + [swap(tile_rows, k) for k in range(1, peers)]
    amp = stage(amplitudes)
    here = me.reshape(1)
    arrived = {0: pick(here, tile_rows, amp, per)}
    for k in range(1, peers):
        after = [rows[j] for j in range(1, peers) if j != k] if k >= near else ()
        arrived[k] = swap(pick(here, rows[k], amp, per, after), k)

    row_tile = mine * row_count + tile_rows
    col_tile = me * ABT_X + tile_cols
    live = (pair_irrep(row_tile, virt_irreps) == pair_irrep(col_tile, virt_irreps)).astype(
        jnp.float32
    )
    share = ABT_X // groups
    xs = groups // CORES
    owner = tile_cols // share
    other_core = (owner % CORES) ^ (mine % CORES)
    other_x = (owner // CORES) ^ (mine // CORES)
    cols = other_core * (ABT_X // CORES) + other_x * share + tile_cols % share
    order = jnp.arange(peers, dtype=jnp.int32) ^ me

    w = w_tiles.reshape(peers, per, BLK, BLK)
    quarter = near // 4
    far = [list(range(near + j * quarter, near + (j + 1) * quarter)) for j in range(4)]
    args = (order, cols, live, w)
    (total,) = ladder(*args, None, arrived, far[0])
    (total,) = ladder(*args, total, arrived, far[1])
    total, held = ladder(*args, total, arrived, list(range(near)), ahead=far[3])
    (total,) = ladder(*args, total, arrived, far[2])
    sizes = (share, (xs - 1) * share) * CORES
    keep, keep_rest, give, give_rest = ladder(
        order, cols, live, held, total, arrived, far[3], last=sizes
    )

    def swap_gy(x, k):
        return lax.ppermute(x, "gy", [(i, i ^ k) for i in range(groups)])

    rest = (keep_rest + swap_gy(give_rest, 1)).reshape(xs - 1, share, occupied, BLK)
    result = keep + swap_gy(give, 1)
    for k in range(1, xs):
        result = result + swap_gy(rest[k - 1], k * CORES)
    return jnp.transpose(result, (1, 0, 2)).reshape(occupied, share * BLK)


def solution(mesh):
    in_specs = (
        P(None, ("gy", "gx")),
        P(),
        P(("gx", "gy"), None, None),
        P(("gx", "gy")),
        P(("gx", "gy")),
    )
    out_specs = P(None, ("gx", "gy"))
    return jax.shard_map(
        per_device, mesh=mesh, in_specs=in_specs, out_specs=out_specs, check_vma=False
    )
```

```python
import functools

import jax
import jax.numpy as jnp
from jax import lax
from jax.experimental import pallas as pl
from jax.experimental.pallas import tpu as pltpu
from jax.sharding import PartitionSpec as P

V = 1024
BLK = 128
ABT_X = 32
CORES = 2
UNROLL = 16
MIB = 1024 * 1024

VMEM_SPEC = pl.BlockSpec(memory_space=pltpu.VMEM)
SMEM_SPEC = pl.BlockSpec(memory_space=pltpu.SMEM)
ANY_SPEC = pl.BlockSpec(memory_space=pl.ANY)


def pair_irrep(tile, virt_irreps):
    first = tile * BLK // V // BLK
    second = tile * BLK % V // BLK
    return jnp.bitwise_xor(virt_irreps[first], virt_irreps[second])


def stage_kernel(source, held, sem):
    copy = pltpu.make_async_copy(source, held, sem)
    copy.start()
    copy.wait()


def stage(x):
    return pl.pallas_call(
        stage_kernel,
        out_shape=pltpu.VMEM(x.shape, x.dtype),
        in_specs=[ANY_SPEC],
        out_specs=VMEM_SPEC,
        scratch_shapes=[pltpu.SemaphoreType.DMA],
        compiler_params=pltpu.CompilerParams(vmem_limit_bytes=8 * MIB),
        cost_estimate=pl.CostEstimate(flops=0, bytes_accessed=2 * x.size, transcendentals=0),
        name="stage_amplitudes",
    )(pltpu.with_memory_space_constraint(x, pltpu.HBM))


def pick_kernel(first, per, local_tiles, me, rows, amp, *refs):
    out = refs[-1]
    base = first + me[0] * per
    origin = me[0] * local_tiles

    def step(i, carry):
        lane = pl.multiple_of((rows[base + i] - origin) * BLK, BLK)
        out[i] = amp[:, pl.ds(lane, BLK)]
        return carry

    lax.fori_loop(0, per, step, 0, unroll=8)


def pick(me, rows, first, amp, per, after=()):
    occupied, width = amp.shape
    return pl.pallas_call(
        functools.partial(pick_kernel, first, per, width // BLK),
        out_shape=jax.ShapeDtypeStruct((per, occupied, BLK), amp.dtype),
        in_specs=[SMEM_SPEC, SMEM_SPEC, VMEM_SPEC] + [ANY_SPEC] * len(after),
        out_specs=VMEM_SPEC,
        compiler_params=pltpu.CompilerParams(vmem_limit_bytes=8 * MIB),
        cost_estimate=pl.CostEstimate(
            flops=0, bytes_accessed=4 * per * occupied * BLK, transcendentals=0
        ),
        name="pick_tiles",
    )(me, rows, amp, *after)


def add_products(per, base, cols, live, piece, weights, total):
    unroll = min(UNROLL, per)

    def step(i, carry):
        slots = [i * unroll + u for u in range(unroll)]
        products = [
            jnp.dot(piece[s], weights[s], preferred_element_type=jnp.float32) for s in slots
        ]
        for s, product in zip(slots, products):
            total[cols[base + s]] += product * live[base + s]
        return carry

    lax.fori_loop(0, per // unroll, step, 0)


def ladder_kernel(peers_at, ahead, per, first, last, order, cols, live, w, *refs):
    count = len(peers_at)
    pieces, refs = refs[:count], refs[count:]
    if not first:
        start, refs = refs[0], refs[1:]
    if last:
        outs, held, total = refs, w, start
    else:
        *outs, held, sems = refs
        total = outs[0]
    copies = []
    for j, k in enumerate([] if last else peers_at + ahead):
        target = held.at[j] if j < count else outs[1].at[j - count]
        copies.append(pltpu.make_async_copy(w.at[order[k]], target, sems.at[j]))
        copies[-1].start()
    if first:
        total[...] = jnp.zeros_like(total)
    for j, k in enumerate(peers_at):
        if not last:
            copies[j].wait()
        add_products(per, order[k] * per, cols, live, pieces[j], held.at[j], total)
    for copy in copies[count:]:
        copy.wait()
    if last:
        at = 0
        for out in outs:
            out[...] = total[at : at + out.shape[0]]
            at += out.shape[0]


def ladder(order, cols, live, w, start, arrived, peers_at, ahead=(), last=None):
    pieces = [arrived[k] for k in peers_at]
    count = len(pieces)
    per, occupied, _ = pieces[0].shape
    first = start is None
    scratch = []
    if last:
        out_shape = [jax.ShapeDtypeStruct((n, occupied, BLK), jnp.float32) for n in last]
    else:
        out_shape = [pltpu.VMEM((ABT_X, occupied, BLK), jnp.float32)]
        if ahead:
            out_shape.append(pltpu.VMEM((len(ahead), per, BLK, BLK), w.dtype))
        scratch = [
            pltpu.VMEM((count, per, BLK, BLK), w.dtype),
            pltpu.SemaphoreType.DMA((count + len(ahead),)),
        ]
        w = pltpu.with_memory_space_constraint(w, pltpu.HBM)
    return pl.pallas_call(
        functools.partial(ladder_kernel, peers_at, list(ahead), per, first, bool(last)),
        out_shape=out_shape,
        in_specs=[SMEM_SPEC] * 3
        + [VMEM_SPEC if last else ANY_SPEC]
        + [VMEM_SPEC] * (count + (not first)),
        out_specs=[VMEM_SPEC] * len(out_shape),
        input_output_aliases={} if first or last else {4 + count: 0},
        scratch_shapes=scratch,
        compiler_params=pltpu.CompilerParams(vmem_limit_bytes=8 * MIB),
        cost_estimate=pl.CostEstimate(
            flops=2 * count * per * occupied * BLK * BLK,
            bytes_accessed=2 * (count + len(ahead)) * per * BLK * BLK,
            transcendentals=0,
        ),
        name="ladder_products",
    )(order, cols, live, w, *pieces, *([] if first else [start]))


def per_device(amplitudes, virt_irreps, w_tiles, tile_rows, tile_cols):
    occupied = amplitudes.shape[0]
    peers = lax.axis_size("gx")
    groups = lax.axis_size("gy")
    me = lax.axis_index("gx")
    mine = lax.axis_index("gy")
    row_count = amplitudes.shape[1] // BLK * peers
    per = tile_rows.shape[0] // peers
    near = peers // 2

    def swap(x, k):
        return lax.ppermute(x, "gx", [(i, i ^ k) for i in range(peers)])

    slots = tile_rows.shape[0]
    rows, bit = tile_rows, 1
    while bit < near:
        rows = jnp.concatenate([rows, swap(rows, bit)])
        bit *= 2
    far_rows = swap(rows, near)

    amp = stage(amplitudes)
    here = me.reshape(1)
    quarter = near // 4
    far = [list(range(near + j * quarter, near + (j + 1) * quarter)) for j in range(4)]
    arrived = {0: pick(here, tile_rows, 0, amp, per)}
    for k in far[0] + far[1] + list(range(1, near)) + far[2] + far[3]:
        source, first = (far_rows, (k - near) * slots) if k >= near else (rows, k * slots)
        after = ()
        if k in far[2]:
            after = (arrived[k - quarter],)
        if k in far[3]:
            after = (arrived[k - 2 * quarter], arrived[k - 3 * quarter])
        arrived[k] = swap(pick(here, source, first, amp, per, after), k)

    row_tile = mine * row_count + tile_rows
    col_tile = me * ABT_X + tile_cols
    live = (pair_irrep(row_tile, virt_irreps) == pair_irrep(col_tile, virt_irreps)).astype(
        jnp.float32
    )
    share = ABT_X // groups
    xs = groups // CORES
    owner = tile_cols // share
    other_core = (owner % CORES) ^ (mine % CORES)
    other_x = (owner // CORES) ^ (mine // CORES)
    cols = other_core * (ABT_X // CORES) + other_x * share + tile_cols % share
    order = jnp.arange(peers, dtype=jnp.int32) ^ me

    w = w_tiles.reshape(peers, per, BLK, BLK)
    args = (order, cols, live, w)
    (total,) = ladder(*args, None, arrived, far[0])
    (total,) = ladder(*args, total, arrived, far[1])
    total, held = ladder(*args, total, arrived, list(range(near)), ahead=far[3])
    (total,) = ladder(*args, total, arrived, far[2])
    sizes = (share, (xs - 1) * share) * CORES
    keep, keep_rest, give, give_rest = ladder(
        order, cols, live, held, total, arrived, far[3], last=sizes
    )

    def swap_gy(x, k):
        return lax.ppermute(x, "gy", [(i, i ^ k) for i in range(groups)])

    rest = (keep_rest + swap_gy(give_rest, 1)).reshape(xs - 1, share, occupied, BLK)
    result = keep + swap_gy(give, 1)
    for k in range(1, xs):
        result = result + swap_gy(rest[k - 1], k * CORES)
    return jnp.transpose(result, (1, 0, 2)).reshape(occupied, share * BLK)


def solution(mesh):
    in_specs = (
        P(None, ("gy", "gx")),
        P(),
        P(("gx", "gy"), None, None),
        P(("gx", "gy")),
        P(("gx", "gy")),
    )
    out_specs = P(None, ("gx", "gy"))
    return jax.shard_map(
        per_device, mesh=mesh, in_specs=in_specs, out_specs=out_specs, check_vma=False
    )
```

```python
import functools

import jax
import jax.numpy as jnp
from jax import lax
from jax.experimental import pallas as pl
from jax.experimental.pallas import tpu as pltpu
from jax.sharding import PartitionSpec as P

V = 1024
BLK = 128
ABT_X = 32
CORES = 2
UNROLL = 16
MIB = 1024 * 1024

VMEM_SPEC = pl.BlockSpec(memory_space=pltpu.VMEM)
SMEM_SPEC = pl.BlockSpec(memory_space=pltpu.SMEM)
ANY_SPEC = pl.BlockSpec(memory_space=pl.ANY)


def pair_irrep(tile, virt_irreps):
    first = tile * BLK // V // BLK
    second = tile * BLK % V // BLK
    return jnp.bitwise_xor(virt_irreps[first], virt_irreps[second])


def stage_kernel(source, held, sem):
    copy = pltpu.make_async_copy(source, held, sem)
    copy.start()
    copy.wait()


def stage(x):
    return pl.pallas_call(
        stage_kernel,
        out_shape=pltpu.VMEM(x.shape, x.dtype),
        in_specs=[ANY_SPEC],
        out_specs=VMEM_SPEC,
        scratch_shapes=[pltpu.SemaphoreType.DMA],
        compiler_params=pltpu.CompilerParams(vmem_limit_bytes=8 * MIB),
        cost_estimate=pl.CostEstimate(flops=0, bytes_accessed=2 * x.size, transcendentals=0),
        name="stage_amplitudes",
    )(pltpu.with_memory_space_constraint(x, pltpu.HBM))


def pick_kernel(first, per, local_tiles, me, rows, amp, *refs):
    out = refs[-1]
    base = first + me[0] * per
    origin = me[0] * local_tiles

    def step(i, carry):
        lane = pl.multiple_of((rows[base + i] - origin) * BLK, BLK)
        out[i] = amp[:, pl.ds(lane, BLK)]
        return carry

    lax.fori_loop(0, per, step, 0, unroll=8)


def pick(me, rows, first, amp, per, after=()):
    occupied, width = amp.shape
    return pl.pallas_call(
        functools.partial(pick_kernel, first, per, width // BLK),
        out_shape=jax.ShapeDtypeStruct((per, occupied, BLK), amp.dtype),
        in_specs=[SMEM_SPEC, SMEM_SPEC, VMEM_SPEC] + [ANY_SPEC] * len(after),
        out_specs=VMEM_SPEC,
        compiler_params=pltpu.CompilerParams(vmem_limit_bytes=8 * MIB),
        cost_estimate=pl.CostEstimate(
            flops=0, bytes_accessed=4 * per * occupied * BLK, transcendentals=0
        ),
        name="pick_tiles",
    )(me, rows, amp, *after)


def add_products(per, base, cols, live, piece, weights, total):
    unroll = min(UNROLL, per)

    def step(i, carry):
        slots = [i * unroll + u for u in range(unroll)]
        products = [
            jnp.dot(piece[s], weights[s], preferred_element_type=jnp.float32) for s in slots
        ]
        for s, product in zip(slots, products):
            total[cols[base + s]] += product * live[base + s]
        return carry

    lax.fori_loop(0, per // unroll, step, 0)


def ladder_kernel(peers_at, ahead, per, first, last, order, cols, live, w, *refs):
    count = len(peers_at)
    pieces, refs = refs[:count], refs[count:]
    if not first:
        start, refs = refs[0], refs[1:]
    if last:
        outs, held, total = refs, w, start
    else:
        *outs, held, sems = refs
        total = outs[0]
    copies = []
    for j, k in enumerate([] if last else peers_at + ahead):
        target = held.at[j] if j < count else outs[1].at[j - count]
        copies.append(pltpu.make_async_copy(w.at[order[k]], target, sems.at[j]))
        copies[-1].start()
    if first:
        total[...] = jnp.zeros_like(total)
    for j, k in enumerate(peers_at):
        if not last:
            copies[j].wait()
        add_products(per, order[k] * per, cols, live, pieces[j], held.at[j], total)
    for copy in copies[count:]:
        copy.wait()
    if last:
        at = 0
        for out in outs:
            out[...] = total[at : at + out.shape[0]]
            at += out.shape[0]


def ladder(order, cols, live, w, start, arrived, peers_at, ahead=(), last=None):
    pieces = [arrived[k] for k in peers_at]
    count = len(pieces)
    per, occupied, _ = pieces[0].shape
    first = start is None
    scratch = []
    if last:
        out_shape = [jax.ShapeDtypeStruct((n, occupied, BLK), jnp.float32) for n in last]
    else:
        out_shape = [pltpu.VMEM((ABT_X, occupied, BLK), jnp.float32)]
        if ahead:
            out_shape.append(pltpu.VMEM((len(ahead), per, BLK, BLK), w.dtype))
        scratch = [
            pltpu.VMEM((count, per, BLK, BLK), w.dtype),
            pltpu.SemaphoreType.DMA((count + len(ahead),)),
        ]
        w = pltpu.with_memory_space_constraint(w, pltpu.HBM)
    return pl.pallas_call(
        functools.partial(ladder_kernel, peers_at, list(ahead), per, first, bool(last)),
        out_shape=out_shape,
        in_specs=[SMEM_SPEC] * 3
        + [VMEM_SPEC if last else ANY_SPEC]
        + [VMEM_SPEC] * (count + (not first)),
        out_specs=[VMEM_SPEC] * len(out_shape),
        input_output_aliases={} if first or last else {4 + count: 0},
        scratch_shapes=scratch,
        compiler_params=pltpu.CompilerParams(vmem_limit_bytes=8 * MIB),
        cost_estimate=pl.CostEstimate(
            flops=2 * count * per * occupied * BLK * BLK,
            bytes_accessed=2 * (count + len(ahead)) * per * BLK * BLK,
            transcendentals=0,
        ),
        name="ladder_products",
    )(order, cols, live, w, *pieces, *([] if first else [start]))


def per_device(amplitudes, virt_irreps, w_tiles, tile_rows, tile_cols):
    occupied = amplitudes.shape[0]
    peers = lax.axis_size("gx")
    groups = lax.axis_size("gy")
    me = lax.axis_index("gx")
    mine = lax.axis_index("gy")
    row_count = amplitudes.shape[1] // BLK * peers
    per = tile_rows.shape[0] // peers
    near = peers // 2

    def swap(x, k):
        return lax.ppermute(x, "gx", [(i, i ^ k) for i in range(peers)])

    slots = tile_rows.shape[0]
    near_even, bit = tile_rows, 2
    while bit < near:
        near_even = jnp.concatenate([near_even, swap(near_even, bit)])
        bit *= 2
    far_even = swap(near_even, near)
    odd = swap(jnp.concatenate([near_even, far_even]), 1)

    amp = stage(amplitudes)
    here = me.reshape(1)
    quarter = near // 4
    far_order = list(range(near, peers, 2)) + list(range(near + 1, peers, 2))
    far = [far_order[j * quarter : (j + 1) * quarter] for j in range(4)]
    arrived = {0: pick(here, tile_rows, 0, amp, per)}
    for k in far[0] + far[1] + list(range(1, near)) + far[2] + far[3]:
        source, first = (odd, k // 2) if k % 2 else (near_even, k // 2)
        if k % 2 == 0 and k >= near:
            source, first = far_even, (k - near) // 2
        after = ()
        if k in far[2]:
            after = (arrived[far[1][far[2].index(k)]],)
        if k in far[3]:
            after = (arrived[far[1][far[3].index(k)]], arrived[far[0][far[3].index(k)]])
        arrived[k] = swap(pick(here, source, first * slots, amp, per, after), k)

    row_tile = mine * row_count + tile_rows
    col_tile = me * ABT_X + tile_cols
    live = (pair_irrep(row_tile, virt_irreps) == pair_irrep(col_tile, virt_irreps)).astype(
        jnp.float32
    )
    share = ABT_X // groups
    xs = groups // CORES
    owner = tile_cols // share
    other_core = (owner % CORES) ^ (mine % CORES)
    other_x = (owner // CORES) ^ (mine // CORES)
    cols = other_core * (ABT_X // CORES) + other_x * share + tile_cols % share
    order = jnp.arange(peers, dtype=jnp.int32) ^ me

    w = w_tiles.reshape(peers, per, BLK, BLK)
    args = (order, cols, live, w)
    (total,) = ladder(*args, None, arrived, far[0])
    (total,) = ladder(*args, total, arrived, far[1])
    total, held = ladder(*args, total, arrived, list(range(near)), ahead=far[3])
    (total,) = ladder(*args, total, arrived, far[2])
    sizes = (share, (xs - 1) * share) * CORES
    keep, keep_rest, give, give_rest = ladder(
        order, cols, live, held, total, arrived, far[3], last=sizes
    )

    def swap_gy(x, k):
        return lax.ppermute(x, "gy", [(i, i ^ k) for i in range(groups)])

    rest = (keep_rest + swap_gy(give_rest, 1)).reshape(xs - 1, share, occupied, BLK)
    result = keep + swap_gy(give, 1)
    for k in range(1, xs):
        result = result + swap_gy(rest[k - 1], k * CORES)
    return jnp.transpose(result, (1, 0, 2)).reshape(occupied, share * BLK)


def solution(mesh):
    in_specs = (
        P(None, ("gy", "gx")),
        P(),
        P(("gx", "gy"), None, None),
        P(("gx", "gy")),
        P(("gx", "gy")),
    )
    out_specs = P(None, ("gx", "gy"))
    return jax.shard_map(
        per_device, mesh=mesh, in_specs=in_specs, out_specs=out_specs, check_vma=False
    )
```

```python
import functools

import jax
import jax.numpy as jnp
from jax import lax
from jax.experimental import pallas as pl
from jax.experimental.pallas import tpu as pltpu
from jax.sharding import PartitionSpec as P

V = 1024
BLK = 128
ABT_X = 32
CORES = 2
UNROLL = 16
MIB = 1024 * 1024

VMEM_SPEC = pl.BlockSpec(memory_space=pltpu.VMEM)
SMEM_SPEC = pl.BlockSpec(memory_space=pltpu.SMEM)
ANY_SPEC = pl.BlockSpec(memory_space=pl.ANY)


def pair_irrep(tile, virt_irreps):
    first = tile * BLK // V // BLK
    second = tile * BLK % V // BLK
    return jnp.bitwise_xor(virt_irreps[first], virt_irreps[second])


def stage_kernel(source, held, sem):
    copy = pltpu.make_async_copy(source, held, sem)
    copy.start()
    copy.wait()


def stage(x):
    return pl.pallas_call(
        stage_kernel,
        out_shape=pltpu.VMEM(x.shape, x.dtype),
        in_specs=[ANY_SPEC],
        out_specs=VMEM_SPEC,
        scratch_shapes=[pltpu.SemaphoreType.DMA],
        compiler_params=pltpu.CompilerParams(vmem_limit_bytes=8 * MIB),
        cost_estimate=pl.CostEstimate(flops=0, bytes_accessed=2 * x.size, transcendentals=0),
        name="stage_amplitudes",
    )(pltpu.with_memory_space_constraint(x, pltpu.HBM))


def pick_kernel(first, per, local_tiles, me, rows, amp, *refs):
    out = refs[-1]
    base = first + me[0] * per
    origin = me[0] * local_tiles

    def step(i, carry):
        lane = pl.multiple_of((rows[base + i] - origin) * BLK, BLK)
        out[i] = amp[:, pl.ds(lane, BLK)]
        return carry

    lax.fori_loop(0, per, step, 0, unroll=8)


def pick(me, rows, first, amp, per, after=()):
    occupied, width = amp.shape
    return pl.pallas_call(
        functools.partial(pick_kernel, first, per, width // BLK),
        out_shape=jax.ShapeDtypeStruct((per, occupied, BLK), amp.dtype),
        in_specs=[SMEM_SPEC, SMEM_SPEC, VMEM_SPEC] + [ANY_SPEC] * len(after),
        out_specs=VMEM_SPEC,
        compiler_params=pltpu.CompilerParams(vmem_limit_bytes=8 * MIB),
        cost_estimate=pl.CostEstimate(
            flops=0, bytes_accessed=4 * per * occupied * BLK, transcendentals=0
        ),
        name="pick_tiles",
    )(me, rows, amp, *after)


def add_products(per, base, cols, live, piece, weights, total):
    unroll = min(UNROLL, per)

    def step(i, carry):
        slots = [i * unroll + u for u in range(unroll)]
        products = [
            jnp.dot(piece[s], weights[s], preferred_element_type=jnp.float32) for s in slots
        ]
        for s, product in zip(slots, products):
            total[cols[base + s]] += product * live[base + s]
        return carry

    lax.fori_loop(0, per // unroll, step, 0)


def ladder_kernel(peers_at, ahead, per, first, last, order, cols, live, w, *refs):
    count = len(peers_at)
    pieces, refs = refs[:count], refs[count:]
    if not first:
        start, refs = refs[0], refs[1:]
    if last:
        outs, held, total = refs, w, start
    else:
        *outs, held, sems = refs
        total = outs[0]
    copies = []
    for j, k in enumerate([] if last else peers_at + ahead):
        target = held.at[j] if j < count else outs[1].at[j - count]
        copies.append(pltpu.make_async_copy(w.at[order[k]], target, sems.at[j]))
        copies[-1].start()
    if first:
        total[...] = jnp.zeros_like(total)
    for j, k in enumerate(peers_at):
        if not last:
            copies[j].wait()
        add_products(per, order[k] * per, cols, live, pieces[j], held.at[j], total)
    for copy in copies[count:]:
        copy.wait()
    if last:
        at = 0
        for out in outs:
            out[...] = total[at : at + out.shape[0]]
            at += out.shape[0]


def ladder(order, cols, live, w, start, arrived, peers_at, ahead=(), last=None):
    pieces = [arrived[k] for k in peers_at]
    count = len(pieces)
    per, occupied, _ = pieces[0].shape
    first = start is None
    scratch = []
    if last:
        out_shape = [jax.ShapeDtypeStruct((n, occupied, BLK), jnp.float32) for n in last]
    else:
        out_shape = [pltpu.VMEM((ABT_X, occupied, BLK), jnp.float32)]
        if ahead:
            out_shape.append(pltpu.VMEM((len(ahead), per, BLK, BLK), w.dtype))
        scratch = [
            pltpu.VMEM((count, per, BLK, BLK), w.dtype),
            pltpu.SemaphoreType.DMA((count + len(ahead),)),
        ]
        w = pltpu.with_memory_space_constraint(w, pltpu.HBM)
    return pl.pallas_call(
        functools.partial(ladder_kernel, peers_at, list(ahead), per, first, bool(last)),
        out_shape=out_shape,
        in_specs=[SMEM_SPEC] * 3
        + [VMEM_SPEC if last else ANY_SPEC]
        + [VMEM_SPEC] * (count + (not first)),
        out_specs=[VMEM_SPEC] * len(out_shape),
        input_output_aliases={} if first or last else {4 + count: 0},
        scratch_shapes=scratch,
        compiler_params=pltpu.CompilerParams(vmem_limit_bytes=8 * MIB),
        cost_estimate=pl.CostEstimate(
            flops=2 * count * per * occupied * BLK * BLK,
            bytes_accessed=2 * (count + len(ahead)) * per * BLK * BLK,
            transcendentals=0,
        ),
        name="ladder_products",
    )(order, cols, live, w, *pieces, *([] if first else [start]))


def per_device(amplitudes, virt_irreps, w_tiles, tile_rows, tile_cols):
    occupied = amplitudes.shape[0]
    peers = lax.axis_size("gx")
    groups = lax.axis_size("gy")
    me = lax.axis_index("gx")
    mine = lax.axis_index("gy")
    row_count = amplitudes.shape[1] // BLK * peers
    per = tile_rows.shape[0] // peers
    near = peers // 2

    def swap(x, k):
        return lax.ppermute(x, "gx", [(i, i ^ k) for i in range(peers)])

    slots = tile_rows.shape[0]
    near_even, bit = tile_rows, 2
    while bit < near:
        near_even = jnp.concatenate([near_even, swap(near_even, bit)])
        bit *= 2
    far_even = swap(near_even, near)
    odd = swap(jnp.concatenate([near_even, far_even]), 1)

    amp = stage(amplitudes)
    here = me.reshape(1)
    quarter = near // 4
    far_order = list(range(near, peers, 2)) + list(range(near + 1, peers, 2))
    far = [far_order[j * quarter : (j + 1) * quarter] for j in range(4)]
    arrived = {0: pick(here, tile_rows, 0, amp, per)}
    for k in far[0] + far[1] + list(range(1, near)) + far[2] + far[3]:
        source, first = (odd, k // 2) if k % 2 else (near_even, k // 2)
        if k % 2 == 0 and k >= near:
            source, first = far_even, (k - near) // 2
        after = ()
        if k in far[2]:
            after = (arrived[far[1][far[2].index(k)]],)
        if k in far[3]:
            after = (arrived[far[1][far[3].index(k)]], arrived[1 + far[3].index(k)])
        arrived[k] = swap(pick(here, source, first * slots, amp, per, after), k)

    row_tile = mine * row_count + tile_rows
    col_tile = me * ABT_X + tile_cols
    live = (pair_irrep(row_tile, virt_irreps) == pair_irrep(col_tile, virt_irreps)).astype(
        jnp.float32
    )
    share = ABT_X // groups
    xs = groups // CORES
    owner = tile_cols // share
    other_core = (owner % CORES) ^ (mine % CORES)
    other_x = (owner // CORES) ^ (mine // CORES)
    cols = other_core * (ABT_X // CORES) + other_x * share + tile_cols % share
    order = jnp.arange(peers, dtype=jnp.int32) ^ me

    w = w_tiles.reshape(peers, per, BLK, BLK)
    args = (order, cols, live, w)
    (total,) = ladder(*args, None, arrived, far[0])
    (total,) = ladder(*args, total, arrived, far[1])
    total, held = ladder(*args, total, arrived, list(range(near)), ahead=far[3])
    (total,) = ladder(*args, total, arrived, far[2])
    sizes = (share, (xs - 1) * share) * CORES
    keep, keep_rest, give, give_rest = ladder(
        order, cols, live, held, total, arrived, far[3], last=sizes
    )

    def swap_gy(x, k):
        return lax.ppermute(x, "gy", [(i, i ^ k) for i in range(groups)])

    rest = (keep_rest + swap_gy(give_rest, 1)).reshape(xs - 1, share, occupied, BLK)
    result = keep + swap_gy(give, 1)
    for k in range(1, xs):
        result = result + swap_gy(rest[k - 1], k * CORES)
    return jnp.transpose(result, (1, 0, 2)).reshape(occupied, share * BLK)


def solution(mesh):
    in_specs = (
        P(None, ("gy", "gx")),
        P(),
        P(("gx", "gy"), None, None),
        P(("gx", "gy")),
        P(("gx", "gy")),
    )
    out_specs = P(None, ("gx", "gy"))
    return jax.shard_map(
        per_device, mesh=mesh, in_specs=in_specs, out_specs=out_specs, check_vma=False
    )
```

```python
import functools

import jax
import jax.numpy as jnp
from jax import lax
from jax.experimental import pallas as pl
from jax.experimental.pallas import tpu as pltpu
from jax.sharding import PartitionSpec as P

V = 1024
BLK = 128
ABT_X = 32
CORES = 2
UNROLL = 16
MIB = 1024 * 1024

VMEM_SPEC = pl.BlockSpec(memory_space=pltpu.VMEM)
SMEM_SPEC = pl.BlockSpec(memory_space=pltpu.SMEM)
ANY_SPEC = pl.BlockSpec(memory_space=pl.ANY)


def pair_irrep(tile, virt_irreps):
    first = tile * BLK // V // BLK
    second = tile * BLK % V // BLK
    return jnp.bitwise_xor(virt_irreps[first], virt_irreps[second])


def stage_kernel(source, held, sem):
    copy = pltpu.make_async_copy(source, held, sem)
    copy.start()
    copy.wait()


def stage(x):
    return pl.pallas_call(
        stage_kernel,
        out_shape=pltpu.VMEM(x.shape, x.dtype),
        in_specs=[ANY_SPEC],
        out_specs=VMEM_SPEC,
        scratch_shapes=[pltpu.SemaphoreType.DMA],
        compiler_params=pltpu.CompilerParams(vmem_limit_bytes=8 * MIB),
        cost_estimate=pl.CostEstimate(flops=0, bytes_accessed=2 * x.size, transcendentals=0),
        name="stage_amplitudes",
    )(pltpu.with_memory_space_constraint(x, pltpu.HBM))


def pick_kernel(first, per, local_tiles, me, rows, amp, *refs):
    out = refs[-1]
    base = first + me[0] * per
    origin = me[0] * local_tiles

    def step(i, carry):
        lane = pl.multiple_of((rows[base + i] - origin) * BLK, BLK)
        out[i] = amp[:, pl.ds(lane, BLK)]
        return carry

    lax.fori_loop(0, per, step, 0, unroll=8)


def pick(me, rows, first, amp, per, after=()):
    occupied, width = amp.shape
    return pl.pallas_call(
        functools.partial(pick_kernel, first, per, width // BLK),
        out_shape=jax.ShapeDtypeStruct((per, occupied, BLK), amp.dtype),
        in_specs=[SMEM_SPEC, SMEM_SPEC, VMEM_SPEC] + [ANY_SPEC] * len(after),
        out_specs=VMEM_SPEC,
        compiler_params=pltpu.CompilerParams(vmem_limit_bytes=8 * MIB),
        cost_estimate=pl.CostEstimate(
            flops=0, bytes_accessed=4 * per * occupied * BLK, transcendentals=0
        ),
        name="pick_tiles",
    )(me, rows, amp, *after)


def add_products(per, base, cols, live, piece, weights, total):
    unroll = min(UNROLL, per)

    def step(i, carry):
        slots = [i * unroll + u for u in range(unroll)]
        products = [
            jnp.dot(piece[s], weights[s], preferred_element_type=jnp.float32) for s in slots
        ]
        for s, product in zip(slots, products):
            total[cols[base + s]] += product * live[base + s]
        return carry

    lax.fori_loop(0, per // unroll, step, 0)


def ladder_kernel(peers_at, ahead, per, first, last, order, cols, live, w, *refs):
    count = len(peers_at)
    pieces, refs = refs[:count], refs[count:]
    if not first:
        start, refs = refs[0], refs[1:]
    if last:
        outs, held, total = refs, w, start
    else:
        *outs, held, sems = refs
        total = outs[0]
    copies = []
    for j, k in enumerate([] if last else peers_at + ahead):
        target = held.at[j] if j < count else outs[1].at[j - count]
        copies.append(pltpu.make_async_copy(w.at[order[k]], target, sems.at[j]))
        copies[-1].start()
    if first:
        total[...] = jnp.zeros_like(total)
    for j, k in enumerate(peers_at):
        if not last:
            copies[j].wait()
        add_products(per, order[k] * per, cols, live, pieces[j], held.at[j], total)
    for copy in copies[count:]:
        copy.wait()
    if last:
        at = 0
        for out in outs:
            out[...] = total[at : at + out.shape[0]]
            at += out.shape[0]


def ladder(order, cols, live, w, start, arrived, peers_at, ahead=(), last=None):
    pieces = [arrived[k] for k in peers_at]
    count = len(pieces)
    per, occupied, _ = pieces[0].shape
    first = start is None
    scratch = []
    if last:
        out_shape = [jax.ShapeDtypeStruct((n, occupied, BLK), jnp.float32) for n in last]
    else:
        out_shape = [pltpu.VMEM((ABT_X, occupied, BLK), jnp.float32)]
        if ahead:
            out_shape.append(pltpu.VMEM((len(ahead), per, BLK, BLK), w.dtype))
        scratch = [
            pltpu.VMEM((count, per, BLK, BLK), w.dtype),
            pltpu.SemaphoreType.DMA((count + len(ahead),)),
        ]
        w = pltpu.with_memory_space_constraint(w, pltpu.HBM)
    return pl.pallas_call(
        functools.partial(ladder_kernel, peers_at, list(ahead), per, first, bool(last)),
        out_shape=out_shape,
        in_specs=[SMEM_SPEC] * 3
        + [VMEM_SPEC if last else ANY_SPEC]
        + [VMEM_SPEC] * (count + (not first)),
        out_specs=[VMEM_SPEC] * len(out_shape),
        input_output_aliases={} if first or last else {4 + count: 0},
        scratch_shapes=scratch,
        compiler_params=pltpu.CompilerParams(vmem_limit_bytes=8 * MIB),
        cost_estimate=pl.CostEstimate(
            flops=2 * count * per * occupied * BLK * BLK,
            bytes_accessed=2 * (count + len(ahead)) * per * BLK * BLK,
            transcendentals=0,
        ),
        name="ladder_products",
    )(order, cols, live, w, *pieces, *([] if first else [start]))


def per_device(amplitudes, virt_irreps, w_tiles, tile_rows, tile_cols):
    occupied = amplitudes.shape[0]
    peers = lax.axis_size("gx")
    groups = lax.axis_size("gy")
    me = lax.axis_index("gx")
    mine = lax.axis_index("gy")
    row_count = amplitudes.shape[1] // BLK * peers
    per = tile_rows.shape[0] // peers
    near = peers // 2

    def swap(x, k):
        return lax.ppermute(x, "gx", [(i, i ^ k) for i in range(peers)])

    slots = tile_rows.shape[0]
    near_even, bit = tile_rows, 2
    while bit < near:
        near_even = jnp.concatenate([near_even, swap(near_even, bit)])
        bit *= 2
    far_even = swap(near_even, near)
    odd = swap(jnp.concatenate([near_even, far_even]), 1)

    amp = stage(amplitudes)
    here = me.reshape(1)
    quarter = near // 4
    far_order = list(range(near, peers, 2)) + list(range(near + 1, peers, 2))
    far = [far_order[j * quarter : (j + 1) * quarter] for j in range(4)]
    arrived = {0: pick(here, tile_rows, 0, amp, per)}
    for k in far[0] + far[1] + list(range(1, near)) + far[2] + far[3]:
        source, first = (odd, k // 2) if k % 2 else (near_even, k // 2)
        if k % 2 == 0 and k >= near:
            source, first = far_even, (k - near) // 2
        after = ()
        if k in far[2]:
            after = (arrived[far[1][far[2].index(k)]],)
        if k in far[3]:
            after = (arrived[far[1][far[3].index(k)]], arrived[2 + far[3].index(k)])
        arrived[k] = swap(pick(here, source, first * slots, amp, per, after), k)

    row_tile = mine * row_count + tile_rows
    col_tile = me * ABT_X + tile_cols
    live = (pair_irrep(row_tile, virt_irreps) == pair_irrep(col_tile, virt_irreps)).astype(
        jnp.float32
    )
    share = ABT_X // groups
    xs = groups // CORES
    owner = tile_cols // share
    other_core = (owner % CORES) ^ (mine % CORES)
    other_x = (owner // CORES) ^ (mine // CORES)
    cols = other_core * (ABT_X // CORES) + other_x * share + tile_cols % share
    order = jnp.arange(peers, dtype=jnp.int32) ^ me

    w = w_tiles.reshape(peers, per, BLK, BLK)
    args = (order, cols, live, w)
    (total,) = ladder(*args, None, arrived, far[0])
    (total,) = ladder(*args, total, arrived, far[1])
    total, held = ladder(*args, total, arrived, list(range(near)), ahead=far[3])
    (total,) = ladder(*args, total, arrived, far[2])
    sizes = (share, (xs - 1) * share) * CORES
    keep, keep_rest, give, give_rest = ladder(
        order, cols, live, held, total, arrived, far[3], last=sizes
    )

    def swap_gy(x, k):
        return lax.ppermute(x, "gy", [(i, i ^ k) for i in range(groups)])

    rest = (keep_rest + swap_gy(give_rest, 1)).reshape(xs - 1, share, occupied, BLK)
    result = keep + swap_gy(give, 1)
    for k in range(1, xs):
        result = result + swap_gy(rest[k - 1], k * CORES)
    return jnp.transpose(result, (1, 0, 2)).reshape(occupied, share * BLK)


def solution(mesh):
    in_specs = (
        P(None, ("gy", "gx")),
        P(),
        P(("gx", "gy"), None, None),
        P(("gx", "gy")),
        P(("gx", "gy")),
    )
    out_specs = P(None, ("gx", "gy"))
    return jax.shard_map(
        per_device, mesh=mesh, in_specs=in_specs, out_specs=out_specs, check_vma=False
    )
```

```python
import functools

import jax
import jax.numpy as jnp
from jax import lax
from jax.experimental import pallas as pl
from jax.experimental.pallas import tpu as pltpu
from jax.sharding import PartitionSpec as P

V = 1024
BLK = 128
ABT_X = 32
CORES = 2
UNROLL = 16
MIB = 1024 * 1024

VMEM_SPEC = pl.BlockSpec(memory_space=pltpu.VMEM)
SMEM_SPEC = pl.BlockSpec(memory_space=pltpu.SMEM)
ANY_SPEC = pl.BlockSpec(memory_space=pl.ANY)


def pair_irrep(tile, virt_irreps):
    first = tile * BLK // V // BLK
    second = tile * BLK % V // BLK
    return jnp.bitwise_xor(virt_irreps[first], virt_irreps[second])


def stage_kernel(source, held, sem):
    copy = pltpu.make_async_copy(source, held, sem)
    copy.start()
    copy.wait()


def stage(x):
    return pl.pallas_call(
        stage_kernel,
        out_shape=pltpu.VMEM(x.shape, x.dtype),
        in_specs=[ANY_SPEC],
        out_specs=VMEM_SPEC,
        scratch_shapes=[pltpu.SemaphoreType.DMA],
        compiler_params=pltpu.CompilerParams(vmem_limit_bytes=8 * MIB),
        cost_estimate=pl.CostEstimate(flops=0, bytes_accessed=2 * x.size, transcendentals=0),
        name="stage_amplitudes",
    )(pltpu.with_memory_space_constraint(x, pltpu.HBM))


def pick_kernel(first, per, local_tiles, me, rows, amp, *refs):
    out = refs[-1]
    base = first + me[0] * per
    origin = me[0] * local_tiles

    def step(i, carry):
        lane = pl.multiple_of((rows[base + i] - origin) * BLK, BLK)
        out[i] = amp[:, pl.ds(lane, BLK)]
        return carry

    lax.fori_loop(0, per, step, 0, unroll=8)


def pick(me, rows, first, amp, per, after=()):
    occupied, width = amp.shape
    return pl.pallas_call(
        functools.partial(pick_kernel, first, per, width // BLK),
        out_shape=jax.ShapeDtypeStruct((per, occupied, BLK), amp.dtype),
        in_specs=[SMEM_SPEC, SMEM_SPEC, VMEM_SPEC] + [ANY_SPEC] * len(after),
        out_specs=VMEM_SPEC,
        compiler_params=pltpu.CompilerParams(vmem_limit_bytes=8 * MIB),
        cost_estimate=pl.CostEstimate(
            flops=0, bytes_accessed=4 * per * occupied * BLK, transcendentals=0
        ),
        name="pick_tiles",
    )(me, rows, amp, *after)


def add_products(per, base, cols, live, piece, weights, total):
    unroll = min(UNROLL, per)

    def step(i, carry):
        slots = [i * unroll + u for u in range(unroll)]
        products = [
            jnp.dot(piece[s], weights[s], preferred_element_type=jnp.float32) for s in slots
        ]
        for s, product in zip(slots, products):
            total[cols[base + s]] += product * live[base + s]
        return carry

    lax.fori_loop(0, per // unroll, step, 0)


def ladder_kernel(peers_at, ahead, per, first, last, order, cols, live, w, *refs):
    count = len(peers_at)
    pieces, refs = refs[:count], refs[count:]
    if not first:
        start, refs = refs[0], refs[1:]
    if last:
        outs, held, total = refs, w, start
    else:
        *outs, held, sems = refs
        total = outs[0]
    copies = []
    for j, k in enumerate([] if last else peers_at + ahead):
        target = held.at[j] if j < count else outs[1].at[j - count]
        copies.append(pltpu.make_async_copy(w.at[order[k]], target, sems.at[j]))
        copies[-1].start()
    if first:
        total[...] = jnp.zeros_like(total)
    for j, k in enumerate(peers_at):
        if not last:
            copies[j].wait()
        add_products(per, order[k] * per, cols, live, pieces[j], held.at[j], total)
    for copy in copies[count:]:
        copy.wait()
    if last:
        at = 0
        for out in outs:
            out[...] = total[at : at + out.shape[0]]
            at += out.shape[0]


def ladder(order, cols, live, w, start, arrived, peers_at, ahead=(), last=None):
    pieces = [arrived[k] for k in peers_at]
    count = len(pieces)
    per, occupied, _ = pieces[0].shape
    first = start is None
    scratch = []
    if last:
        out_shape = [jax.ShapeDtypeStruct((n, occupied, BLK), jnp.float32) for n in last]
    else:
        out_shape = [pltpu.VMEM((ABT_X, occupied, BLK), jnp.float32)]
        if ahead:
            out_shape.append(pltpu.VMEM((len(ahead), per, BLK, BLK), w.dtype))
        scratch = [
            pltpu.VMEM((count, per, BLK, BLK), w.dtype),
            pltpu.SemaphoreType.DMA((count + len(ahead),)),
        ]
        w = pltpu.with_memory_space_constraint(w, pltpu.HBM)
    return pl.pallas_call(
        functools.partial(ladder_kernel, peers_at, list(ahead), per, first, bool(last)),
        out_shape=out_shape,
        in_specs=[SMEM_SPEC] * 3
        + [VMEM_SPEC if last else ANY_SPEC]
        + [VMEM_SPEC] * (count + (not first)),
        out_specs=[VMEM_SPEC] * len(out_shape),
        input_output_aliases={} if first or last else {4 + count: 0},
        scratch_shapes=scratch,
        compiler_params=pltpu.CompilerParams(vmem_limit_bytes=8 * MIB),
        cost_estimate=pl.CostEstimate(
            flops=2 * count * per * occupied * BLK * BLK,
            bytes_accessed=2 * (count + len(ahead)) * per * BLK * BLK,
            transcendentals=0,
        ),
        name="ladder_products",
    )(order, cols, live, w, *pieces, *([] if first else [start]))


def per_device(amplitudes, virt_irreps, w_tiles, tile_rows, tile_cols):
    occupied = amplitudes.shape[0]
    peers = lax.axis_size("gx")
    groups = lax.axis_size("gy")
    me = lax.axis_index("gx")
    mine = lax.axis_index("gy")
    row_count = amplitudes.shape[1] // BLK * peers
    per = tile_rows.shape[0] // peers
    near = peers // 2

    def swap(x, k):
        return lax.ppermute(x, "gx", [(i, i ^ k) for i in range(peers)])

    slots = tile_rows.shape[0]
    first_far = swap(tile_rows, near)
    place = {near: (first_far, 0)}
    known, rows, bit = [0, near], jnp.concatenate([tile_rows, first_far]), 2
    while bit < near:
        rows = jnp.concatenate([rows, swap(rows, bit)])
        known = known + [k ^ bit for k in known]
        bit *= 2
    odd = swap(rows, 1)
    for j, k in enumerate(known):
        place.setdefault(k, (rows, j * slots))
        place[k ^ 1] = (odd, j * slots)

    amp = stage(amplitudes)
    here = me.reshape(1)
    quarter = near // 4
    far_order = list(range(near, peers, 2)) + list(range(near + 1, peers, 2))
    far = [far_order[j * quarter : (j + 1) * quarter] for j in range(4)]
    arrived = {0: pick(here, tile_rows, 0, amp, per)}
    for k in far[0] + far[1] + list(range(1, near)) + far[2] + far[3]:
        after = ()
        if k in far[2]:
            after = (arrived[far[0][far[2].index(k)]],)
        if k in far[3]:
            after = (arrived[far[0][far[3].index(k)]], arrived[2 + far[3].index(k)])
        arrived[k] = swap(pick(here, *place[k], amp, per, after), k)

    row_tile = mine * row_count + tile_rows
    col_tile = me * ABT_X + tile_cols
    live = (pair_irrep(row_tile, virt_irreps) == pair_irrep(col_tile, virt_irreps)).astype(
        jnp.float32
    )
    share = ABT_X // groups
    xs = groups // CORES
    owner = tile_cols // share
    other_core = (owner % CORES) ^ (mine % CORES)
    other_x = (owner // CORES) ^ (mine // CORES)
    cols = other_core * (ABT_X // CORES) + other_x * share + tile_cols % share
    order = jnp.arange(peers, dtype=jnp.int32) ^ me

    w = w_tiles.reshape(peers, per, BLK, BLK)
    args = (order, cols, live, w)
    (total,) = ladder(*args, None, arrived, far[0])
    (total,) = ladder(*args, total, arrived, far[1])
    total, held = ladder(*args, total, arrived, list(range(near)), ahead=far[3])
    (total,) = ladder(*args, total, arrived, far[2])
    sizes = (share, (xs - 1) * share) * CORES
    keep, keep_rest, give, give_rest = ladder(
        order, cols, live, held, total, arrived, far[3], last=sizes
    )

    def swap_gy(x, k):
        return lax.ppermute(x, "gy", [(i, i ^ k) for i in range(groups)])

    rest = (keep_rest + swap_gy(give_rest, 1)).reshape(xs - 1, share, occupied, BLK)
    result = keep + swap_gy(give, 1)
    for k in range(1, xs):
        result = result + swap_gy(rest[k - 1], k * CORES)
    return jnp.transpose(result, (1, 0, 2)).reshape(occupied, share * BLK)


def solution(mesh):
    in_specs = (
        P(None, ("gy", "gx")),
        P(),
        P(("gx", "gy"), None, None),
        P(("gx", "gy")),
        P(("gx", "gy")),
    )
    out_specs = P(None, ("gx", "gy"))
    return jax.shard_map(
        per_device, mesh=mesh, in_specs=in_specs, out_specs=out_specs, check_vma=False
    )
```

```python
import functools

import jax
import jax.numpy as jnp
from jax import lax
from jax.experimental import pallas as pl
from jax.experimental.pallas import tpu as pltpu
from jax.sharding import PartitionSpec as P

V = 1024
BLK = 128
ABT_X = 32
CORES = 2
UNROLL = 32
CODE_TOP = 32000.0
MIB = 1024 * 1024

VMEM_SPEC = pl.BlockSpec(memory_space=pltpu.VMEM)
SMEM_SPEC = pl.BlockSpec(memory_space=pltpu.SMEM)
ANY_SPEC = pl.BlockSpec(memory_space=pl.ANY)


def pair_irrep(tile, virt_irreps):
    first = tile * BLK // V // BLK
    second = tile * BLK % V // BLK
    return jnp.bitwise_xor(virt_irreps[first], virt_irreps[second])


def stage_kernel(source, held, sem):
    copy = pltpu.make_async_copy(source, held, sem)
    copy.start()
    copy.wait()


def stage(x):
    return pl.pallas_call(
        stage_kernel,
        out_shape=pltpu.VMEM(x.shape, x.dtype),
        in_specs=[ANY_SPEC],
        out_specs=VMEM_SPEC,
        scratch_shapes=[pltpu.SemaphoreType.DMA],
        compiler_params=pltpu.CompilerParams(vmem_limit_bytes=8 * MIB),
        cost_estimate=pl.CostEstimate(flops=0, bytes_accessed=2 * x.size, transcendentals=0),
        name="stage_amplitudes",
    )(pltpu.with_memory_space_constraint(x, pltpu.HBM))


def pick_kernel(first, per, local_tiles, me, rows, amp, *refs):
    out = refs[-1]
    base = first + me[0] * per
    origin = me[0] * local_tiles

    def step(i, carry):
        lane = pl.multiple_of((rows[base + i] - origin) * BLK, BLK)
        out[i] = amp[:, pl.ds(lane, BLK)]
        return carry

    lax.fori_loop(0, per, step, 0, unroll=8)


def pick(me, rows, first, amp, per, after=()):
    occupied, width = amp.shape
    return pl.pallas_call(
        functools.partial(pick_kernel, first, per, width // BLK),
        out_shape=jax.ShapeDtypeStruct((per, occupied, BLK), amp.dtype),
        in_specs=[SMEM_SPEC, SMEM_SPEC, VMEM_SPEC] + [ANY_SPEC] * len(after),
        out_specs=VMEM_SPEC,
        compiler_params=pltpu.CompilerParams(vmem_limit_bytes=8 * MIB),
        cost_estimate=pl.CostEstimate(
            flops=0, bytes_accessed=4 * per * occupied * BLK, transcendentals=0
        ),
        name="pick_tiles",
    )(me, rows, amp, *after)


def add_products(per, base, cols, live, piece, weights, total):
    unroll = min(UNROLL, per)

    def step(i, carry):
        slots = [i * unroll + u for u in range(unroll)]
        products = [
            jnp.dot(piece[s], weights[s], preferred_element_type=jnp.float32) for s in slots
        ]
        for s, product in zip(slots, products):
            total[cols[base + s]] += product * live[base + s]
        return carry

    lax.fori_loop(0, per // unroll, step, 0)


def ladder_kernel(peers_at, ahead, per, first, last, order, cols, live, w, *refs):
    count = len(peers_at)
    pieces, refs = refs[:count], refs[count:]
    if not first:
        start, refs = refs[0], refs[1:]
    if last:
        outs, held, total = refs, w, start
    else:
        *outs, held, sems = refs
        total = outs[0]
    copies = []
    for j, k in enumerate([] if last else peers_at + ahead):
        target = held.at[j] if j < count else outs[1].at[j - count]
        copies.append(pltpu.make_async_copy(w.at[order[k]], target, sems.at[j]))
        copies[-1].start()
    if first:
        total[...] = jnp.zeros_like(total)
    for j, k in enumerate(peers_at):
        if not last:
            copies[j].wait()
        add_products(per, order[k] * per, cols, live, pieces[j], held.at[j], total)
    for copy in copies[count:]:
        copy.wait()
    if last:
        at = 0
        for out in outs:
            out[...] = total[at : at + out.shape[0]]
            at += out.shape[0]


def ladder(order, cols, live, w, start, arrived, peers_at, ahead=(), last=None):
    pieces = [arrived[k] for k in peers_at]
    count = len(pieces)
    per, occupied, _ = pieces[0].shape
    first = start is None
    scratch = []
    if last:
        out_shape = [jax.ShapeDtypeStruct((n, occupied, BLK), jnp.float32) for n in last]
    else:
        out_shape = [pltpu.VMEM((ABT_X, occupied, BLK), jnp.float32)]
        if ahead:
            out_shape.append(pltpu.VMEM((len(ahead), per, BLK, BLK), w.dtype))
        scratch = [
            pltpu.VMEM((count, per, BLK, BLK), w.dtype),
            pltpu.SemaphoreType.DMA((count + len(ahead),)),
        ]
        w = pltpu.with_memory_space_constraint(w, pltpu.HBM)
    return pl.pallas_call(
        functools.partial(ladder_kernel, peers_at, list(ahead), per, first, bool(last)),
        out_shape=out_shape,
        in_specs=[SMEM_SPEC] * 3
        + [VMEM_SPEC if last else ANY_SPEC]
        + [VMEM_SPEC] * (count + (not first)),
        out_specs=[VMEM_SPEC] * len(out_shape),
        input_output_aliases={} if first or last else {4 + count: 0},
        scratch_shapes=scratch,
        compiler_params=pltpu.CompilerParams(vmem_limit_bytes=8 * MIB),
        cost_estimate=pl.CostEstimate(
            flops=2 * count * per * occupied * BLK * BLK,
            bytes_accessed=2 * (count + len(ahead)) * per * BLK * BLK,
            transcendentals=0,
        ),
        name="ladder_products",
    )(order, cols, live, w, *pieces, *([] if first else [start]))


def encode_kernel(kept, got, *outs):
    share = outs[0].shape[0] - 1
    lane = lax.broadcasted_iota(jnp.int32, kept.shape[1:], 1)
    for b, out in enumerate(outs):
        powers = jnp.zeros(kept.shape[1:], jnp.int32)
        for j in range(share):
            value = kept[b * share + j] + got[b * share + j]
            top = jnp.max(jnp.abs(value), axis=1, keepdims=True)
            power = jnp.ceil(jnp.log2(jnp.maximum(top, 2.0**-100)))
            code = jnp.round(value * (jnp.exp2(-power) * CODE_TOP))
            out[j] = code.astype(jnp.int32).astype(jnp.int16)
            powers = jnp.where(lane == j, power.astype(jnp.int32), powers)
        out[share] = powers.astype(jnp.int16)


def encode(kept, got, parts):
    tiles, occupied, _ = kept.shape
    shape = jax.ShapeDtypeStruct((tiles // parts + 1, occupied, BLK), jnp.int16)
    return pl.pallas_call(
        encode_kernel,
        out_shape=[shape] * parts,
        in_specs=[VMEM_SPEC] * 2,
        out_specs=[VMEM_SPEC] * parts,
        compiler_params=pltpu.CompilerParams(vmem_limit_bytes=8 * MIB),
        cost_estimate=pl.CostEstimate(
            flops=8 * kept.size, bytes_accessed=10 * kept.size, transcendentals=0
        ),
        name="encode_sums",
    )(kept, got)


def decode_kernel(kept, got, *refs):
    arrived, out = refs[:-1], refs[-1]
    share = kept.shape[0]
    lane = lax.broadcasted_iota(jnp.int32, kept.shape[1:], 1)
    for j in range(share):
        value = kept[j] + got[j]
        for part in arrived:
            powers = jnp.where(lane == j, part[share].astype(jnp.int32), 0)
            power = jnp.sum(powers.astype(jnp.float32), axis=1, keepdims=True)
            code = part[j].astype(jnp.int32).astype(jnp.float32)
            value = value + code * (jnp.exp2(power) * (1.0 / CODE_TOP))
        out[:, j * BLK : (j + 1) * BLK] = value


def decode(kept, got, arrived):
    share, occupied, _ = kept.shape
    return pl.pallas_call(
        decode_kernel,
        out_shape=jax.ShapeDtypeStruct((occupied, share * BLK), jnp.float32),
        in_specs=[VMEM_SPEC] * (2 + len(arrived)),
        out_specs=VMEM_SPEC,
        compiler_params=pltpu.CompilerParams(vmem_limit_bytes=8 * MIB),
        cost_estimate=pl.CostEstimate(
            flops=8 * kept.size, bytes_accessed=14 * kept.size, transcendentals=0
        ),
        name="decode_sums",
    )(kept, got, *arrived)


def per_device(amplitudes, virt_irreps, w_tiles, tile_rows, tile_cols):
    occupied = amplitudes.shape[0]
    peers = lax.axis_size("gx")
    groups = lax.axis_size("gy")
    me = lax.axis_index("gx")
    mine = lax.axis_index("gy")
    row_count = amplitudes.shape[1] // BLK * peers
    per = tile_rows.shape[0] // peers
    near = peers // 2

    def swap(x, k):
        return lax.ppermute(x, "gx", [(i, i ^ k) for i in range(peers)])

    slots = tile_rows.shape[0]
    first_far = swap(tile_rows, near)
    place = {near: (first_far, 0)}
    known, rows, bit = [0, near], jnp.concatenate([tile_rows, first_far]), 2
    while bit < near:
        rows = jnp.concatenate([rows, swap(rows, bit)])
        known = known + [k ^ bit for k in known]
        bit *= 2
    odd = swap(rows, 1)
    for j, k in enumerate(known):
        place.setdefault(k, (rows, j * slots))
        place[k ^ 1] = (odd, j * slots)

    amp = stage(amplitudes)
    here = me.reshape(1)
    quarter = near // 4
    far_order = list(range(near, peers, 2)) + list(range(near + 1, peers, 2))
    far = [far_order[j * quarter : (j + 1) * quarter] for j in range(4)]
    arrived = {0: pick(here, tile_rows, 0, amp, per)}
    for k in far[0] + far[1] + list(range(1, near)) + far[2] + far[3]:
        after = ()
        if k in far[2]:
            after = (arrived[far[0][far[2].index(k)]],)
        if k in far[3]:
            after = (arrived[far[0][far[3].index(k)]], arrived[2 + far[3].index(k)])
        arrived[k] = swap(pick(here, *place[k], amp, per, after), k)

    row_tile = mine * row_count + tile_rows
    col_tile = me * ABT_X + tile_cols
    live = (pair_irrep(row_tile, virt_irreps) == pair_irrep(col_tile, virt_irreps)).astype(
        jnp.float32
    )
    share = ABT_X // groups
    xs = groups // CORES
    owner = tile_cols // share
    other_core = (owner % CORES) ^ (mine % CORES)
    other_x = (owner // CORES) ^ (mine // CORES)
    cols = other_core * (ABT_X // CORES) + other_x * share + tile_cols % share
    order = jnp.arange(peers, dtype=jnp.int32) ^ me

    w = w_tiles.reshape(peers, per, BLK, BLK)
    args = (order, cols, live, w)
    (total,) = ladder(*args, None, arrived, far[0])
    (total,) = ladder(*args, total, arrived, far[1])
    total, held = ladder(*args, total, arrived, list(range(near)), ahead=far[3])
    (total,) = ladder(*args, total, arrived, far[2])
    sizes = (share, (xs - 1) * share) * CORES
    keep, keep_rest, give, give_rest = ladder(
        order, cols, live, held, total, arrived, far[3], last=sizes
    )

    def swap_gy(x, k):
        return lax.ppermute(x, "gy", [(i, i ^ k) for i in range(groups)])

    coded = encode(keep_rest, swap_gy(give_rest, 1), xs - 1)
    got = swap_gy(give, 1)
    return decode(keep, got, [swap_gy(coded[k - 1], k * CORES) for k in range(1, xs)])


def solution(mesh):
    in_specs = (
        P(None, ("gy", "gx")),
        P(),
        P(("gx", "gy"), None, None),
        P(("gx", "gy")),
        P(("gx", "gy")),
    )
    out_specs = P(None, ("gx", "gy"))
    return jax.shard_map(
        per_device, mesh=mesh, in_specs=in_specs, out_specs=out_specs, check_vma=False
    )
```

```python
import functools

import jax
import jax.numpy as jnp
from jax import lax
from jax.experimental import pallas as pl
from jax.experimental.pallas import tpu as pltpu
from jax.sharding import PartitionSpec as P

V = 1024
BLK = 128
ABT_X = 32
CORES = 2
UNROLL = 32
CODE_TOP = 32000.0
STAGE_ROWS = 16
MIB = 1024 * 1024

VMEM_SPEC = pl.BlockSpec(memory_space=pltpu.VMEM)
SMEM_SPEC = pl.BlockSpec(memory_space=pltpu.SMEM)
ANY_SPEC = pl.BlockSpec(memory_space=pl.ANY)


def pair_irrep(tile, virt_irreps):
    first = tile * BLK // V // BLK
    second = tile * BLK % V // BLK
    return jnp.bitwise_xor(virt_irreps[first], virt_irreps[second])


def stage_kernel(rows, source, held, sems):
    copies = []
    for j in range(held.shape[0] // rows):
        part = pl.ds(j * rows, rows)
        copies.append(pltpu.make_async_copy(source.at[part], held.at[part], sems.at[j]))
        copies[-1].start()
    for copy in copies:
        copy.wait()


def stage(x):
    rows = STAGE_ROWS if x.shape[0] % STAGE_ROWS == 0 else x.shape[0]
    return pl.pallas_call(
        functools.partial(stage_kernel, rows),
        out_shape=pltpu.VMEM(x.shape, x.dtype),
        in_specs=[ANY_SPEC],
        out_specs=VMEM_SPEC,
        scratch_shapes=[pltpu.SemaphoreType.DMA((x.shape[0] // rows,))],
        compiler_params=pltpu.CompilerParams(vmem_limit_bytes=8 * MIB),
        cost_estimate=pl.CostEstimate(flops=0, bytes_accessed=2 * x.size, transcendentals=0),
        name="stage_amplitudes",
    )(pltpu.with_memory_space_constraint(x, pltpu.HBM))


def pick_kernel(first, per, local_tiles, me, rows, amp, *refs):
    out = refs[-1]
    base = first + me[0] * per
    origin = me[0] * local_tiles

    def step(i, carry):
        lane = pl.multiple_of((rows[base + i] - origin) * BLK, BLK)
        out[i] = amp[:, pl.ds(lane, BLK)]
        return carry

    lax.fori_loop(0, per, step, 0, unroll=8)


def pick(me, rows, first, amp, per, after=()):
    occupied, width = amp.shape
    return pl.pallas_call(
        functools.partial(pick_kernel, first, per, width // BLK),
        out_shape=jax.ShapeDtypeStruct((per, occupied, BLK), amp.dtype),
        in_specs=[SMEM_SPEC, SMEM_SPEC, VMEM_SPEC] + [ANY_SPEC] * len(after),
        out_specs=VMEM_SPEC,
        compiler_params=pltpu.CompilerParams(vmem_limit_bytes=8 * MIB),
        cost_estimate=pl.CostEstimate(
            flops=0, bytes_accessed=4 * per * occupied * BLK, transcendentals=0
        ),
        name="pick_tiles",
    )(me, rows, amp, *after)


def add_products(per, base, cols, live, piece, weights, total):
    unroll = min(UNROLL, per)

    def step(i, carry):
        slots = [i * unroll + u for u in range(unroll)]
        products = [
            jnp.dot(piece[s], weights[s], preferred_element_type=jnp.float32) for s in slots
        ]
        for s, product in zip(slots, products):
            total[cols[base + s]] += product * live[base + s]
        return carry

    lax.fori_loop(0, per // unroll, step, 0)


def ladder_kernel(peers_at, ahead, per, first, last, order, cols, live, w, *refs):
    count = len(peers_at)
    pieces, refs = refs[:count], refs[count:]
    if not first:
        start, refs = refs[0], refs[1:]
    if last:
        outs, held, total = refs, w, start
    else:
        *outs, held, sems = refs
        total = outs[0]
    copies = []
    for j, k in enumerate([] if last else peers_at + ahead):
        target = held.at[j] if j < count else outs[1].at[j - count]
        copies.append(pltpu.make_async_copy(w.at[order[k]], target, sems.at[j]))
        copies[-1].start()
    if first:
        total[...] = jnp.zeros_like(total)
    for j, k in enumerate(peers_at):
        if not last:
            copies[j].wait()
        add_products(per, order[k] * per, cols, live, pieces[j], held.at[j], total)
    for copy in copies[count:]:
        copy.wait()
    if last:
        at = 0
        for out in outs:
            out[...] = total[at : at + out.shape[0]]
            at += out.shape[0]


def ladder(order, cols, live, w, start, arrived, peers_at, ahead=(), last=None):
    pieces = [arrived[k] for k in peers_at]
    count = len(pieces)
    per, occupied, _ = pieces[0].shape
    first = start is None
    scratch = []
    if last:
        out_shape = [jax.ShapeDtypeStruct((n, occupied, BLK), jnp.float32) for n in last]
    else:
        out_shape = [pltpu.VMEM((ABT_X, occupied, BLK), jnp.float32)]
        if ahead:
            out_shape.append(pltpu.VMEM((len(ahead), per, BLK, BLK), w.dtype))
        scratch = [
            pltpu.VMEM((count, per, BLK, BLK), w.dtype),
            pltpu.SemaphoreType.DMA((count + len(ahead),)),
        ]
        w = pltpu.with_memory_space_constraint(w, pltpu.HBM)
    return pl.pallas_call(
        functools.partial(ladder_kernel, peers_at, list(ahead), per, first, bool(last)),
        out_shape=out_shape,
        in_specs=[SMEM_SPEC] * 3
        + [VMEM_SPEC if last else ANY_SPEC]
        + [VMEM_SPEC] * (count + (not first)),
        out_specs=[VMEM_SPEC] * len(out_shape),
        input_output_aliases={} if first or last else {4 + count: 0},
        scratch_shapes=scratch,
        compiler_params=pltpu.CompilerParams(vmem_limit_bytes=8 * MIB),
        cost_estimate=pl.CostEstimate(
            flops=2 * count * per * occupied * BLK * BLK,
            bytes_accessed=2 * (count + len(ahead)) * per * BLK * BLK,
            transcendentals=0,
        ),
        name="ladder_products",
    )(order, cols, live, w, *pieces, *([] if first else [start]))


def encode_kernel(kept, got, *outs):
    share = outs[0].shape[0] - 1
    lane = lax.broadcasted_iota(jnp.int32, kept.shape[1:], 1)
    for b, out in enumerate(outs):
        powers = jnp.zeros(kept.shape[1:], jnp.int32)
        for j in range(share):
            value = kept[b * share + j] + got[b * share + j]
            top = jnp.max(jnp.abs(value), axis=1, keepdims=True)
            power = jnp.ceil(jnp.log2(jnp.maximum(top, 2.0**-100)))
            code = jnp.round(value * (jnp.exp2(-power) * CODE_TOP))
            out[j] = code.astype(jnp.int32).astype(jnp.int16)
            powers = jnp.where(lane == j, power.astype(jnp.int32), powers)
        out[share] = powers.astype(jnp.int16)


def encode(kept, got, parts):
    tiles, occupied, _ = kept.shape
    shape = jax.ShapeDtypeStruct((tiles // parts + 1, occupied, BLK), jnp.int16)
    return pl.pallas_call(
        encode_kernel,
        out_shape=[shape] * parts,
        in_specs=[VMEM_SPEC] * 2,
        out_specs=[VMEM_SPEC] * parts,
        compiler_params=pltpu.CompilerParams(vmem_limit_bytes=8 * MIB),
        cost_estimate=pl.CostEstimate(
            flops=8 * kept.size, bytes_accessed=10 * kept.size, transcendentals=0
        ),
        name="encode_sums",
    )(kept, got)


def decode_kernel(kept, got, *refs):
    arrived, out = refs[:-1], refs[-1]
    share = kept.shape[0]
    lane = lax.broadcasted_iota(jnp.int32, kept.shape[1:], 1)
    for j in range(share):
        value = kept[j] + got[j]
        for part in arrived:
            powers = jnp.where(lane == j, part[share].astype(jnp.int32), 0)
            power = jnp.sum(powers.astype(jnp.float32), axis=1, keepdims=True)
            code = part[j].astype(jnp.int32).astype(jnp.float32)
            value = value + code * (jnp.exp2(power) * (1.0 / CODE_TOP))
        out[:, j * BLK : (j + 1) * BLK] = value


def decode(kept, got, arrived):
    share, occupied, _ = kept.shape
    return pl.pallas_call(
        decode_kernel,
        out_shape=jax.ShapeDtypeStruct((occupied, share * BLK), jnp.float32),
        in_specs=[VMEM_SPEC] * (2 + len(arrived)),
        out_specs=VMEM_SPEC,
        compiler_params=pltpu.CompilerParams(vmem_limit_bytes=8 * MIB),
        cost_estimate=pl.CostEstimate(
            flops=8 * kept.size, bytes_accessed=14 * kept.size, transcendentals=0
        ),
        name="decode_sums",
    )(kept, got, *arrived)


def per_device(amplitudes, virt_irreps, w_tiles, tile_rows, tile_cols):
    occupied = amplitudes.shape[0]
    peers = lax.axis_size("gx")
    groups = lax.axis_size("gy")
    me = lax.axis_index("gx")
    mine = lax.axis_index("gy")
    row_count = amplitudes.shape[1] // BLK * peers
    per = tile_rows.shape[0] // peers
    near = peers // 2

    def swap(x, k):
        return lax.ppermute(x, "gx", [(i, i ^ k) for i in range(peers)])

    slots = tile_rows.shape[0]
    first_far = swap(tile_rows, near)
    place = {near: (first_far, 0)}
    known, rows, bit = [0, near], jnp.concatenate([tile_rows, first_far]), 2
    while bit < near:
        rows = jnp.concatenate([rows, swap(rows, bit)])
        known = known + [k ^ bit for k in known]
        bit *= 2
    odd = swap(rows, 1)
    for j, k in enumerate(known):
        place.setdefault(k, (rows, j * slots))
        place[k ^ 1] = (odd, j * slots)

    amp = stage(amplitudes)
    here = me.reshape(1)
    quarter = near // 4
    far_order = list(range(near, peers, 2)) + list(range(near + 1, peers, 2))
    far = [far_order[j * quarter : (j + 1) * quarter] for j in range(4)]
    arrived = {0: pick(here, tile_rows, 0, amp, per)}
    for k in far[0] + far[1] + list(range(1, near)) + far[2] + far[3]:
        after = ()
        if k in far[2]:
            after = (arrived[far[0][far[2].index(k)]],)
        if k in far[3]:
            after = (arrived[far[0][far[3].index(k)]], arrived[2 + far[3].index(k)])
        arrived[k] = swap(pick(here, *place[k], amp, per, after), k)

    row_tile = mine * row_count + tile_rows
    col_tile = me * ABT_X + tile_cols
    live = (pair_irrep(row_tile, virt_irreps) == pair_irrep(col_tile, virt_irreps)).astype(
        jnp.float32
    )
    share = ABT_X // groups
    xs = groups // CORES
    owner = tile_cols // share
    other_core = (owner % CORES) ^ (mine % CORES)
    other_x = (owner // CORES) ^ (mine // CORES)
    cols = other_core * (ABT_X // CORES) + other_x * share + tile_cols % share
    order = jnp.arange(peers, dtype=jnp.int32) ^ me

    w = w_tiles.reshape(peers, per, BLK, BLK)
    args = (order, cols, live, w)
    (total,) = ladder(*args, None, arrived, far[0])
    (total,) = ladder(*args, total, arrived, far[1])
    total, held = ladder(*args, total, arrived, list(range(near)), ahead=far[3])
    (total,) = ladder(*args, total, arrived, far[2])
    sizes = (share, (xs - 1) * share) * CORES
    keep, keep_rest, give, give_rest = ladder(
        order, cols, live, held, total, arrived, far[3], last=sizes
    )

    def swap_gy(x, k):
        return lax.ppermute(x, "gy", [(i, i ^ k) for i in range(groups)])

    coded = encode(keep_rest, swap_gy(give_rest, 1), xs - 1)
    got = swap_gy(give, 1)
    return decode(keep, got, [swap_gy(coded[k - 1], k * CORES) for k in range(1, xs)])


def solution(mesh):
    in_specs = (
        P(None, ("gy", "gx")),
        P(),
        P(("gx", "gy"), None, None),
        P(("gx", "gy")),
        P(("gx", "gy")),
    )
    out_specs = P(None, ("gx", "gy"))
    return jax.shard_map(
        per_device, mesh=mesh, in_specs=in_specs, out_specs=out_specs, check_vma=False
    )
```

```python
import functools

import jax
import jax.numpy as jnp
from jax import lax
from jax.experimental import pallas as pl
from jax.experimental.pallas import tpu as pltpu
from jax.sharding import PartitionSpec as P

V = 1024
BLK = 128
ABT_X = 32
CORES = 2
UNROLL = 32
CODE_TOP = 32000.0
MIB = 1024 * 1024

VMEM_SPEC = pl.BlockSpec(memory_space=pltpu.VMEM)
SMEM_SPEC = pl.BlockSpec(memory_space=pltpu.SMEM)
ANY_SPEC = pl.BlockSpec(memory_space=pl.ANY)


def pair_irrep(tile, virt_irreps):
    first = tile * BLK // V // BLK
    second = tile * BLK % V // BLK
    return jnp.bitwise_xor(virt_irreps[first], virt_irreps[second])


def stage_kernel(source, *refs):
    held, sem = refs[-2:]
    copy = pltpu.make_async_copy(source, held, sem)
    copy.start()
    copy.wait()


def stage(x, after):
    return pl.pallas_call(
        stage_kernel,
        out_shape=pltpu.VMEM(x.shape, x.dtype),
        in_specs=[ANY_SPEC] * (1 + len(after)),
        out_specs=VMEM_SPEC,
        scratch_shapes=[pltpu.SemaphoreType.DMA],
        compiler_params=pltpu.CompilerParams(vmem_limit_bytes=8 * MIB),
        cost_estimate=pl.CostEstimate(flops=0, bytes_accessed=2 * x.size, transcendentals=0),
        name="stage_amplitudes",
    )(pltpu.with_memory_space_constraint(x, pltpu.HBM), *after)


def fetch_kernel(first, per, local_tiles, me, rows, amp, out, sem):
    base = first + me[0] * per
    origin = me[0] * local_tiles

    def start(i, carry):
        lane = pl.multiple_of((rows[base + i] - origin) * BLK, BLK)
        pltpu.make_async_copy(amp.at[:, pl.ds(lane, BLK)], out.at[i], sem).start()
        return carry

    lax.fori_loop(0, per, start, 0, unroll=8)
    pltpu.make_async_copy(out, out, sem).wait()


def fetch(me, rows, first, amp, per):
    occupied, width = amp.shape
    return pl.pallas_call(
        functools.partial(fetch_kernel, first, per, width // BLK),
        out_shape=pltpu.VMEM((per, occupied, BLK), amp.dtype),
        in_specs=[SMEM_SPEC, SMEM_SPEC, ANY_SPEC],
        out_specs=VMEM_SPEC,
        scratch_shapes=[pltpu.SemaphoreType.DMA],
        compiler_params=pltpu.CompilerParams(vmem_limit_bytes=8 * MIB),
        cost_estimate=pl.CostEstimate(
            flops=0, bytes_accessed=4 * per * occupied * BLK, transcendentals=0
        ),
        name="fetch_tiles",
    )(me, rows, pltpu.with_memory_space_constraint(amp, pltpu.HBM))


def pick_kernel(first, per, local_tiles, me, rows, amp, *refs):
    out = refs[-1]
    base = first + me[0] * per
    origin = me[0] * local_tiles

    def step(i, carry):
        lane = pl.multiple_of((rows[base + i] - origin) * BLK, BLK)
        out[i] = amp[:, pl.ds(lane, BLK)]
        return carry

    lax.fori_loop(0, per, step, 0, unroll=8)


def pick(me, rows, first, amp, per, after=()):
    occupied, width = amp.shape
    return pl.pallas_call(
        functools.partial(pick_kernel, first, per, width // BLK),
        out_shape=jax.ShapeDtypeStruct((per, occupied, BLK), amp.dtype),
        in_specs=[SMEM_SPEC, SMEM_SPEC, VMEM_SPEC] + [ANY_SPEC] * len(after),
        out_specs=VMEM_SPEC,
        compiler_params=pltpu.CompilerParams(vmem_limit_bytes=8 * MIB),
        cost_estimate=pl.CostEstimate(
            flops=0, bytes_accessed=4 * per * occupied * BLK, transcendentals=0
        ),
        name="pick_tiles",
    )(me, rows, amp, *after)


def add_products(per, base, cols, live, piece, weights, total):
    unroll = min(UNROLL, per)

    def step(i, carry):
        slots = [i * unroll + u for u in range(unroll)]
        products = [
            jnp.dot(piece[s], weights[s], preferred_element_type=jnp.float32) for s in slots
        ]
        for s, product in zip(slots, products):
            total[cols[base + s]] += product * live[base + s]
        return carry

    lax.fori_loop(0, per // unroll, step, 0)


def ladder_kernel(peers_at, ahead, per, first, last, order, cols, live, w, *refs):
    count = len(peers_at)
    pieces, refs = refs[:count], refs[count:]
    if not first:
        start, refs = refs[0], refs[1:]
    if last:
        outs, held, total = refs, w, start
    else:
        *outs, held, sems = refs
        total = outs[0]
    copies = []
    for j, k in enumerate([] if last else peers_at + ahead):
        target = held.at[j] if j < count else outs[1].at[j - count]
        copies.append(pltpu.make_async_copy(w.at[order[k]], target, sems.at[j]))
        copies[-1].start()
    if first:
        total[...] = jnp.zeros_like(total)
    for j, k in enumerate(peers_at):
        if not last:
            copies[j].wait()
        add_products(per, order[k] * per, cols, live, pieces[j], held.at[j], total)
    for copy in copies[count:]:
        copy.wait()
    if last:
        at = 0
        for out in outs:
            out[...] = total[at : at + out.shape[0]]
            at += out.shape[0]


def ladder(order, cols, live, w, start, arrived, peers_at, ahead=(), last=None):
    pieces = [arrived[k] for k in peers_at]
    count = len(pieces)
    per, occupied, _ = pieces[0].shape
    first = start is None
    scratch = []
    if last:
        out_shape = [jax.ShapeDtypeStruct((n, occupied, BLK), jnp.float32) for n in last]
    else:
        out_shape = [pltpu.VMEM((ABT_X, occupied, BLK), jnp.float32)]
        if ahead:
            out_shape.append(pltpu.VMEM((len(ahead), per, BLK, BLK), w.dtype))
        scratch = [
            pltpu.VMEM((count, per, BLK, BLK), w.dtype),
            pltpu.SemaphoreType.DMA((count + len(ahead),)),
        ]
        w = pltpu.with_memory_space_constraint(w, pltpu.HBM)
    return pl.pallas_call(
        functools.partial(ladder_kernel, peers_at, list(ahead), per, first, bool(last)),
        out_shape=out_shape,
        in_specs=[SMEM_SPEC] * 3
        + [VMEM_SPEC if last else ANY_SPEC]
        + [VMEM_SPEC] * (count + (not first)),
        out_specs=[VMEM_SPEC] * len(out_shape),
        input_output_aliases={} if first or last else {4 + count: 0},
        scratch_shapes=scratch,
        compiler_params=pltpu.CompilerParams(vmem_limit_bytes=8 * MIB),
        cost_estimate=pl.CostEstimate(
            flops=2 * count * per * occupied * BLK * BLK,
            bytes_accessed=2 * (count + len(ahead)) * per * BLK * BLK,
            transcendentals=0,
        ),
        name="ladder_products",
    )(order, cols, live, w, *pieces, *([] if first else [start]))


def encode_kernel(kept, got, *outs):
    share = outs[0].shape[0] - 1
    lane = lax.broadcasted_iota(jnp.int32, kept.shape[1:], 1)
    for b, out in enumerate(outs):
        powers = jnp.zeros(kept.shape[1:], jnp.int32)
        for j in range(share):
            value = kept[b * share + j] + got[b * share + j]
            top = jnp.max(jnp.abs(value), axis=1, keepdims=True)
            power = jnp.ceil(jnp.log2(jnp.maximum(top, 2.0**-100)))
            code = jnp.round(value * (jnp.exp2(-power) * CODE_TOP))
            out[j] = code.astype(jnp.int32).astype(jnp.int16)
            powers = jnp.where(lane == j, power.astype(jnp.int32), powers)
        out[share] = powers.astype(jnp.int16)


def encode(kept, got, parts):
    tiles, occupied, _ = kept.shape
    shape = jax.ShapeDtypeStruct((tiles // parts + 1, occupied, BLK), jnp.int16)
    return pl.pallas_call(
        encode_kernel,
        out_shape=[shape] * parts,
        in_specs=[VMEM_SPEC] * 2,
        out_specs=[VMEM_SPEC] * parts,
        compiler_params=pltpu.CompilerParams(vmem_limit_bytes=8 * MIB),
        cost_estimate=pl.CostEstimate(
            flops=8 * kept.size, bytes_accessed=10 * kept.size, transcendentals=0
        ),
        name="encode_sums",
    )(kept, got)


def decode_kernel(kept, got, *refs):
    arrived, out = refs[:-1], refs[-1]
    share = kept.shape[0]
    lane = lax.broadcasted_iota(jnp.int32, kept.shape[1:], 1)
    for j in range(share):
        value = kept[j] + got[j]
        for part in arrived:
            powers = jnp.where(lane == j, part[share].astype(jnp.int32), 0)
            power = jnp.sum(powers.astype(jnp.float32), axis=1, keepdims=True)
            code = part[j].astype(jnp.int32).astype(jnp.float32)
            value = value + code * (jnp.exp2(power) * (1.0 / CODE_TOP))
        out[:, j * BLK : (j + 1) * BLK] = value


def decode(kept, got, arrived):
    share, occupied, _ = kept.shape
    return pl.pallas_call(
        decode_kernel,
        out_shape=jax.ShapeDtypeStruct((occupied, share * BLK), jnp.float32),
        in_specs=[VMEM_SPEC] * (2 + len(arrived)),
        out_specs=VMEM_SPEC,
        compiler_params=pltpu.CompilerParams(vmem_limit_bytes=8 * MIB),
        cost_estimate=pl.CostEstimate(
            flops=8 * kept.size, bytes_accessed=14 * kept.size, transcendentals=0
        ),
        name="decode_sums",
    )(kept, got, *arrived)


def per_device(amplitudes, virt_irreps, w_tiles, tile_rows, tile_cols):
    occupied = amplitudes.shape[0]
    peers = lax.axis_size("gx")
    groups = lax.axis_size("gy")
    me = lax.axis_index("gx")
    mine = lax.axis_index("gy")
    row_count = amplitudes.shape[1] // BLK * peers
    per = tile_rows.shape[0] // peers
    near = peers // 2

    def swap(x, k):
        return lax.ppermute(x, "gx", [(i, i ^ k) for i in range(peers)])

    slots = tile_rows.shape[0]
    first_far = swap(tile_rows, near)
    place = {near: (first_far, 0)}
    known, rows, bit = [0, near], jnp.concatenate([tile_rows, first_far]), 2
    while bit < near:
        rows = jnp.concatenate([rows, swap(rows, bit)])
        known = known + [k ^ bit for k in known]
        bit *= 2
    odd = swap(rows, 1)
    for j, k in enumerate(known):
        place.setdefault(k, (rows, j * slots))
        place[k ^ 1] = (odd, j * slots)

    here = me.reshape(1)
    fetched = fetch(here, *place[near], amplitudes, per)
    amp = stage(amplitudes, (fetched,))
    quarter = near // 4
    far_order = list(range(near, peers, 2)) + list(range(near + 1, peers, 2))
    far = [far_order[j * quarter : (j + 1) * quarter] for j in range(4)]
    arrived = {0: pick(here, tile_rows, 0, amp, per), near: swap(fetched, near)}
    for k in far[0][1:] + far[1] + list(range(1, near)) + far[2] + far[3]:
        after = ()
        if k in far[2]:
            after = (arrived[far[0][far[2].index(k)]],)
        if k in far[3]:
            after = (arrived[far[0][far[3].index(k)]], arrived[2 + far[3].index(k)])
        arrived[k] = swap(pick(here, *place[k], amp, per, after), k)

    row_tile = mine * row_count + tile_rows
    col_tile = me * ABT_X + tile_cols
    live = (pair_irrep(row_tile, virt_irreps) == pair_irrep(col_tile, virt_irreps)).astype(
        jnp.float32
    )
    share = ABT_X // groups
    xs = groups // CORES
    owner = tile_cols // share
    other_core = (owner % CORES) ^ (mine % CORES)
    other_x = (owner // CORES) ^ (mine // CORES)
    cols = other_core * (ABT_X // CORES) + other_x * share + tile_cols % share
    order = jnp.arange(peers, dtype=jnp.int32) ^ me

    w = w_tiles.reshape(peers, per, BLK, BLK)
    args = (order, cols, live, w)
    (total,) = ladder(*args, None, arrived, far[0])
    (total,) = ladder(*args, total, arrived, far[1])
    total, held = ladder(*args, total, arrived, list(range(near)), ahead=far[3])
    (total,) = ladder(*args, total, arrived, far[2])
    sizes = (share, (xs - 1) * share) * CORES
    keep, keep_rest, give, give_rest = ladder(
        order, cols, live, held, total, arrived, far[3], last=sizes
    )

    def swap_gy(x, k):
        return lax.ppermute(x, "gy", [(i, i ^ k) for i in range(groups)])

    coded = encode(keep_rest, swap_gy(give_rest, 1), xs - 1)
    got = swap_gy(give, 1)
    return decode(keep, got, [swap_gy(coded[k - 1], k * CORES) for k in range(1, xs)])


def solution(mesh):
    in_specs = (
        P(None, ("gy", "gx")),
        P(),
        P(("gx", "gy"), None, None),
        P(("gx", "gy")),
        P(("gx", "gy")),
    )
    out_specs = P(None, ("gx", "gy"))
    return jax.shard_map(
        per_device, mesh=mesh, in_specs=in_specs, out_specs=out_specs, check_vma=False
    )
```

```python
import functools

import jax
import jax.numpy as jnp
from jax import lax
from jax.experimental import pallas as pl
from jax.experimental.pallas import tpu as pltpu
from jax.sharding import PartitionSpec as P

V = 1024
BLK = 128
ABT_X = 32
CORES = 2
UNROLL = 32
CODE_TOP = 32000.0
MIB = 1024 * 1024

VMEM_SPEC = pl.BlockSpec(memory_space=pltpu.VMEM)
SMEM_SPEC = pl.BlockSpec(memory_space=pltpu.SMEM)
ANY_SPEC = pl.BlockSpec(memory_space=pl.ANY)


def pair_irrep(tile, virt_irreps):
    first = tile * BLK // V // BLK
    second = tile * BLK % V // BLK
    return jnp.bitwise_xor(virt_irreps[first], virt_irreps[second])


def stage_kernel(source, held, sem):
    copy = pltpu.make_async_copy(source, held, sem)
    copy.start()
    copy.wait()


def stage(x):
    return pl.pallas_call(
        stage_kernel,
        out_shape=pltpu.VMEM(x.shape, x.dtype),
        in_specs=[ANY_SPEC],
        out_specs=VMEM_SPEC,
        scratch_shapes=[pltpu.SemaphoreType.DMA],
        compiler_params=pltpu.CompilerParams(vmem_limit_bytes=8 * MIB),
        cost_estimate=pl.CostEstimate(flops=0, bytes_accessed=2 * x.size, transcendentals=0),
        name="stage_amplitudes",
    )(pltpu.with_memory_space_constraint(x, pltpu.HBM))


def pick_kernel(first, per, local_tiles, me, rows, amp, *refs):
    out = refs[-1]
    base = first + me[0] * per
    origin = me[0] * local_tiles

    def step(i, carry):
        lane = pl.multiple_of((rows[base + i] - origin) * BLK, BLK)
        out[i] = amp[:, pl.ds(lane, BLK)]
        return carry

    lax.fori_loop(0, per, step, 0, unroll=8)


def pick(me, rows, first, amp, per, after=()):
    occupied, width = amp.shape
    return pl.pallas_call(
        functools.partial(pick_kernel, first, per, width // BLK),
        out_shape=jax.ShapeDtypeStruct((per, occupied, BLK), amp.dtype),
        in_specs=[SMEM_SPEC, SMEM_SPEC, VMEM_SPEC] + [ANY_SPEC] * len(after),
        out_specs=VMEM_SPEC,
        compiler_params=pltpu.CompilerParams(vmem_limit_bytes=8 * MIB),
        cost_estimate=pl.CostEstimate(
            flops=0, bytes_accessed=4 * per * occupied * BLK, transcendentals=0
        ),
        name="pick_tiles",
    )(me, rows, amp, *after)


def add_products(per, base, cols, live, piece, weights, total):
    unroll = min(UNROLL, per)

    def step(i, carry):
        slots = [i * unroll + u for u in range(unroll)]
        products = [
            jnp.dot(piece[s], weights[s], preferred_element_type=jnp.float32) for s in slots
        ]
        for s, product in zip(slots, products):
            total[cols[base + s]] += product * live[base + s]
        return carry

    lax.fori_loop(0, per // unroll, step, 0)


def ladder_kernel(peers_at, ahead, per, first, last, order, cols, live, w, *refs):
    count = len(peers_at)
    pieces, refs = refs[:count], refs[count:]
    if not first:
        start, refs = refs[0], refs[1:]
    if last:
        outs, held, total = refs, w, start
    else:
        *outs, held, sems = refs
        total = outs[0]
    copies = []
    for j, k in enumerate([] if last else peers_at + ahead):
        target = held.at[j] if j < count else outs[1].at[j - count]
        copies.append(pltpu.make_async_copy(w.at[order[k]], target, sems.at[j]))
        copies[-1].start()
    if first:
        total[...] = jnp.zeros_like(total)
    for j, k in enumerate(peers_at):
        if not last:
            copies[j].wait()
        add_products(per, order[k] * per, cols, live, pieces[j], held.at[j], total)
    for copy in copies[count:]:
        copy.wait()
    if last:
        at = 0
        for out in outs:
            out[...] = total[at : at + out.shape[0]]
            at += out.shape[0]


def ladder(order, cols, live, w, start, arrived, peers_at, ahead=(), last=None):
    pieces = [arrived[k] for k in peers_at]
    count = len(pieces)
    per, occupied, _ = pieces[0].shape
    first = start is None
    scratch = []
    if last:
        out_shape = [jax.ShapeDtypeStruct((n, occupied, BLK), jnp.float32) for n in last]
    else:
        out_shape = [pltpu.VMEM((ABT_X, occupied, BLK), jnp.float32)]
        if ahead:
            out_shape.append(pltpu.VMEM((len(ahead), per, BLK, BLK), w.dtype))
        scratch = [
            pltpu.VMEM((count, per, BLK, BLK), w.dtype),
            pltpu.SemaphoreType.DMA((count + len(ahead),)),
        ]
        w = pltpu.with_memory_space_constraint(w, pltpu.HBM)
    return pl.pallas_call(
        functools.partial(ladder_kernel, peers_at, list(ahead), per, first, bool(last)),
        out_shape=out_shape,
        in_specs=[SMEM_SPEC] * 3
        + [VMEM_SPEC if last else ANY_SPEC]
        + [VMEM_SPEC] * (count + (not first)),
        out_specs=[VMEM_SPEC] * len(out_shape),
        input_output_aliases={} if first or last else {4 + count: 0},
        scratch_shapes=scratch,
        compiler_params=pltpu.CompilerParams(vmem_limit_bytes=8 * MIB),
        cost_estimate=pl.CostEstimate(
            flops=2 * count * per * occupied * BLK * BLK,
            bytes_accessed=2 * (count + len(ahead)) * per * BLK * BLK,
            transcendentals=0,
        ),
        name="ladder_products",
    )(order, cols, live, w, *pieces, *([] if first else [start]))


def encode_kernel(kept, got, *outs):
    share = outs[0].shape[0] - 1
    lane = lax.broadcasted_iota(jnp.int32, kept.shape[1:], 1)
    for b, out in enumerate(outs):
        powers = jnp.zeros(kept.shape[1:], jnp.int32)
        for j in range(share):
            value = kept[b * share + j] + got[b * share + j]
            top = jnp.max(jnp.abs(value), axis=1, keepdims=True)
            power = jnp.ceil(jnp.log2(jnp.maximum(top, 2.0**-100)))
            code = jnp.round(value * (jnp.exp2(-power) * CODE_TOP))
            out[j] = code.astype(jnp.int32).astype(jnp.int16)
            powers = jnp.where(lane == j, power.astype(jnp.int32), powers)
        out[share] = powers.astype(jnp.int16)


def encode(kept, got, parts):
    tiles, occupied, _ = kept.shape
    shape = jax.ShapeDtypeStruct((tiles // parts + 1, occupied, BLK), jnp.int16)
    return pl.pallas_call(
        encode_kernel,
        out_shape=[shape] * parts,
        in_specs=[VMEM_SPEC] * 2,
        out_specs=[VMEM_SPEC] * parts,
        compiler_params=pltpu.CompilerParams(vmem_limit_bytes=8 * MIB),
        cost_estimate=pl.CostEstimate(
            flops=8 * kept.size, bytes_accessed=10 * kept.size, transcendentals=0
        ),
        name="encode_sums",
    )(kept, got)


def decode_kernel(kept, got, *refs):
    arrived, out = refs[:-1], refs[-1]
    share = kept.shape[0]
    lane = lax.broadcasted_iota(jnp.int32, kept.shape[1:], 1)
    for j in range(share):
        value = kept[j] + got[j]
        for part in arrived:
            powers = jnp.where(lane == j, part[share].astype(jnp.int32), 0)
            power = jnp.sum(powers.astype(jnp.float32), axis=1, keepdims=True)
            code = part[j].astype(jnp.int32).astype(jnp.float32)
            value = value + code * (jnp.exp2(power) * (1.0 / CODE_TOP))
        out[:, j * BLK : (j + 1) * BLK] = value


def decode(kept, got, arrived):
    share, occupied, _ = kept.shape
    return pl.pallas_call(
        decode_kernel,
        out_shape=jax.ShapeDtypeStruct((occupied, share * BLK), jnp.float32),
        in_specs=[VMEM_SPEC] * (2 + len(arrived)),
        out_specs=VMEM_SPEC,
        compiler_params=pltpu.CompilerParams(vmem_limit_bytes=8 * MIB),
        cost_estimate=pl.CostEstimate(
            flops=8 * kept.size, bytes_accessed=14 * kept.size, transcendentals=0
        ),
        name="decode_sums",
    )(kept, got, *arrived)


def per_device(amplitudes, virt_irreps, w_tiles, tile_rows, tile_cols):
    occupied = amplitudes.shape[0]
    peers = lax.axis_size("gx")
    groups = lax.axis_size("gy")
    me = lax.axis_index("gx")
    mine = lax.axis_index("gy")
    row_count = amplitudes.shape[1] // BLK * peers
    per = tile_rows.shape[0] // peers
    near = peers // 2

    def swap(x, k):
        return lax.ppermute(x, "gx", [(i, i ^ k) for i in range(peers)])

    slots = tile_rows.shape[0]
    first_far = swap(tile_rows, near)
    place = {near: (first_far, 0)}
    known, rows, bit = [0, near], jnp.concatenate([tile_rows, first_far]), 2
    while bit < near:
        rows = jnp.concatenate([rows, swap(rows, bit)])
        known = known + [k ^ bit for k in known]
        bit *= 2
    odd = swap(rows, 1)
    for j, k in enumerate(known):
        place.setdefault(k, (rows, j * slots))
        place[k ^ 1] = (odd, j * slots)

    amp = stage(amplitudes)
    here = me.reshape(1)
    quarter = near // 4
    far_order = list(range(near, peers, 2)) + list(range(near + 1, peers, 2))
    far = [far_order[j * quarter : (j + 1) * quarter] for j in range(4)]
    arrived = {0: pick(here, tile_rows, 0, amp, per)}
    for k in far[0] + far[1] + list(range(1, near)) + far[2] + far[3]:
        after = ()
        if k in far[2]:
            after = (arrived[far[0][far[2].index(k)]],)
        if k in far[3]:
            after = (arrived[far[0][far[3].index(k)]], arrived[far[1][far[3].index(k)]])
        arrived[k] = swap(pick(here, *place[k], amp, per, after), k)

    row_tile = mine * row_count + tile_rows
    col_tile = me * ABT_X + tile_cols
    live = (pair_irrep(row_tile, virt_irreps) == pair_irrep(col_tile, virt_irreps)).astype(
        jnp.float32
    )
    share = ABT_X // groups
    xs = groups // CORES
    owner = tile_cols // share
    other_core = (owner % CORES) ^ (mine % CORES)
    other_x = (owner // CORES) ^ (mine // CORES)
    cols = other_core * (ABT_X // CORES) + other_x * share + tile_cols % share
    order = jnp.arange(peers, dtype=jnp.int32) ^ me

    w = w_tiles.reshape(peers, per, BLK, BLK)
    args = (order, cols, live, w)
    (total,) = ladder(*args, None, arrived, far[0])
    (total,) = ladder(*args, total, arrived, far[1])
    total, held = ladder(*args, total, arrived, list(range(near)), ahead=far[3])
    (total,) = ladder(*args, total, arrived, far[2])
    sizes = (share, (xs - 1) * share) * CORES
    keep, keep_rest, give, give_rest = ladder(
        order, cols, live, held, total, arrived, far[3], last=sizes
    )

    def swap_gy(x, k):
        return lax.ppermute(x, "gy", [(i, i ^ k) for i in range(groups)])

    coded = encode(keep_rest, swap_gy(give_rest, 1), xs - 1)
    got = swap_gy(give, 1)
    return decode(keep, got, [swap_gy(coded[k - 1], k * CORES) for k in range(1, xs)])


def solution(mesh):
    in_specs = (
        P(None, ("gy", "gx")),
        P(),
        P(("gx", "gy"), None, None),
        P(("gx", "gy")),
        P(("gx", "gy")),
    )
    out_specs = P(None, ("gx", "gy"))
    return jax.shard_map(
        per_device, mesh=mesh, in_specs=in_specs, out_specs=out_specs, check_vma=False
    )
```

```python
import functools

import jax
import jax.numpy as jnp
from jax import lax
from jax.experimental import pallas as pl
from jax.experimental.pallas import tpu as pltpu
from jax.sharding import PartitionSpec as P

V = 1024
BLK = 128
ABT_X = 32
CORES = 2
UNROLL = 32
CODE_TOP = 32000.0
MIB = 1024 * 1024

VMEM_SPEC = pl.BlockSpec(memory_space=pltpu.VMEM)
SMEM_SPEC = pl.BlockSpec(memory_space=pltpu.SMEM)
ANY_SPEC = pl.BlockSpec(memory_space=pl.ANY)


def pair_irrep(tile, virt_irreps):
    first = tile * BLK // V // BLK
    second = tile * BLK % V // BLK
    return jnp.bitwise_xor(virt_irreps[first], virt_irreps[second])


def stage_kernel(source, rows, held, pair, sems):
    copies = [
        pltpu.make_async_copy(source, held, sems.at[0]),
        pltpu.make_async_copy(rows, pair.at[pl.ds(0, rows.shape[0])], sems.at[1]),
    ]
    for copy in copies:
        copy.start()
    for copy in copies:
        copy.wait()


def stage(x, rows):
    return pl.pallas_call(
        stage_kernel,
        out_shape=[
            pltpu.VMEM(x.shape, x.dtype),
            pltpu.VMEM((2 * rows.shape[0],), rows.dtype),
        ],
        in_specs=[ANY_SPEC] * 2,
        out_specs=[VMEM_SPEC] * 2,
        scratch_shapes=[pltpu.SemaphoreType.DMA((2,))],
        compiler_params=pltpu.CompilerParams(vmem_limit_bytes=8 * MIB),
        cost_estimate=pl.CostEstimate(flops=0, bytes_accessed=2 * x.size, transcendentals=0),
        name="stage_amplitudes",
    )(*[pltpu.with_memory_space_constraint(a, pltpu.HBM) for a in (x, rows)])


def pick_kernel(first, per, local_tiles, me, rows, amp, *refs):
    out = refs[-1]
    base = first + me[0] * per
    origin = me[0] * local_tiles

    def step(i, carry):
        lane = pl.multiple_of((rows[base + i] - origin) * BLK, BLK)
        out[i] = amp[:, pl.ds(lane, BLK)]
        return carry

    lax.fori_loop(0, per, step, 0, unroll=8)


def pick(me, rows, first, amp, per, after=()):
    occupied, width = amp.shape
    return pl.pallas_call(
        functools.partial(pick_kernel, first, per, width // BLK),
        out_shape=jax.ShapeDtypeStruct((per, occupied, BLK), amp.dtype),
        in_specs=[SMEM_SPEC, SMEM_SPEC, VMEM_SPEC] + [ANY_SPEC] * len(after),
        out_specs=VMEM_SPEC,
        compiler_params=pltpu.CompilerParams(vmem_limit_bytes=8 * MIB),
        cost_estimate=pl.CostEstimate(
            flops=0, bytes_accessed=4 * per * occupied * BLK, transcendentals=0
        ),
        name="pick_tiles",
    )(me, rows, amp, *after)


def add_products(per, base, cols, live, piece, weights, total):
    unroll = min(UNROLL, per)

    def step(i, carry):
        slots = [i * unroll + u for u in range(unroll)]
        products = [
            jnp.dot(piece[s], weights[s], preferred_element_type=jnp.float32) for s in slots
        ]
        for s, product in zip(slots, products):
            total[cols[base + s]] += product * live[base + s]
        return carry

    lax.fori_loop(0, per // unroll, step, 0)


def ladder_kernel(peers_at, ahead, per, first, last, order, cols, live, w, *refs):
    count = len(peers_at)
    pieces, refs = refs[:count], refs[count:]
    if not first:
        start, refs = refs[0], refs[1:]
    if last:
        outs, held, total = refs, w, start
    else:
        *outs, held, sems = refs
        total = outs[0]
    copies = []
    for j, k in enumerate([] if last else peers_at + ahead):
        target = held.at[j] if j < count else outs[1].at[j - count]
        copies.append(pltpu.make_async_copy(w.at[order[k]], target, sems.at[j]))
        copies[-1].start()
    if first:
        total[...] = jnp.zeros_like(total)
    for j, k in enumerate(peers_at):
        if not last:
            copies[j].wait()
        add_products(per, order[k] * per, cols, live, pieces[j], held.at[j], total)
    for copy in copies[count:]:
        copy.wait()
    if last:
        at = 0
        for out in outs:
            out[...] = total[at : at + out.shape[0]]
            at += out.shape[0]


def ladder(order, cols, live, w, start, arrived, peers_at, ahead=(), last=None):
    pieces = [arrived[k] for k in peers_at]
    count = len(pieces)
    per, occupied, _ = pieces[0].shape
    first = start is None
    scratch = []
    if last:
        out_shape = [jax.ShapeDtypeStruct((n, occupied, BLK), jnp.float32) for n in last]
    else:
        out_shape = [pltpu.VMEM((ABT_X, occupied, BLK), jnp.float32)]
        if ahead:
            out_shape.append(pltpu.VMEM((len(ahead), per, BLK, BLK), w.dtype))
        scratch = [
            pltpu.VMEM((count, per, BLK, BLK), w.dtype),
            pltpu.SemaphoreType.DMA((count + len(ahead),)),
        ]
        w = pltpu.with_memory_space_constraint(w, pltpu.HBM)
    return pl.pallas_call(
        functools.partial(ladder_kernel, peers_at, list(ahead), per, first, bool(last)),
        out_shape=out_shape,
        in_specs=[SMEM_SPEC] * 3
        + [VMEM_SPEC if last else ANY_SPEC]
        + [VMEM_SPEC] * (count + (not first)),
        out_specs=[VMEM_SPEC] * len(out_shape),
        input_output_aliases={} if first or last else {4 + count: 0},
        scratch_shapes=scratch,
        compiler_params=pltpu.CompilerParams(vmem_limit_bytes=8 * MIB),
        cost_estimate=pl.CostEstimate(
            flops=2 * count * per * occupied * BLK * BLK,
            bytes_accessed=2 * (count + len(ahead)) * per * BLK * BLK,
            transcendentals=0,
        ),
        name="ladder_products",
    )(order, cols, live, w, *pieces, *([] if first else [start]))


def encode_kernel(kept, got, *outs):
    share = outs[0].shape[0] - 1
    lane = lax.broadcasted_iota(jnp.int32, kept.shape[1:], 1)
    for b, out in enumerate(outs):
        powers = jnp.zeros(kept.shape[1:], jnp.int32)
        for j in range(share):
            value = kept[b * share + j] + got[b * share + j]
            top = jnp.max(jnp.abs(value), axis=1, keepdims=True)
            power = jnp.ceil(jnp.log2(jnp.maximum(top, 2.0**-100)))
            code = jnp.round(value * (jnp.exp2(-power) * CODE_TOP))
            out[j] = code.astype(jnp.int32).astype(jnp.int16)
            powers = jnp.where(lane == j, power.astype(jnp.int32), powers)
        out[share] = powers.astype(jnp.int16)


def encode(kept, got, parts):
    tiles, occupied, _ = kept.shape
    shape = jax.ShapeDtypeStruct((tiles // parts + 1, occupied, BLK), jnp.int16)
    return pl.pallas_call(
        encode_kernel,
        out_shape=[shape] * parts,
        in_specs=[VMEM_SPEC] * 2,
        out_specs=[VMEM_SPEC] * parts,
        compiler_params=pltpu.CompilerParams(vmem_limit_bytes=8 * MIB),
        cost_estimate=pl.CostEstimate(
            flops=8 * kept.size, bytes_accessed=10 * kept.size, transcendentals=0
        ),
        name="encode_sums",
    )(kept, got)


def decode_kernel(kept, got, *refs):
    arrived, out = refs[:-1], refs[-1]
    share = kept.shape[0]
    lane = lax.broadcasted_iota(jnp.int32, kept.shape[1:], 1)
    for j in range(share):
        value = kept[j] + got[j]
        for part in arrived:
            powers = jnp.where(lane == j, part[share].astype(jnp.int32), 0)
            power = jnp.sum(powers.astype(jnp.float32), axis=1, keepdims=True)
            code = part[j].astype(jnp.int32).astype(jnp.float32)
            value = value + code * (jnp.exp2(power) * (1.0 / CODE_TOP))
        out[:, j * BLK : (j + 1) * BLK] = value


def decode(kept, got, arrived):
    share, occupied, _ = kept.shape
    return pl.pallas_call(
        decode_kernel,
        out_shape=jax.ShapeDtypeStruct((occupied, share * BLK), jnp.float32),
        in_specs=[VMEM_SPEC] * (2 + len(arrived)),
        out_specs=VMEM_SPEC,
        compiler_params=pltpu.CompilerParams(vmem_limit_bytes=8 * MIB),
        cost_estimate=pl.CostEstimate(
            flops=8 * kept.size, bytes_accessed=14 * kept.size, transcendentals=0
        ),
        name="decode_sums",
    )(kept, got, *arrived)


def per_device(amplitudes, virt_irreps, w_tiles, tile_rows, tile_cols):
    occupied = amplitudes.shape[0]
    peers = lax.axis_size("gx")
    groups = lax.axis_size("gy")
    me = lax.axis_index("gx")
    mine = lax.axis_index("gy")
    row_count = amplitudes.shape[1] // BLK * peers
    per = tile_rows.shape[0] // peers
    near = peers // 2

    def swap(x, k):
        return lax.ppermute(x, "gx", [(i, i ^ k) for i in range(peers)])

    slots = tile_rows.shape[0]
    first_far = swap(tile_rows, near)
    place = {near: (first_far, 0)}
    amp, pair = stage(amplitudes, tile_rows)
    known, rows, bit = [0, near], lax.dynamic_update_slice(pair, first_far, (slots,)), 2
    while bit < near:
        rows = jnp.concatenate([rows, swap(rows, bit)])
        known = known + [k ^ bit for k in known]
        bit *= 2
    odd = swap(rows, 1)
    for j, k in enumerate(known):
        place.setdefault(k, (rows, j * slots))
        place[k ^ 1] = (odd, j * slots)

    here = me.reshape(1)
    quarter = near // 4
    far_order = list(range(near, peers, 2)) + list(range(near + 1, peers, 2))
    far = [far_order[j * quarter : (j + 1) * quarter] for j in range(4)]
    arrived = {0: pick(here, tile_rows, 0, amp, per)}
    for k in far[0] + far[1] + list(range(1, near)) + far[2] + far[3]:
        after = ()
        if k in far[2]:
            after = (arrived[far[0][far[2].index(k)]],)
        if k in far[3]:
            after = (arrived[far[0][far[3].index(k)]], arrived[2 + far[3].index(k)])
        arrived[k] = swap(pick(here, *place[k], amp, per, after), k)

    row_tile = mine * row_count + tile_rows
    col_tile = me * ABT_X + tile_cols
    live = (pair_irrep(row_tile, virt_irreps) == pair_irrep(col_tile, virt_irreps)).astype(
        jnp.float32
    )
    share = ABT_X // groups
    xs = groups // CORES
    owner = tile_cols // share
    other_core = (owner % CORES) ^ (mine % CORES)
    other_x = (owner // CORES) ^ (mine // CORES)
    cols = other_core * (ABT_X // CORES) + other_x * share + tile_cols % share
    order = jnp.arange(peers, dtype=jnp.int32) ^ me

    w = w_tiles.reshape(peers, per, BLK, BLK)
    args = (order, cols, live, w)
    (total,) = ladder(*args, None, arrived, far[0])
    (total,) = ladder(*args, total, arrived, far[1])
    total, held = ladder(*args, total, arrived, list(range(near)), ahead=far[3])
    (total,) = ladder(*args, total, arrived, far[2])
    sizes = (share, (xs - 1) * share) * CORES
    keep, keep_rest, give, give_rest = ladder(
        order, cols, live, held, total, arrived, far[3], last=sizes
    )

    def swap_gy(x, k):
        return lax.ppermute(x, "gy", [(i, i ^ k) for i in range(groups)])

    coded = encode(keep_rest, swap_gy(give_rest, 1), xs - 1)
    got = swap_gy(give, 1)
    return decode(keep, got, [swap_gy(coded[k - 1], k * CORES) for k in range(1, xs)])


def solution(mesh):
    in_specs = (
        P(None, ("gy", "gx")),
        P(),
        P(("gx", "gy"), None, None),
        P(("gx", "gy")),
        P(("gx", "gy")),
    )
    out_specs = P(None, ("gx", "gy"))
    return jax.shard_map(
        per_device, mesh=mesh, in_specs=in_specs, out_specs=out_specs, check_vma=False
    )
```

```python
import functools

import jax
import jax.numpy as jnp
from jax import lax
from jax.experimental import pallas as pl
from jax.experimental.pallas import tpu as pltpu
from jax.sharding import PartitionSpec as P

V = 1024
BLK = 128
ABT_X = 32
CORES = 2
UNROLL = 32
CODE_TOP = 32000.0
MIB = 1024 * 1024

VMEM_SPEC = pl.BlockSpec(memory_space=pltpu.VMEM)
SMEM_SPEC = pl.BlockSpec(memory_space=pltpu.SMEM)
ANY_SPEC = pl.BlockSpec(memory_space=pl.ANY)


def pair_irrep(tile, virt_irreps):
    first = tile * BLK // V // BLK
    second = tile * BLK % V // BLK
    return jnp.bitwise_xor(virt_irreps[first], virt_irreps[second])


def stage_kernel(source, held, sem):
    copy = pltpu.make_async_copy(source, held, sem)
    copy.start()
    copy.wait()


def stage(x):
    return pl.pallas_call(
        stage_kernel,
        out_shape=pltpu.VMEM(x.shape, x.dtype),
        in_specs=[ANY_SPEC],
        out_specs=VMEM_SPEC,
        scratch_shapes=[pltpu.SemaphoreType.DMA],
        compiler_params=pltpu.CompilerParams(vmem_limit_bytes=8 * MIB),
        cost_estimate=pl.CostEstimate(flops=0, bytes_accessed=2 * x.size, transcendentals=0),
        name="stage_amplitudes",
    )(pltpu.with_memory_space_constraint(x, pltpu.HBM))


def pick_kernel(first, per, local_tiles, me, rows, amp, *refs):
    out = refs[-1]
    base = first + me[0] * per
    origin = me[0] * local_tiles

    def step(i, carry):
        lane = pl.multiple_of((rows[base + i] - origin) * BLK, BLK)
        out[i] = amp[:, pl.ds(lane, BLK)]
        return carry

    lax.fori_loop(0, per, step, 0, unroll=8)


def pick(me, rows, first, amp, per, after=()):
    occupied, width = amp.shape
    return pl.pallas_call(
        functools.partial(pick_kernel, first, per, width // BLK),
        out_shape=jax.ShapeDtypeStruct((per, occupied, BLK), amp.dtype),
        in_specs=[SMEM_SPEC, SMEM_SPEC, VMEM_SPEC] + [ANY_SPEC] * len(after),
        out_specs=VMEM_SPEC,
        compiler_params=pltpu.CompilerParams(vmem_limit_bytes=8 * MIB),
        cost_estimate=pl.CostEstimate(
            flops=0, bytes_accessed=4 * per * occupied * BLK, transcendentals=0
        ),
        name="pick_tiles",
    )(me, rows, amp, *after)


def add_products(per, base, cols, live, piece, weights, total):
    unroll = min(UNROLL, per)

    def step(i, carry):
        slots = [i * unroll + u for u in range(unroll)]
        products = [
            jnp.dot(piece[s], weights[s], preferred_element_type=jnp.float32) for s in slots
        ]
        for s, product in zip(slots, products):
            total[cols[base + s]] += product * live[base + s]
        return carry

    lax.fori_loop(0, per // unroll, step, 0)


def ladder_kernel(peers_at, ahead, per, first, last, order, cols, live, w, *refs):
    count = len(peers_at)
    pieces, refs = refs[:count], refs[count:]
    if not first:
        start, refs = refs[0], refs[1:]
    if last:
        outs, held, total = refs, w, start
    else:
        *outs, held, sems = refs
        total = outs[0]
    copies = []
    for j, k in enumerate([] if last else peers_at + ahead):
        target = held.at[j] if j < count else outs[1].at[j - count]
        copies.append(pltpu.make_async_copy(w.at[order[k]], target, sems.at[j]))
        copies[-1].start()
    if first:
        total[...] = jnp.zeros_like(total)
    for j, k in enumerate(peers_at):
        if not last:
            copies[j].wait()
        add_products(per, order[k] * per, cols, live, pieces[j], held.at[j], total)
    for copy in copies[count:]:
        copy.wait()
    if last:
        at = 0
        for out in outs:
            out[...] = total[at : at + out.shape[0]]
            at += out.shape[0]


def ladder(order, cols, live, w, start, arrived, peers_at, ahead=(), last=None):
    pieces = [arrived[k] for k in peers_at]
    count = len(pieces)
    per, occupied, _ = pieces[0].shape
    first = start is None
    scratch = []
    if last:
        out_shape = [jax.ShapeDtypeStruct((n, occupied, BLK), jnp.float32) for n in last]
    else:
        out_shape = [pltpu.VMEM((ABT_X, occupied, BLK), jnp.float32)]
        if ahead:
            out_shape.append(pltpu.VMEM((len(ahead), per, BLK, BLK), w.dtype))
        scratch = [
            pltpu.VMEM((count, per, BLK, BLK), w.dtype),
            pltpu.SemaphoreType.DMA((count + len(ahead),)),
        ]
        w = pltpu.with_memory_space_constraint(w, pltpu.HBM)
    return pl.pallas_call(
        functools.partial(ladder_kernel, peers_at, list(ahead), per, first, bool(last)),
        out_shape=out_shape,
        in_specs=[SMEM_SPEC] * 3
        + [VMEM_SPEC if last else ANY_SPEC]
        + [VMEM_SPEC] * (count + (not first)),
        out_specs=[VMEM_SPEC] * len(out_shape),
        input_output_aliases={} if first or last else {4 + count: 0},
        scratch_shapes=scratch,
        compiler_params=pltpu.CompilerParams(vmem_limit_bytes=8 * MIB),
        cost_estimate=pl.CostEstimate(
            flops=2 * count * per * occupied * BLK * BLK,
            bytes_accessed=2 * (count + len(ahead)) * per * BLK * BLK,
            transcendentals=0,
        ),
        name="ladder_products",
    )(order, cols, live, w, *pieces, *([] if first else [start]))


def encode_kernel(kept, got, *outs):
    share = outs[0].shape[0] - 1
    lane = lax.broadcasted_iota(jnp.int32, kept.shape[1:], 1)
    for b, out in enumerate(outs):
        powers = jnp.zeros(kept.shape[1:], jnp.int32)
        for j in range(share):
            value = kept[b * share + j] + got[b * share + j]
            top = jnp.max(jnp.abs(value), axis=1, keepdims=True)
            power = jnp.ceil(jnp.log2(jnp.maximum(top, 2.0**-100)))
            code = jnp.round(value * (jnp.exp2(-power) * CODE_TOP))
            out[j] = code.astype(jnp.int32).astype(jnp.int16)
            powers = jnp.where(lane == j, power.astype(jnp.int32), powers)
        out[share] = powers.astype(jnp.int16)


def encode(kept, got, parts):
    tiles, occupied, _ = kept.shape
    shape = jax.ShapeDtypeStruct((tiles // parts + 1, occupied, BLK), jnp.int16)
    return pl.pallas_call(
        encode_kernel,
        out_shape=[shape] * parts,
        in_specs=[VMEM_SPEC] * 2,
        out_specs=[VMEM_SPEC] * parts,
        compiler_params=pltpu.CompilerParams(vmem_limit_bytes=8 * MIB),
        cost_estimate=pl.CostEstimate(
            flops=8 * kept.size, bytes_accessed=10 * kept.size, transcendentals=0
        ),
        name="encode_sums",
    )(kept, got)


def decode_kernel(kept, got, *refs):
    *arrived, out, held, sems = refs
    share = kept.shape[0]
    lane = lax.broadcasted_iota(jnp.int32, kept.shape[1:], 1)
    copies = []
    for j in range(share):
        value = kept[j] + got[j]
        for part in arrived:
            powers = jnp.where(lane == j, part[share].astype(jnp.int32), 0)
            power = jnp.sum(powers.astype(jnp.float32), axis=1, keepdims=True)
            code = part[j].astype(jnp.int32).astype(jnp.float32)
            value = value + code * (jnp.exp2(power) * (1.0 / CODE_TOP))
        held[j] = value
        columns = out.at[:, pl.ds(j * BLK, BLK)]
        copies.append(pltpu.make_async_copy(held.at[j], columns, sems.at[j]))
        copies[-1].start()
    for copy in copies:
        copy.wait()


def decode(kept, got, arrived):
    share, occupied, _ = kept.shape
    return pl.pallas_call(
        decode_kernel,
        out_shape=jax.ShapeDtypeStruct((occupied, share * BLK), jnp.float32),
        in_specs=[VMEM_SPEC] * (2 + len(arrived)),
        out_specs=ANY_SPEC,
        scratch_shapes=[
            pltpu.VMEM(kept.shape, jnp.float32),
            pltpu.SemaphoreType.DMA((share,)),
        ],
        compiler_params=pltpu.CompilerParams(vmem_limit_bytes=8 * MIB),
        cost_estimate=pl.CostEstimate(
            flops=8 * kept.size, bytes_accessed=14 * kept.size, transcendentals=0
        ),
        name="decode_sums",
    )(kept, got, *arrived)


def per_device(amplitudes, virt_irreps, w_tiles, tile_rows, tile_cols):
    occupied = amplitudes.shape[0]
    peers = lax.axis_size("gx")
    groups = lax.axis_size("gy")
    me = lax.axis_index("gx")
    mine = lax.axis_index("gy")
    row_count = amplitudes.shape[1] // BLK * peers
    per = tile_rows.shape[0] // peers
    near = peers // 2

    def swap(x, k):
        return lax.ppermute(x, "gx", [(i, i ^ k) for i in range(peers)])

    slots = tile_rows.shape[0]
    first_far = swap(tile_rows, near)
    place = {near: (first_far, 0)}
    known, rows, bit = [0, near], jnp.concatenate([tile_rows, first_far]), 2
    while bit < near:
        rows = jnp.concatenate([rows, swap(rows, bit)])
        known = known + [k ^ bit for k in known]
        bit *= 2
    odd = swap(rows, 1)
    for j, k in enumerate(known):
        place.setdefault(k, (rows, j * slots))
        place[k ^ 1] = (odd, j * slots)

    amp = stage(amplitudes)
    here = me.reshape(1)
    quarter = near // 4
    far_order = list(range(near, peers, 2)) + list(range(near + 1, peers, 2))
    far = [far_order[j * quarter : (j + 1) * quarter] for j in range(4)]
    arrived = {0: pick(here, tile_rows, 0, amp, per)}
    for k in far[0] + far[1] + list(range(2, near, 2)) + list(range(1, near, 2)) + far[2] + far[3]:
        after = (arrived[far[0][0]],) if k < near else ()
        if k in far[2]:
            after = (arrived[far[0][far[2].index(k)]],)
        if k in far[3]:
            after = (arrived[far[0][far[3].index(k)]], arrived[far[1][far[3].index(k)]])
        arrived[k] = swap(pick(here, *place[k], amp, per, after), k)

    row_tile = mine * row_count + tile_rows
    col_tile = me * ABT_X + tile_cols
    live = (pair_irrep(row_tile, virt_irreps) == pair_irrep(col_tile, virt_irreps)).astype(
        jnp.float32
    )
    share = ABT_X // groups
    xs = groups // CORES
    owner = tile_cols // share
    other_core = (owner % CORES) ^ (mine % CORES)
    other_x = (owner // CORES) ^ (mine // CORES)
    cols = other_core * (ABT_X // CORES) + other_x * share + tile_cols % share
    order = jnp.arange(peers, dtype=jnp.int32) ^ me

    w = w_tiles.reshape(peers, per, BLK, BLK)
    args = (order, cols, live, w)
    (total,) = ladder(*args, None, arrived, far[0])
    (total,) = ladder(*args, total, arrived, far[1])
    total, held = ladder(*args, total, arrived, list(range(near)), ahead=far[3])
    (total,) = ladder(*args, total, arrived, far[2])
    sizes = (share, (xs - 1) * share) * CORES
    keep, keep_rest, give, give_rest = ladder(
        order, cols, live, held, total, arrived, far[3], last=sizes
    )

    def swap_gy(x, k):
        return lax.ppermute(x, "gy", [(i, i ^ k) for i in range(groups)])

    coded = encode(keep_rest, swap_gy(give_rest, 1), xs - 1)
    got = swap_gy(give, 1)
    return decode(keep, got, [swap_gy(coded[k - 1], k * CORES) for k in range(1, xs)])


def solution(mesh):
    in_specs = (
        P(None, ("gy", "gx")),
        P(),
        P(("gx", "gy"), None, None),
        P(("gx", "gy")),
        P(("gx", "gy")),
    )
    out_specs = P(None, ("gx", "gy"))
    return jax.shard_map(
        per_device, mesh=mesh, in_specs=in_specs, out_specs=out_specs, check_vma=False
    )
```

```python
import functools

import jax
import jax.numpy as jnp
from jax import lax
from jax.experimental import pallas as pl
from jax.experimental.pallas import tpu as pltpu
from jax.sharding import PartitionSpec as P

V = 1024
BLK = 128
ABT_X = 32
CORES = 2
UNROLL = 32
CODE_TOP = 32000.0
MIB = 1024 * 1024

VMEM_SPEC = pl.BlockSpec(memory_space=pltpu.VMEM)
SMEM_SPEC = pl.BlockSpec(memory_space=pltpu.SMEM)
ANY_SPEC = pl.BlockSpec(memory_space=pl.ANY)


def pair_irrep(tile, virt_irreps):
    first = tile * BLK // V // BLK
    second = tile * BLK % V // BLK
    return jnp.bitwise_xor(virt_irreps[first], virt_irreps[second])


def stage_kernel(source, held, sem):
    copy = pltpu.make_async_copy(source, held, sem)
    copy.start()
    copy.wait()


def stage(x):
    return pl.pallas_call(
        stage_kernel,
        out_shape=pltpu.VMEM(x.shape, x.dtype),
        in_specs=[ANY_SPEC],
        out_specs=VMEM_SPEC,
        scratch_shapes=[pltpu.SemaphoreType.DMA],
        compiler_params=pltpu.CompilerParams(vmem_limit_bytes=8 * MIB),
        cost_estimate=pl.CostEstimate(flops=0, bytes_accessed=2 * x.size, transcendentals=0),
        name="stage_amplitudes",
    )(pltpu.with_memory_space_constraint(x, pltpu.HBM))


def pick_kernel(first, per, local_tiles, me, rows, amp, *refs):
    out = refs[-1]
    base = first + me[0] * per
    origin = me[0] * local_tiles

    def step(i, carry):
        lane = pl.multiple_of((rows[base + i] - origin) * BLK, BLK)
        out[i] = amp[:, pl.ds(lane, BLK)]
        return carry

    lax.fori_loop(0, per, step, 0, unroll=8)


def passing_pick_kernel(first, per, local_tiles, me, rows, amp, *refs):
    pick_kernel(first, per, local_tiles, me, rows, amp, refs[-2])


def pick(me, rows, first, amp, per, after=(), passed=None):
    occupied, width = amp.shape
    shape = jax.ShapeDtypeStruct((per, occupied, BLK), amp.dtype)
    through = passed is not None
    if through:
        after = (passed, *after)
    kernel = passing_pick_kernel if through else pick_kernel
    return pl.pallas_call(
        functools.partial(kernel, first, per, width // BLK),
        out_shape=[shape, jax.ShapeDtypeStruct(passed.shape, passed.dtype)] if through else shape,
        in_specs=[SMEM_SPEC, SMEM_SPEC, VMEM_SPEC] + [ANY_SPEC] * len(after),
        out_specs=[VMEM_SPEC, ANY_SPEC] if through else VMEM_SPEC,
        input_output_aliases={3: 1} if through else {},
        compiler_params=pltpu.CompilerParams(vmem_limit_bytes=8 * MIB),
        cost_estimate=pl.CostEstimate(
            flops=0, bytes_accessed=4 * per * occupied * BLK, transcendentals=0
        ),
        name="pick_tiles",
    )(me, rows, amp, *after)


def add_products(per, base, cols, live, piece, weights, total):
    unroll = min(UNROLL, per)

    def step(i, carry):
        slots = [i * unroll + u for u in range(unroll)]
        products = [
            jnp.dot(piece[s], weights[s], preferred_element_type=jnp.float32) for s in slots
        ]
        for s, product in zip(slots, products):
            total[cols[base + s]] += product * live[base + s]
        return carry

    lax.fori_loop(0, per // unroll, step, 0)


def ladder_kernel(peers_at, ahead, per, first, last, order, cols, live, w, *refs):
    count = len(peers_at)
    pieces, refs = refs[:count], refs[count:]
    if not first:
        start, refs = refs[0], refs[1:]
    if last:
        outs, held, total = refs, w, start
    else:
        *outs, held, sems = refs
        total = outs[0]
    copies = []
    for j, k in enumerate([] if last else peers_at + ahead):
        target = held.at[j] if j < count else outs[1].at[j - count]
        copies.append(pltpu.make_async_copy(w.at[order[k]], target, sems.at[j]))
        copies[-1].start()
    if first:
        total[...] = jnp.zeros_like(total)
    for j, k in enumerate(peers_at):
        if not last:
            copies[j].wait()
        add_products(per, order[k] * per, cols, live, pieces[j], held.at[j], total)
    for copy in copies[count:]:
        copy.wait()
    if last:
        at = 0
        for out in outs:
            out[...] = total[at : at + out.shape[0]]
            at += out.shape[0]


def ladder(order, cols, live, w, start, arrived, peers_at, ahead=(), last=None):
    pieces = [arrived[k] for k in peers_at]
    count = len(pieces)
    per, occupied, _ = pieces[0].shape
    first = start is None
    scratch = []
    if last:
        out_shape = [jax.ShapeDtypeStruct((n, occupied, BLK), jnp.float32) for n in last]
    else:
        out_shape = [pltpu.VMEM((ABT_X, occupied, BLK), jnp.float32)]
        if ahead:
            out_shape.append(pltpu.VMEM((len(ahead), per, BLK, BLK), w.dtype))
        scratch = [
            pltpu.VMEM((count, per, BLK, BLK), w.dtype),
            pltpu.SemaphoreType.DMA((count + len(ahead),)),
        ]
        w = pltpu.with_memory_space_constraint(w, pltpu.HBM)
    return pl.pallas_call(
        functools.partial(ladder_kernel, peers_at, list(ahead), per, first, bool(last)),
        out_shape=out_shape,
        in_specs=[SMEM_SPEC] * 3
        + [VMEM_SPEC if last else ANY_SPEC]
        + [VMEM_SPEC] * (count + (not first)),
        out_specs=[VMEM_SPEC] * len(out_shape),
        input_output_aliases={} if first or last else {4 + count: 0},
        scratch_shapes=scratch,
        compiler_params=pltpu.CompilerParams(vmem_limit_bytes=8 * MIB),
        cost_estimate=pl.CostEstimate(
            flops=2 * count * per * occupied * BLK * BLK,
            bytes_accessed=2 * (count + len(ahead)) * per * BLK * BLK,
            transcendentals=0,
        ),
        name="ladder_products",
    )(order, cols, live, w, *pieces, *([] if first else [start]))


def encode_kernel(kept, got, *outs):
    share = outs[0].shape[0] - 1
    lane = lax.broadcasted_iota(jnp.int32, kept.shape[1:], 1)
    for b, out in enumerate(outs):
        powers = jnp.zeros(kept.shape[1:], jnp.int32)
        for j in range(share):
            value = kept[b * share + j] + got[b * share + j]
            top = jnp.max(jnp.abs(value), axis=1, keepdims=True)
            power = jnp.ceil(jnp.log2(jnp.maximum(top, 2.0**-100)))
            code = jnp.round(value * (jnp.exp2(-power) * CODE_TOP))
            out[j] = code.astype(jnp.int32).astype(jnp.int16)
            powers = jnp.where(lane == j, power.astype(jnp.int32), powers)
        out[share] = powers.astype(jnp.int16)


def encode(kept, got, parts):
    tiles, occupied, _ = kept.shape
    shape = jax.ShapeDtypeStruct((tiles // parts + 1, occupied, BLK), jnp.int16)
    return pl.pallas_call(
        encode_kernel,
        out_shape=[shape] * parts,
        in_specs=[VMEM_SPEC] * 2,
        out_specs=[VMEM_SPEC] * parts,
        compiler_params=pltpu.CompilerParams(vmem_limit_bytes=8 * MIB),
        cost_estimate=pl.CostEstimate(
            flops=8 * kept.size, bytes_accessed=10 * kept.size, transcendentals=0
        ),
        name="encode_sums",
    )(kept, got)


def decode_kernel(kept, got, *refs):
    arrived, out = refs[:-1], refs[-1]
    share = kept.shape[0]
    lane = lax.broadcasted_iota(jnp.int32, kept.shape[1:], 1)
    for j in range(share):
        value = kept[j] + got[j]
        for part in arrived:
            powers = jnp.where(lane == j, part[share].astype(jnp.int32), 0)
            power = jnp.sum(powers.astype(jnp.float32), axis=1, keepdims=True)
            code = part[j].astype(jnp.int32).astype(jnp.float32)
            value = value + code * (jnp.exp2(power) * (1.0 / CODE_TOP))
        out[:, j * BLK : (j + 1) * BLK] = value


def decode(kept, got, arrived):
    share, occupied, _ = kept.shape
    return pl.pallas_call(
        decode_kernel,
        out_shape=jax.ShapeDtypeStruct((occupied, share * BLK), jnp.float32),
        in_specs=[VMEM_SPEC] * (2 + len(arrived)),
        out_specs=VMEM_SPEC,
        compiler_params=pltpu.CompilerParams(vmem_limit_bytes=8 * MIB),
        cost_estimate=pl.CostEstimate(
            flops=8 * kept.size, bytes_accessed=14 * kept.size, transcendentals=0
        ),
        name="decode_sums",
    )(kept, got, *arrived)


def per_device(amplitudes, virt_irreps, w_tiles, tile_rows, tile_cols):
    occupied = amplitudes.shape[0]
    peers = lax.axis_size("gx")
    groups = lax.axis_size("gy")
    me = lax.axis_index("gx")
    mine = lax.axis_index("gy")
    row_count = amplitudes.shape[1] // BLK * peers
    per = tile_rows.shape[0] // peers
    near = peers // 2

    def swap(x, k):
        return lax.ppermute(x, "gx", [(i, i ^ k) for i in range(peers)])

    slots = tile_rows.shape[0]
    first_far = swap(tile_rows, near)
    place = {near: (first_far, 0)}
    amp = stage(amplitudes)
    here = me.reshape(1)
    picked, own_rows = pick(here, first_far, 0, amp, per, passed=tile_rows)
    known, rows, bit = [0, near], jnp.concatenate([own_rows, first_far]), 1
    while bit < near:
        got = swap(rows, bit)
        for j, k in enumerate(known):
            place[k ^ bit] = (got, j * slots)
        rows = jnp.concatenate([rows, got])
        known = known + [k ^ bit for k in known]
        bit *= 2

    quarter = near // 4
    far_order = list(range(near, peers))
    far = [far_order[j * quarter : (j + 1) * quarter] for j in range(4)]
    arrived = {0: pick(here, own_rows, 0, amp, per), near: swap(picked, near)}
    for k in far[0][1:] + far[1] + list(range(1, near)) + far[2] + far[3]:
        after = ()
        if k in far[2]:
            after = (arrived[far[0][far[2].index(k)]],)
        if k in far[3]:
            after = (arrived[far[0][far[3].index(k)]], arrived[far[1][far[3].index(k)]])
        arrived[k] = swap(pick(here, *place[k], amp, per, after), k)

    row_tile = mine * row_count + tile_rows
    col_tile = me * ABT_X + tile_cols
    live = (pair_irrep(row_tile, virt_irreps) == pair_irrep(col_tile, virt_irreps)).astype(
        jnp.float32
    )
    share = ABT_X // groups
    xs = groups // CORES
    owner = tile_cols // share
    other_core = (owner % CORES) ^ (mine % CORES)
    other_x = (owner // CORES) ^ (mine // CORES)
    cols = other_core * (ABT_X // CORES) + other_x * share + tile_cols % share
    order = jnp.arange(peers, dtype=jnp.int32) ^ me

    w = w_tiles.reshape(peers, per, BLK, BLK)
    args = (order, cols, live, w)
    (total,) = ladder(*args, None, arrived, far[0])
    (total,) = ladder(*args, total, arrived, far[1])
    total, held = ladder(*args, total, arrived, list(range(near)), ahead=far[3])
    (total,) = ladder(*args, total, arrived, far[2])
    sizes = (share, (xs - 1) * share) * CORES
    keep, keep_rest, give, give_rest = ladder(
        order, cols, live, held, total, arrived, far[3], last=sizes
    )

    def swap_gy(x, k):
        return lax.ppermute(x, "gy", [(i, i ^ k) for i in range(groups)])

    coded = encode(keep_rest, swap_gy(give_rest, 1), xs - 1)
    got = swap_gy(give, 1)
    return decode(keep, got, [swap_gy(coded[k - 1], k * CORES) for k in range(1, xs)])


def solution(mesh):
    in_specs = (
        P(None, ("gy", "gx")),
        P(),
        P(("gx", "gy"), None, None),
        P(("gx", "gy")),
        P(("gx", "gy")),
    )
    out_specs = P(None, ("gx", "gy"))
    return jax.shard_map(
        per_device, mesh=mesh, in_specs=in_specs, out_specs=out_specs, check_vma=False
    )
```

```python
import functools
import math

import jax
import jax.numpy as jnp
from jax import lax
from jax.experimental import pallas as pl
from jax.experimental.pallas import tpu as pltpu
from jax.sharding import PartitionSpec as P

V = 1024
BLK = 128
ABT_X = 32
CORES = 2
UNROLL = 32
CODE_TOP = 32000.0
MIB = 1024 * 1024

VMEM_SPEC = pl.BlockSpec(memory_space=pltpu.VMEM)
SMEM_SPEC = pl.BlockSpec(memory_space=pltpu.SMEM)
ANY_SPEC = pl.BlockSpec(memory_space=pl.ANY)


def pair_irrep(tile, virt_irreps):
    first = tile * BLK // V // BLK
    second = tile * BLK % V // BLK
    return jnp.bitwise_xor(virt_irreps[first], virt_irreps[second])


def stage_kernel(source, held, sem):
    copy = pltpu.make_async_copy(source, held, sem)
    copy.start()
    copy.wait()


def stage(x):
    return pl.pallas_call(
        stage_kernel,
        out_shape=pltpu.VMEM(x.shape, x.dtype),
        in_specs=[ANY_SPEC],
        out_specs=VMEM_SPEC,
        scratch_shapes=[pltpu.SemaphoreType.DMA],
        compiler_params=pltpu.CompilerParams(vmem_limit_bytes=8 * MIB),
        cost_estimate=pl.CostEstimate(flops=0, bytes_accessed=2 * x.size, transcendentals=0),
        name="stage_amplitudes",
    )(pltpu.with_memory_space_constraint(x, pltpu.HBM))


def pick_kernel(first, per, local_tiles, me, rows, amp, *refs):
    out = refs[-1]
    base = first + me[0] * per
    origin = me[0] * local_tiles

    def step(i, carry):
        lane = pl.multiple_of((rows[base + i] - origin) * BLK, BLK)
        out[i] = amp[:, pl.ds(lane, BLK)]
        return carry

    lax.fori_loop(0, out.shape[0], step, 0, unroll=math.gcd(out.shape[0], 8))


def pick(me, rows, first, amp, per, part, after=()):
    occupied, width = amp.shape
    low, count = part
    return pl.pallas_call(
        functools.partial(pick_kernel, first + low, per, width // BLK),
        out_shape=jax.ShapeDtypeStruct((count, occupied, BLK), amp.dtype),
        in_specs=[SMEM_SPEC, SMEM_SPEC, VMEM_SPEC] + [ANY_SPEC] * len(after),
        out_specs=VMEM_SPEC,
        compiler_params=pltpu.CompilerParams(vmem_limit_bytes=8 * MIB),
        cost_estimate=pl.CostEstimate(
            flops=0, bytes_accessed=4 * count * occupied * BLK, transcendentals=0
        ),
        name="pick_tiles",
    )(me, rows, amp, *after)


def add_products(base, cols, live, piece, weights, total):
    count = piece.shape[0]
    unroll = min(UNROLL, count)

    def step(i, carry):
        slots = [i * unroll + u for u in range(unroll)]
        products = [
            jnp.dot(piece[s], weights[s], preferred_element_type=jnp.float32) for s in slots
        ]
        for s, product in zip(slots, products):
            total[cols[base + s]] += product * live[base + s]
        return carry

    lax.fori_loop(0, count // unroll, step, 0)


def ladder_kernel(parts, ahead, per, first, last, order, cols, live, w, *refs):
    count = len(parts)
    pieces, refs = refs[:count], refs[count:]
    if not first:
        start, refs = refs[0], refs[1:]
    if last:
        outs, held, total = refs, w, start
    else:
        *outs, held, sems = refs
        total = outs[0]
    copies = []
    for j, (k, low, size) in enumerate([] if last else parts + ahead):
        target = held.at[j] if j < count else outs[1].at[j - count]
        source = w.at[order[k], pl.ds(low, size)]
        copies.append(pltpu.make_async_copy(source, target, sems.at[j]))
        copies[-1].start()
    if first:
        total[...] = jnp.zeros_like(total)
    for j, (k, low, _) in enumerate(parts):
        if not last:
            copies[j].wait()
        add_products(order[k] * per + low, cols, live, pieces[j], held.at[j], total)
    for copy in copies[count:]:
        copy.wait()
    if last:
        at = 0
        for out in outs:
            out[...] = total[at : at + out.shape[0]]
            at += out.shape[0]


def ladder(order, cols, live, w, start, arrived, per, parts, ahead=(), last=None):
    pieces = [arrived[part] for part in parts]
    count = len(pieces)
    size, occupied, _ = pieces[0].shape
    first = start is None
    scratch = []
    if last:
        out_shape = [jax.ShapeDtypeStruct((n, occupied, BLK), jnp.float32) for n in last]
    else:
        out_shape = [pltpu.VMEM((ABT_X, occupied, BLK), jnp.float32)]
        if ahead:
            out_shape.append(pltpu.VMEM((len(ahead), ahead[0][2], BLK, BLK), w.dtype))
        scratch = [
            pltpu.VMEM((count, size, BLK, BLK), w.dtype),
            pltpu.SemaphoreType.DMA((count + len(ahead),)),
        ]
        w = pltpu.with_memory_space_constraint(w, pltpu.HBM)
    return pl.pallas_call(
        functools.partial(ladder_kernel, parts, list(ahead), per, first, bool(last)),
        out_shape=out_shape,
        in_specs=[SMEM_SPEC] * 3
        + [VMEM_SPEC if last else ANY_SPEC]
        + [VMEM_SPEC] * (count + (not first)),
        out_specs=[VMEM_SPEC] * len(out_shape),
        input_output_aliases={} if first or last else {4 + count: 0},
        scratch_shapes=scratch,
        compiler_params=pltpu.CompilerParams(vmem_limit_bytes=8 * MIB),
        cost_estimate=pl.CostEstimate(
            flops=2 * count * size * occupied * BLK * BLK,
            bytes_accessed=2 * (count + len(ahead)) * size * BLK * BLK,
            transcendentals=0,
        ),
        name="ladder_products",
    )(order, cols, live, w, *pieces, *([] if first else [start]))


def encode_kernel(kept, got, *outs):
    share = outs[0].shape[0] - 1
    lane = lax.broadcasted_iota(jnp.int32, kept.shape[1:], 1)
    for b, out in enumerate(outs):
        powers = jnp.zeros(kept.shape[1:], jnp.int32)
        for j in range(share):
            value = kept[b * share + j] + got[b * share + j]
            top = jnp.max(jnp.abs(value), axis=1, keepdims=True)
            power = jnp.ceil(jnp.log2(jnp.maximum(top, 2.0**-100)))
            code = jnp.round(value * (jnp.exp2(-power) * CODE_TOP))
            out[j] = code.astype(jnp.int32).astype(jnp.int16)
            powers = jnp.where(lane == j, power.astype(jnp.int32), powers)
        out[share] = powers.astype(jnp.int16)


def encode(kept, got, parts):
    tiles, occupied, _ = kept.shape
    shape = jax.ShapeDtypeStruct((tiles // parts + 1, occupied, BLK), jnp.int16)
    return pl.pallas_call(
        encode_kernel,
        out_shape=[shape] * parts,
        in_specs=[VMEM_SPEC] * 2,
        out_specs=[VMEM_SPEC] * parts,
        compiler_params=pltpu.CompilerParams(vmem_limit_bytes=8 * MIB),
        cost_estimate=pl.CostEstimate(
            flops=8 * kept.size, bytes_accessed=10 * kept.size, transcendentals=0
        ),
        name="encode_sums",
    )(kept, got)


def decode_kernel(kept, got, *refs):
    arrived, out = refs[:-1], refs[-1]
    share = kept.shape[0]
    lane = lax.broadcasted_iota(jnp.int32, kept.shape[1:], 1)
    for j in range(share):
        value = kept[j] + got[j]
        for part in arrived:
            powers = jnp.where(lane == j, part[share].astype(jnp.int32), 0)
            power = jnp.sum(powers.astype(jnp.float32), axis=1, keepdims=True)
            code = part[j].astype(jnp.int32).astype(jnp.float32)
            value = value + code * (jnp.exp2(power) * (1.0 / CODE_TOP))
        out[:, j * BLK : (j + 1) * BLK] = value


def decode(kept, got, arrived):
    share, occupied, _ = kept.shape
    return pl.pallas_call(
        decode_kernel,
        out_shape=jax.ShapeDtypeStruct((occupied, share * BLK), jnp.float32),
        in_specs=[VMEM_SPEC] * (2 + len(arrived)),
        out_specs=VMEM_SPEC,
        compiler_params=pltpu.CompilerParams(vmem_limit_bytes=8 * MIB),
        cost_estimate=pl.CostEstimate(
            flops=8 * kept.size, bytes_accessed=14 * kept.size, transcendentals=0
        ),
        name="decode_sums",
    )(kept, got, *arrived)


def per_device(amplitudes, virt_irreps, w_tiles, tile_rows, tile_cols):
    occupied = amplitudes.shape[0]
    peers = lax.axis_size("gx")
    groups = lax.axis_size("gy")
    me = lax.axis_index("gx")
    mine = lax.axis_index("gy")
    row_count = amplitudes.shape[1] // BLK * peers
    per = tile_rows.shape[0] // peers
    near = peers // 2

    def swap(x, k):
        return lax.ppermute(x, "gx", [(i, i ^ k) for i in range(peers)])

    slots = tile_rows.shape[0]
    first_far = swap(tile_rows, near)
    place = {near: (first_far, 0)}
    known, rows, bit = [0, near], jnp.concatenate([tile_rows, first_far]), 2
    while bit < near:
        rows = jnp.concatenate([rows, swap(rows, bit)])
        known = known + [k ^ bit for k in known]
        bit *= 2
    odd = swap(rows, 1)
    for j, k in enumerate(known):
        place.setdefault(k, (rows, j * slots))
        place[k ^ 1] = (odd, j * slots)

    amp = stage(amplitudes)
    here = me.reshape(1)
    quarter = near // 4
    far_order = list(range(near, peers, 2)) + list(range(near + 1, peers, 2))
    far = [far_order[j * quarter : (j + 1) * quarter] for j in range(4)]
    every = (0, per)
    late = per // 4
    cut = [(0, per - late), (per - late, late)]
    arrived = {(0, *every): pick(here, tile_rows, 0, amp, per, every)}

    def send(k, part, after=()):
        arrived[k, *part] = swap(pick(here, *place[k], amp, per, part, after), k)

    for k in far[0] + far[1] + list(range(1, near)):
        send(k, every)
    for j in range(quarter):
        first, second, beside = arrived[far[0][j], *every], arrived[far[1][j], *every], arrived[2 + j, *every]
        send(far[2][j], every, (first,))
        send(far[3][j], cut[0], (first, second))
        send(far[3][j], cut[1], (first, second, beside))

    row_tile = mine * row_count + tile_rows
    col_tile = me * ABT_X + tile_cols
    live = (pair_irrep(row_tile, virt_irreps) == pair_irrep(col_tile, virt_irreps)).astype(
        jnp.float32
    )
    share = ABT_X // groups
    xs = groups // CORES
    owner = tile_cols // share
    other_core = (owner % CORES) ^ (mine % CORES)
    other_x = (owner // CORES) ^ (mine // CORES)
    cols = other_core * (ABT_X // CORES) + other_x * share + tile_cols % share
    order = jnp.arange(peers, dtype=jnp.int32) ^ me

    w = w_tiles.reshape(peers, per, BLK, BLK)
    args = (order, cols, live, w)

    def parts(ks, part=every):
        return [(k, *part) for k in ks]

    heads, tails = parts(far[3], cut[0]), parts(far[3], cut[1])
    (total,) = ladder(*args, None, arrived, per, parts(far[0]))
    (total,) = ladder(*args, total, arrived, per, parts(far[1]))
    total, held = ladder(*args, total, arrived, per, parts(range(near)), ahead=tails)
    (total,) = ladder(*args, total, arrived, per, parts(far[2]))
    (total,) = ladder(*args, total, arrived, per, heads)
    sizes = (share, (xs - 1) * share) * CORES
    keep, keep_rest, give, give_rest = ladder(
        order, cols, live, held, total, arrived, per, tails, last=sizes
    )

    def swap_gy(x, k):
        return lax.ppermute(x, "gy", [(i, i ^ k) for i in range(groups)])

    coded = encode(keep_rest, swap_gy(give_rest, 1), xs - 1)
    got = swap_gy(give, 1)
    return decode(keep, got, [swap_gy(coded[k - 1], k * CORES) for k in range(1, xs)])


def solution(mesh):
    in_specs = (
        P(None, ("gy", "gx")),
        P(),
        P(("gx", "gy"), None, None),
        P(("gx", "gy")),
        P(("gx", "gy")),
    )
    out_specs = P(None, ("gx", "gy"))
    return jax.shard_map(
        per_device, mesh=mesh, in_specs=in_specs, out_specs=out_specs, check_vma=False
    )
```

```python
import functools
import math

import jax
import jax.numpy as jnp
from jax import lax
from jax.experimental import pallas as pl
from jax.experimental.pallas import tpu as pltpu
from jax.sharding import PartitionSpec as P

V = 1024
BLK = 128
ABT_X = 32
CORES = 2
UNROLL = 32
CODE_TOP = 32000.0
MIB = 1024 * 1024

VMEM_SPEC = pl.BlockSpec(memory_space=pltpu.VMEM)
SMEM_SPEC = pl.BlockSpec(memory_space=pltpu.SMEM)
ANY_SPEC = pl.BlockSpec(memory_space=pl.ANY)


def pair_irrep(tile, virt_irreps):
    first = tile * BLK // V // BLK
    second = tile * BLK % V // BLK
    return jnp.bitwise_xor(virt_irreps[first], virt_irreps[second])


def stage_kernel(source, held, sem):
    copy = pltpu.make_async_copy(source, held, sem)
    copy.start()
    copy.wait()


def stage(x):
    return pl.pallas_call(
        stage_kernel,
        out_shape=pltpu.VMEM(x.shape, x.dtype),
        in_specs=[ANY_SPEC],
        out_specs=VMEM_SPEC,
        scratch_shapes=[pltpu.SemaphoreType.DMA],
        compiler_params=pltpu.CompilerParams(vmem_limit_bytes=8 * MIB),
        cost_estimate=pl.CostEstimate(flops=0, bytes_accessed=2 * x.size, transcendentals=0),
        name="stage_amplitudes",
    )(pltpu.with_memory_space_constraint(x, pltpu.HBM))


def pick_kernel(first, per, local_tiles, me, rows, amp, *refs):
    out = refs[-1]
    base = first + me[0] * per
    origin = me[0] * local_tiles

    def step(i, carry):
        lane = pl.multiple_of((rows[base + i] - origin) * BLK, BLK)
        out[i] = amp[:, pl.ds(lane, BLK)]
        return carry

    lax.fori_loop(0, out.shape[0], step, 0, unroll=math.gcd(out.shape[0], 8))


def pick(me, rows, first, amp, per, part, after=()):
    occupied, width = amp.shape
    low, count = part
    return pl.pallas_call(
        functools.partial(pick_kernel, first + low, per, width // BLK),
        out_shape=jax.ShapeDtypeStruct((count, occupied, BLK), amp.dtype),
        in_specs=[SMEM_SPEC, SMEM_SPEC, VMEM_SPEC] + [ANY_SPEC] * len(after),
        out_specs=VMEM_SPEC,
        compiler_params=pltpu.CompilerParams(vmem_limit_bytes=8 * MIB),
        cost_estimate=pl.CostEstimate(
            flops=0, bytes_accessed=4 * count * occupied * BLK, transcendentals=0
        ),
        name="pick_tiles",
    )(me, rows, amp, *after)


def add_products(base, cols, live, piece, weights, total):
    count = piece.shape[0]
    unroll = min(UNROLL, count)

    def step(i, carry):
        slots = [i * unroll + u for u in range(unroll)]
        products = [
            jnp.dot(piece[s], weights[s], preferred_element_type=jnp.float32) for s in slots
        ]
        for s, product in zip(slots, products):
            total[cols[base + s]] += product * live[base + s]
        return carry

    lax.fori_loop(0, count // unroll, step, 0)


def ladder_kernel(parts, ahead, per, first, last, order, cols, live, w, *refs):
    count = len(parts)
    pieces, refs = refs[:count], refs[count:]
    if not first:
        start, refs = refs[0], refs[1:]
    if last:
        outs, held, total = refs, w, start
    else:
        *outs, held, sems = refs
        total = outs[0]
    copies = []
    for j, (k, low, size) in enumerate([] if last else parts + ahead):
        target = held.at[j] if j < count else outs[1].at[j - count]
        source = w.at[order[k], pl.ds(low, size)]
        copies.append(pltpu.make_async_copy(source, target, sems.at[j]))
        copies[-1].start()
    if first:
        total[...] = jnp.zeros_like(total)
    for j, (k, low, _) in enumerate(parts):
        if not last:
            copies[j].wait()
        add_products(order[k] * per + low, cols, live, pieces[j], held.at[j], total)
    for copy in copies[count:]:
        copy.wait()
    if last:
        at = 0
        for out in outs:
            out[...] = total[at : at + out.shape[0]]
            at += out.shape[0]


def ladder(order, cols, live, w, start, arrived, per, parts, ahead=(), last=None):
    pieces = [arrived[part] for part in parts]
    count = len(pieces)
    size, occupied, _ = pieces[0].shape
    first = start is None
    scratch = []
    if last:
        out_shape = [jax.ShapeDtypeStruct((n, occupied, BLK), jnp.float32) for n in last]
    else:
        out_shape = [pltpu.VMEM((ABT_X, occupied, BLK), jnp.float32)]
        if ahead:
            out_shape.append(pltpu.VMEM((len(ahead), ahead[0][2], BLK, BLK), w.dtype))
        scratch = [
            pltpu.VMEM((count, size, BLK, BLK), w.dtype),
            pltpu.SemaphoreType.DMA((count + len(ahead),)),
        ]
        w = pltpu.with_memory_space_constraint(w, pltpu.HBM)
    return pl.pallas_call(
        functools.partial(ladder_kernel, parts, list(ahead), per, first, bool(last)),
        out_shape=out_shape,
        in_specs=[SMEM_SPEC] * 3
        + [VMEM_SPEC if last else ANY_SPEC]
        + [VMEM_SPEC] * (count + (not first)),
        out_specs=[VMEM_SPEC] * len(out_shape),
        input_output_aliases={} if first or last else {4 + count: 0},
        scratch_shapes=scratch,
        compiler_params=pltpu.CompilerParams(vmem_limit_bytes=8 * MIB),
        cost_estimate=pl.CostEstimate(
            flops=2 * count * size * occupied * BLK * BLK,
            bytes_accessed=2 * (count + len(ahead)) * size * BLK * BLK,
            transcendentals=0,
        ),
        name="ladder_products",
    )(order, cols, live, w, *pieces, *([] if first else [start]))


def encode_kernel(kept, got, *outs):
    share = outs[0].shape[0] - 1
    lane = lax.broadcasted_iota(jnp.int32, kept.shape[1:], 1)
    for b, out in enumerate(outs):
        powers = jnp.zeros(kept.shape[1:], jnp.int32)
        for j in range(share):
            value = kept[b * share + j] + got[b * share + j]
            top = jnp.max(jnp.abs(value), axis=1, keepdims=True)
            power = jnp.ceil(jnp.log2(jnp.maximum(top, 2.0**-100)))
            code = jnp.round(value * (jnp.exp2(-power) * CODE_TOP))
            out[j] = code.astype(jnp.int32).astype(jnp.int16)
            powers = jnp.where(lane == j, power.astype(jnp.int32), powers)
        out[share] = powers.astype(jnp.int16)


def encode(kept, got, parts):
    tiles, occupied, _ = kept.shape
    shape = jax.ShapeDtypeStruct((tiles // parts + 1, occupied, BLK), jnp.int16)
    return pl.pallas_call(
        encode_kernel,
        out_shape=[shape] * parts,
        in_specs=[VMEM_SPEC] * 2,
        out_specs=[VMEM_SPEC] * parts,
        compiler_params=pltpu.CompilerParams(vmem_limit_bytes=8 * MIB),
        cost_estimate=pl.CostEstimate(
            flops=8 * kept.size, bytes_accessed=10 * kept.size, transcendentals=0
        ),
        name="encode_sums",
    )(kept, got)


def decode_kernel(kept, got, *refs):
    arrived, out = refs[:-1], refs[-1]
    share = kept.shape[0]
    lane = lax.broadcasted_iota(jnp.int32, kept.shape[1:], 1)
    for j in range(share):
        value = kept[j] + got[j]
        for part in arrived:
            powers = jnp.where(lane == j, part[share].astype(jnp.int32), 0)
            power = jnp.sum(powers.astype(jnp.float32), axis=1, keepdims=True)
            code = part[j].astype(jnp.int32).astype(jnp.float32)
            value = value + code * (jnp.exp2(power) * (1.0 / CODE_TOP))
        out[:, j * BLK : (j + 1) * BLK] = value


def decode(kept, got, arrived):
    share, occupied, _ = kept.shape
    return pl.pallas_call(
        decode_kernel,
        out_shape=jax.ShapeDtypeStruct((occupied, share * BLK), jnp.float32),
        in_specs=[VMEM_SPEC] * (2 + len(arrived)),
        out_specs=VMEM_SPEC,
        compiler_params=pltpu.CompilerParams(vmem_limit_bytes=8 * MIB),
        cost_estimate=pl.CostEstimate(
            flops=8 * kept.size, bytes_accessed=14 * kept.size, transcendentals=0
        ),
        name="decode_sums",
    )(kept, got, *arrived)


def per_device(amplitudes, virt_irreps, w_tiles, tile_rows, tile_cols):
    occupied = amplitudes.shape[0]
    peers = lax.axis_size("gx")
    groups = lax.axis_size("gy")
    me = lax.axis_index("gx")
    mine = lax.axis_index("gy")
    row_count = amplitudes.shape[1] // BLK * peers
    per = tile_rows.shape[0] // peers
    near = peers // 2

    def swap(x, k):
        return lax.ppermute(x, "gx", [(i, i ^ k) for i in range(peers)])

    slots = tile_rows.shape[0]
    first_far = swap(tile_rows, near)
    place = {near: (first_far, 0)}
    known, rows, bit = [0, near], jnp.concatenate([tile_rows, first_far]), 2
    while bit < near:
        rows = jnp.concatenate([rows, swap(rows, bit)])
        known = known + [k ^ bit for k in known]
        bit *= 2
    odd = swap(rows, 1)
    for j, k in enumerate(known):
        place.setdefault(k, (rows, j * slots))
        place[k ^ 1] = (odd, j * slots)

    amp = stage(amplitudes)
    here = me.reshape(1)
    quarter = near // 4
    far_order = list(range(near, peers, 2)) + list(range(near + 1, peers, 2))
    far = [far_order[j * quarter : (j + 1) * quarter] for j in range(4)]
    every = (0, per)
    late = per // 2
    cut = [(0, per - late), (per - late, late)]
    arrived = {(0, *every): pick(here, tile_rows, 0, amp, per, every)}

    def send(k, part, after=()):
        arrived[k, *part] = swap(pick(here, *place[k], amp, per, part, after), k)

    for k in far[0] + far[1] + list(range(1, near)):
        send(k, every)
    for j in range(quarter):
        first, second, beside = arrived[far[0][j], *every], arrived[far[1][j], *every], arrived[2 + j, *every]
        send(far[2][j], every, (first,))
        send(far[3][j], cut[0], (first, second))
        send(far[3][j], cut[1], (first, second, beside))

    row_tile = mine * row_count + tile_rows
    col_tile = me * ABT_X + tile_cols
    live = (pair_irrep(row_tile, virt_irreps) == pair_irrep(col_tile, virt_irreps)).astype(
        jnp.float32
    )
    share = ABT_X // groups
    xs = groups // CORES
    owner = tile_cols // share
    other_core = (owner % CORES) ^ (mine % CORES)
    other_x = (owner // CORES) ^ (mine // CORES)
    cols = other_core * (ABT_X // CORES) + other_x * share + tile_cols % share
    order = jnp.arange(peers, dtype=jnp.int32) ^ me

    w = w_tiles.reshape(peers, per, BLK, BLK)
    args = (order, cols, live, w)

    def parts(ks, part=every):
        return [(k, *part) for k in ks]

    heads, tails = parts(far[3], cut[0]), parts(far[3], cut[1])
    (total,) = ladder(*args, None, arrived, per, parts(far[0]))
    (total,) = ladder(*args, total, arrived, per, parts(far[1]))
    total, held = ladder(*args, total, arrived, per, parts(range(near)), ahead=tails)
    (total,) = ladder(*args, total, arrived, per, parts(far[2]))
    (total,) = ladder(*args, total, arrived, per, heads)
    sizes = (share, (xs - 1) * share) * CORES
    keep, keep_rest, give, give_rest = ladder(
        order, cols, live, held, total, arrived, per, tails, last=sizes
    )

    def swap_gy(x, k):
        return lax.ppermute(x, "gy", [(i, i ^ k) for i in range(groups)])

    coded = encode(keep_rest, swap_gy(give_rest, 1), xs - 1)
    got = swap_gy(give, 1)
    return decode(keep, got, [swap_gy(coded[k - 1], k * CORES) for k in range(1, xs)])


def solution(mesh):
    in_specs = (
        P(None, ("gy", "gx")),
        P(),
        P(("gx", "gy"), None, None),
        P(("gx", "gy")),
        P(("gx", "gy")),
    )
    out_specs = P(None, ("gx", "gy"))
    return jax.shard_map(
        per_device, mesh=mesh, in_specs=in_specs, out_specs=out_specs, check_vma=False
    )
```
